256 devices in a mesh: group: 8 (over z_lo, core), section: 8 (over z_hi, x), tensor: 4 (over y).
Axes of the slice: x: 4, y: 4, z: 8 (z_hi: 2, z_lo: 4; z = z_hi * 4 + z_lo), core: 2. Of those that a mesh axis runs over, the one named last changes fastest.
Arguments:
- hidden_in: bfloat16 [256, 4096], P('group'), may hold values from -6 to 6
- queries: bfloat16 [8, 256, 4096], P('section', 'group', 'tensor'), may hold values from -5 to 5
- cache: bfloat16 [8, 256, 64, 1024], P('section', 'group', None, 'tensor'), may hold values from -5 to 5
- lengths: int32 [256], P('group'), may hold values from 2 to 63, as said below
- moves: int32 [48, 3], P('group'), may hold values from 0 to 31, as said below
- norm_gain: float32 [8, 4096], P('section'), may hold values from 0.5 to 1.5
- kv_weight: bfloat16 [8, 4096, 1024], P('section', None, 'tensor'), may hold values from -0.09375 to 0.09375
- out_weight: bfloat16 [8, 4096, 4096], P('section', 'tensor'), may hold values from -0.1875 to 0.1875
Outputs:
- layer_out: bfloat16 [8, 256, 4096], P('section', 'group', 'tensor')
- new_cache: bfloat16 [8, 256, 64, 1024], P('section', 'group', None, 'tensor')
The draws below stay inside these ranges and needn't reach their ends.
Inputs may be any that keep to these rules, and one draw needn't show every extreme that they name: `moves`: each group's 6 rows name distinct slots of that group. They come in 3 runs of 2 rows, each run with one destination group; the runs' destinations differ from one another and from the sender, and the first run of every group goes to the group half the number of groups further on, counted round. Every group receives 6 requests, into exactly the slots whose requests left it. `lengths`: cache rows at positions from the length on are unused.
All inputs are finite; a program needn't handle non-finite values.
Results may differ from the reference program's by a relative error of at most 0.024.
Values may be sent and summed in bfloat16 or wider, within the bound.
A program may use at most 64 MiB of HBM per device.

```python
import jax
import jax.numpy as jnp
from jax import lax

D = 4096
QH = 32
KVH = 4
HD = 128
SLOTS = 32
CTX = 64
PAIR = 2
FANOUT = 3
MOV = 6
LAYERS = 8
REQS = 256


def draw_queries(key, part):
    key = jax.random.fold_in(key, 11)
    first_key = jax.random.fold_in(key, 0)
    values = jax.random.truncated_normal(first_key, -5.0, 5.0, (LAYERS, REQS, QH, HD), jnp.float32)
    return values.reshape(LAYERS, REQS, QH * HD).astype(jnp.bfloat16)


def draw_cache(key, part):
    key = jax.random.fold_in(key, 12)
    values = jax.random.truncated_normal(key, -5.0, 5.0, (LAYERS, REQS, CTX, KVH, 2, HD), jnp.float32)
    return values.reshape(LAYERS, REQS, CTX, KVH * 2 * HD).astype(jnp.bfloat16)


def draw_lengths(key, part):
    key = jax.random.fold_in(key, 13)
    first_key, second_key, third_key = jax.random.split(key, 3)
    groups = REQS // SLOTS
    ceilings = jax.random.randint(first_key, (groups,), CTX // 4, CTX)
    repeated = jnp.repeat(ceilings, SLOTS)
    counts = jax.random.randint(second_key, (REQS,), 2, repeated + 1)
    chosen = jax.random.randint(third_key, (), 0, REQS)
    return counts.at[chosen].set(CTX - 1).astype(jnp.int32)


def draw_moves(key, part):
    key = jax.random.fold_in(key, 14)
    first_key, second_key = jax.random.split(key)
    groups = REQS // SLOTS
    half = groups // 2
    group_keys = jax.random.split(first_key, groups)
    leaving = jax.vmap(lambda k: jax.random.permutation(k, SLOTS))(group_keys)[:, :MOV].astype(jnp.int32)
    others = (jax.random.permutation(second_key, groups - 2) + 1).astype(jnp.int32)
    others = jnp.where(others >= half, others + 1, others)
    offsets = jnp.concatenate([jnp.full((1,), half, jnp.int32), others[:FANOUT - 1]]).astype(jnp.int32)
    run_index = jnp.arange(MOV, dtype=jnp.int32) // PAIR
    sender = jnp.arange(groups, dtype=jnp.int32)[:, None]
    receiver = (sender + offsets[run_index][None, :]) % groups
    arrival = leaving[receiver, jnp.arange(MOV, dtype=jnp.int32)[None, :]]
    table = jnp.stack([leaving, receiver, arrival], axis=-1)
    return table.reshape(groups * MOV, 3).astype(jnp.int32)


def block_scale(key, shape, cuts, smallest, top_value):
    loudness, own = 1.0, jax.random.fold_in(key, 6)
    for axis_at, parts in cuts:
        draws = jnp.exp(jax.random.uniform(jax.random.fold_in(own, axis_at), (parts,), jnp.float32, smallest / len(cuts), top_value / len(cuts)))
        loudness = loudness * jnp.repeat(draws, shape[axis_at] // parts).reshape([-1 if axis == axis_at else 1 for axis in range(len(shape))])
    return loudness


def normal_values(key, shape, width, bound, cuts=(), kind=jnp.bfloat16):
    level = block_scale(key, shape, cuts, -0.22, 0.18) if cuts else 1.0
    result = jax.random.normal(key, shape, jnp.float32) * width * level
    return jnp.minimum(jnp.maximum(result, -bound), bound).astype(kind)


def setup_inputs(seed: int = 0) -> dict:
    key_list = jax.random.split(jax.random.key(seed), 9)
    hidden_in = normal_values(key_list[0], (REQS, D), 1.0, 6.0, ((0, 8),))
    queries = draw_queries(jax.random.fold_in(key_list[8], 71), 0)
    cache = draw_cache(jax.random.fold_in(key_list[8], 71), 0)
    lengths = draw_lengths(jax.random.fold_in(key_list[8], 71), 0)
    moves = draw_moves(jax.random.fold_in(key_list[8], 71), 0)
    norm_gain = jnp.clip(1.0 + 0.1 * jax.random.normal(key_list[5], (LAYERS, D), jnp.float32), 0.5, 1.5)
    kv_weight = normal_values(key_list[6], (LAYERS, D, KVH * 2 * HD), D ** -0.5, 0.09375, ((0, 8), (2, 4)))
    out_weight = normal_values(key_list[7], (LAYERS, QH * HD, D), (QH * HD // 4) ** -0.5, 0.1875, ((0, 8), (1, 4)))
    return dict(hidden_in=hidden_in, queries=queries, cache=cache, lengths=lengths, moves=moves, norm_gain=norm_gain, kv_weight=kv_weight, out_weight=out_weight)


def decode_layer(hidden, gain, kv_weight, query, cache, lengths, out_weight):
    rows = hidden.shape[0]
    ctx = cache.shape[1]
    kv_heads = cache.shape[-1] // (2 * HD)
    q_heads = query.shape[-1] // HD
    group_size = q_heads // kv_heads
    widef = hidden.astype(jnp.float32)
    normed = (widef * jax.lax.rsqrt(lax.optimization_barrier(jnp.mean(widef * widef, -1, keepdims=True)) + 1e-06) * gain).astype(jnp.bfloat16)
    fresh = jnp.dot(normed, kv_weight, preferred_element_type=jnp.float32).astype(jnp.bfloat16)
    fresh_split = fresh.reshape(rows, kv_heads, 2, HD).astype(jnp.float32)
    cache_split = cache.reshape(rows, ctx, kv_heads, 2, HD).astype(jnp.float32)
    query_split = query.reshape(rows, kv_heads, group_size, HD).astype(jnp.float32)
    scale = HD ** (-0.5)
    scores = jnp.einsum('rhgd,rlhd->rhgl', query_split, cache_split[:, :, :, 0]) * scale
    own = jnp.einsum('rhgd,rhd->rhg', query_split, fresh_split[:, :, 0]) * scale
    valid = (jnp.arange(ctx, dtype=jnp.int32)[None, :] < lengths[:, None])[:, None, None, :]
    scores = jnp.where(valid, scores, -jnp.inf)
    top = jnp.maximum(lax.optimization_barrier(jnp.max(scores, -1)), own)
    weights = jnp.where(valid, jnp.exp(scores - top[..., None]), 0.0)
    own_weight = jnp.exp(own - top)
    total = lax.optimization_barrier(jnp.sum(weights, -1)) + own_weight
    probs = (weights / total[..., None]).astype(jnp.bfloat16).astype(jnp.float32)
    own_prob = (own_weight / total).astype(jnp.bfloat16).astype(jnp.float32)
    context = jnp.einsum('rhgl,rlhd->rhgd', probs, cache_split[:, :, :, 1])
    context = context + own_prob[..., None] * fresh_split[:, :, 1][:, :, None, :]
    context = context.astype(jnp.bfloat16).reshape(rows, q_heads * HD)
    partial_value = jnp.dot(context, out_weight, preferred_element_type=jnp.float32)
    return (widef, partial_value, fresh)

def write_fresh(cache, lengths, fresh):
    ctx = cache.shape[1]
    marked = jnp.arange(ctx, dtype=jnp.int32)[None, :] == lengths[:, None]
    return jnp.where(marked[:, :, None], fresh[:, None, :], cache)

def reference(hidden_in, queries, cache, lengths, moves, norm_gain, kv_weight, out_weight):
    requests = hidden_in.shape[0]
    row_group = (jnp.arange(moves.shape[0], dtype=jnp.int32) // MOV).astype(jnp.int32)
    anchor = (row_group * SLOTS + moves[:, 0]).astype(jnp.int32)
    target = (moves[:, 1] * SLOTS + moves[:, 2]).astype(jnp.int32)
    dest = jnp.arange(requests, dtype=jnp.int32).at[anchor].set(target)
    state = hidden_in
    outputs = []
    stores = []
    for layer in range(LAYERS):
        widef, partial_value, fresh = decode_layer(state, norm_gain[layer], kv_weight[layer], queries[layer], cache[layer], lengths, out_weight[layer])
        state = (widef + partial_value).astype(jnp.bfloat16)
        outputs.append(jnp.zeros_like(state).at[dest].set(state))
        written = write_fresh(cache[layer], lengths, fresh)
        stores.append(jnp.zeros_like(written).at[dest].set(written))
    return (jnp.stack(outputs), jnp.stack(stores))
```

```python
import functools

import jax
import jax.numpy as jnp
from jax import lax
from jax.experimental import pallas as pl
from jax.experimental.pallas import tpu as pltpu
from jax.sharding import PartitionSpec as P

HD = 128
PAIR = 2
ROWS = 16
HALVES = 2
MESH = pl.DeviceIdType.MESH
F32 = jnp.float32
BF16 = jnp.bfloat16
NONE = 255
LOW = -1e30


def iota(shape, axis):
    return lax.broadcasted_iota(jnp.int32, shape, axis)


def kernel(
    sizes,
    lens_in, moves_in, hidden, query, cache, gain, kvw, outw,
    xout_ref, fresh_out_ref, count_ref, base_v,
    lens_ref, moves_ref, xin, x0_v, q_v, qf_v, cache_v, gain_v, kvw_v, outw_v,
    mc_ref, sc_ref, ctx_ref, fresh_f, own_part, xnew, xnew_f, rs_send, rs_recv,
    pack, arr, info_pack, info_arr, place_v, place_s,
    perm_s, pick_ref, back_ref, sel_ref, sel2_ref, moved_ref, row_pack, row_arr,
    load_sem, outw_sem,
    rs_ss, rs_rs, ag_ss, ag_rs, hop_rs, fwd_ss, gc_ss, gc_rs, info_ss, info_rs, row_ss, row_rs,
    local_sem,
):
    G, L, T, micros, slots, width, ctx_len = sizes
    W = width // T
    H = HALVES
    S = W // H
    heads = W // HD
    pieces = heads + 2
    g = lax.axis_index("group")
    l = lax.axis_index("section")
    t = lax.axis_index("tensor")
    R = ROWS
    last = L - 1
    half = L // 2

    order = tuple(sorted(range(1, T), key=lambda d: -min(d, T - d)))

    def rs_copy(m, h, d):
        return pltpu.make_async_remote_copy(
            src_ref=rs_send.at[m, h, d - 1], dst_ref=rs_recv.at[m, h, d - 1],
            send_sem=rs_ss.at[m, h, d - 1], recv_sem=rs_rs.at[m, h],
            device_id={"tensor": lax.rem(t + d, T)}, device_id_type=MESH)

    def ag_copy(m, h, d):
        return pltpu.make_async_remote_copy(
            src_ref=xnew.at[m, h], dst_ref=xin.at[m, h, t],
            send_sem=ag_ss.at[m, h, d], recv_sem=ag_rs.at[m, h],
            device_id={"section": l + 1, "tensor": lax.rem(t + d, T)}, device_id_type=MESH)

    def hop_copy(m, h):
        return pltpu.make_async_remote_copy(
            src_ref=xnew.at[m, h], dst_ref=xin.at[m, h, t],
            send_sem=ag_ss.at[m, h, 0], recv_sem=hop_rs.at[m, h],
            device_id={"section": l + 1}, device_id_type=MESH)

    def fwd_copy(m, h, d):
        return pltpu.make_async_remote_copy(
            src_ref=xin.at[m, h, t], dst_ref=xin.at[m, h, t],
            send_sem=fwd_ss.at[m, h, d - 1], recv_sem=ag_rs.at[m, h],
            device_id={"tensor": lax.rem(t + d, T)}, device_id_type=MESH)

    def arrived(ref, sem):
        pltpu.make_async_copy(ref, ref, sem).wait()

    def to_group(src, dst, ss, rs, d):
        return pltpu.make_async_remote_copy(
            src_ref=src, dst_ref=dst, send_sem=ss.at[d - 1], recv_sem=rs.at[d - 1],
            device_id={"group": lax.rem(g + d, G)}, device_id_type=MESH)

    def gc_copy(d):
        e = PAIR * (d - 1)
        return to_group(pack.at[pl.ds(e, PAIR)], arr.at[pl.ds(e, PAIR)], gc_ss, gc_rs, d)

    def info_copy(d):
        return to_group(info_pack.at[d - 1], info_arr.at[d - 1], info_ss, info_rs, d)

    def row_copy(d):
        return to_group(row_pack.at[d - 1], row_arr.at[d - 1], row_ss, row_rs, d)

    def outw_load(h, d):
        start = pl.multiple_of(lax.rem(t + d, T) * W + h * S, S)
        place = order.index(d) if d else T - 1
        return pltpu.make_async_copy(
            outw.at[0, :, pl.ds(start, S)], outw_v.at[h, :, pl.ds(place * S, S)], outw_sem.at[h, d])

    query_load = pltpu.make_async_copy(query.at[0], q_v, load_sem.at[0])
    cache_load = pltpu.make_async_copy(cache.at[0], cache_v, load_sem.at[1])
    lens_load = pltpu.make_async_copy(lens_in, lens_ref, load_sem.at[5])
    moves_load = pltpu.make_async_copy(moves_in, moves_ref, load_sem.at[6])
    x_load = pltpu.make_async_copy(hidden, x0_v, load_sem.at[4])
    gain_load = pltpu.make_async_copy(gain, gain_v, load_sem.at[2])
    movers = moves_ref.shape[1]
    place_load = pltpu.make_async_copy(place_v.at[0], place_s, local_sem.at[0])

    lens_load.start()
    moves_load.start()
    query_load.start()
    cache_load.start()

    @pl.when(l == 0)
    def _():
        x_load.start()

    gain_load.start()
    for h in range(H):
        for q in range(T):
            pltpu.make_async_copy(
                kvw.at[0, pl.ds(q * W + h * S, S)], kvw_v.at[h, pl.ds(q * S, S)],
                load_sem.at[3]).start()

    for h in range(H):
        for d in order:
            outw_load(h, d).start()
    for h in range(H):
        outw_load(h, 0).start()

    barrier = pltpu.get_barrier_semaphore()
    for d in range(1, T):
        pl.semaphore_signal(barrier, inc=1, device_id={"tensor": lax.rem(t + d, T)}, device_id_type=MESH)
    for d in range(1, G):
        pl.semaphore_signal(barrier, inc=1, device_id={"group": lax.rem(g + d, G)}, device_id_type=MESH)

    @pl.when(l > 0)
    def _():
        for k in range(T):
            pl.semaphore_signal(
                barrier, inc=1, device_id={"section": l - 1, "tensor": k}, device_id_type=MESH)

    @pl.when((l > 0) & (l < last))
    def _():
        pl.semaphore_wait(barrier, T - 1 + G - 1 + T)

    @pl.when(l == last)
    def _():
        pl.semaphore_wait(barrier, T - 1 + G - 1)

    def arrange():
        leaving = [moves_ref[0, i] for i in range(movers)]
        ranked = list(leaving)
        for end in range(movers - 1, 0, -1):
            for i in range(end):
                low = jnp.minimum(ranked[i], ranked[i + 1])
                high = jnp.maximum(ranked[i], ranked[i + 1])
                ranked[i], ranked[i + 1] = low, high

        def staying(position):
            slot = position - movers
            for k in range(movers):
                slot = slot + (slot >= ranked[k]).astype(jnp.int32)
            return slot

        def slot_of(position):
            slot = staying(position)
            for i in range(movers):
                slot = jnp.where(position == i, leaving[i], slot)
            return slot

        def place(p, carry):
            perm_s[p] = staying(p)
            return carry

        for i in range(movers):
            perm_s[i] = leaving[i]
        lax.fori_loop(movers, slots, place, 0)
        square = (slots, slots)
        row, col = iota(square, 0), iota(square, 1)
        pick_ref[...] = jnp.where(slot_of(row) == col, 1.0, 0.0).astype(BF16)
        back_ref[...] = jnp.where((staying(col) == row) & (col >= movers), 1.0, 0.0).astype(BF16)

    block = 8
    blocks = slots // block

    def attend(first, end):
        span = block * ctx_len
        scale = HD ** -0.5

        def one(b, carry):
            rows = pl.ds(pl.multiple_of(b * block, block), block)
            lens = jnp.zeros((block, span), jnp.int32)
            row = iota((block, span), 0)
            slot = [perm_s[b * block + n] for n in range(block)]
            for n in range(block):
                lens = jnp.where(row == n, lens_ref[slot[n]], lens)
            tokens = jnp.concatenate([cache_v[slot[n]] for n in range(block)], axis=0)
            col = iota((block, span), 1)
            ok = (col // ctx_len == row) & (col % ctx_len < lens)
            bias = jnp.where(ok, 0.0, LOW).astype(F32)
            stacked = jnp.concatenate(
                [qf_v[rows, a * HD:(a + 1) * HD] for a in range(heads)], axis=0).astype(BF16)
            keys = tokens[:, 0:HD]
            values = tokens[:, HD:2 * HD]
            score = lax.dot_general(
                stacked, keys, (((1,), (1,)), ((), ())), preferred_element_type=F32)
            score = score.reshape(heads, block, span) * scale + bias[None]
            top = jnp.max(score, axis=-1, keepdims=True)
            weight = jnp.exp(score - top)
            total = jnp.sum(weight, axis=-1, keepdims=True)
            mixed = jnp.dot(
                weight.reshape(heads * block, span).astype(BF16), values,
                preferred_element_type=F32)
            ctx_ref[:, rows, :] = mixed.reshape(heads, block, HD)
            mc_ref[:, rows, :] = jnp.broadcast_to(top, (heads, block, HD))
            sc_ref[:, rows, :] = jnp.broadcast_to(total, (heads, block, HD))
            return carry

        lax.fori_loop(first, end, one, 0)

    def depart():
        lane = iota((8, 256), 1)
        sel_row = iota(sel_ref.shape, 0)
        slot_at = jnp.full(sel_ref.shape, NONE, jnp.int32)
        for d in range(1, G):
            e = d - 1
            dest = lax.rem(g + d, G)
            place_vec = jnp.zeros((8, 256), jnp.int32)
            len_vec = jnp.zeros((8, 256), jnp.int32)
            for i in range(PAIR):
                slot = jnp.int32(NONE)
                place = jnp.int32(NONE)
                from_slot = jnp.int32(0)
                for k in range(movers // PAIR):
                    hit = moves_ref[1, PAIR * k] == dest
                    slot = jnp.where(hit, PAIR * k + i, slot)
                    place = jnp.where(hit, moves_ref[2, PAIR * k + i], place)
                    from_slot = jnp.where(hit, moves_ref[0, PAIR * k + i], from_slot)
                here = lane // 16 == e * PAIR + i
                place_vec = jnp.where(here, place, place_vec)
                len_vec = jnp.where(here, lens_ref[from_slot], len_vec)
                slot_at = jnp.where(sel_row // 16 == e * PAIR + i, slot, slot_at)
                pack[PAIR * e + i] = cache_v[from_slot]
            info_pack[e, 0:8, :] = place_vec
            info_pack[e, 8:16, :] = len_vec
            info_copy(d).start()
            gc_copy(d).start()
        sel_col = iota(sel_ref.shape, 1)
        chosen = (sel_row % 16 == sel_col // R) & (slot_at == sel_col % R)
        sel_ref[...] = jnp.where(chosen, 1.0, 0.0).astype(BF16)

    def arrive():
        for d in range(1, G):
            info_copy(d).wait_recv()
        place = info_arr[0, 0:8, :]
        length = info_arr[0, 8:16, :]
        for e in range(1, G - 1):
            place = place + info_arr[e, 0:8, :]
            length = length + info_arr[e, 8:16, :]
        lane8 = iota((8, 256), 1)
        place = jnp.where(lane8 < (G - 1) * PAIR * 16, place, NONE)
        place_v[0] = place
        place_load.start()
        wide = (slots, 256)
        spot = jnp.broadcast_to(place[0:1, :], wide)
        long = jnp.broadcast_to(length[0:1, :], wide)
        lane = iota(wide, 1)
        row = iota(wide, 0)
        match = spot == row
        first = match & (lane % 16 == 0)
        has = jnp.max(jnp.where(first, 1.0, 0.0), axis=-1, keepdims=True)
        moved_len = jnp.max(jnp.where(first, long.astype(F32), 0.0), axis=-1, keepdims=True)
        own_len = jnp.zeros((slots, HD), F32)
        narrow = iota((slots, HD), 0)
        for n in range(slots):
            own_len = jnp.where(narrow == n, lens_ref[n].astype(F32), own_len)
        count_ref[...] = jnp.where(has > 0.5, moved_len, own_len).astype(jnp.int32)
        for c in range(pieces):
            sel2_ref[c * slots:(c + 1) * slots, :] = jnp.where(
                match & (lane % 16 == c), 1.0, 0.0).astype(BF16)
        for d in range(1, G):
            gc_copy(d).wait_recv()
        place_load.wait()

        def fill(j, carry):
            index = jnp.int32(-1)
            for e in range((G - 1) * PAIR):
                index = jnp.where(place_s[0, e * 16] == j, e, index)
            moved = arr[jnp.maximum(index, 0)]
            kept = cache_v[j]
            base_v[j] = lax.select_n(index >= 0, kept, moved)
            return carry

        lax.fori_loop(0, slots, fill, 0)

    def pass_on(m, h):
        arrived(xin.at[m, h, t], hop_rs.at[m, h])
        for d in order:
            fwd_copy(m, h, d).start()

    def forward(m):
        @pl.when(l == half)
        def _():
            for h in range(H):
                pass_on(m, h)

    def whole_fresh():
        acc = jnp.zeros((slots, 2 * HD), F32)
        square = jnp.zeros((slots, 1), F32)
        for h in range(H):
            scaled = []
            for q in range(T):
                cols = slice(q * W + h * S, q * W + (h + 1) * S)
                xq = x0_v[:, cols].astype(F32)
                square = square + jnp.sum(xq * xq, axis=-1, keepdims=True)
                scaled.append((xq * gain_v[:, cols]).astype(BF16))
            acc = acc + jnp.dot(
                jnp.concatenate(scaled, axis=1), kvw_v[h], preferred_element_type=F32)
        fresh = (acc * lax.rsqrt(square * (1.0 / width) + 1e-06)).astype(BF16)
        fresh_f[...] = jnp.dot(pick_ref[...], fresh, preferred_element_type=F32)
        mine = x0_v[:, pl.ds(pl.multiple_of(t * W, W), W)]
        ordered = jnp.dot(pick_ref[...], mine, preferred_element_type=F32).astype(BF16)
        for m in range(micros):
            for h in range(H):
                xin[m, h, t] = ordered[m * R:(m + 1) * R, h * S:(h + 1) * S]

    def fresh_part(m):
        rows = pl.ds(pl.multiple_of(m * R, R), R)
        acc = jnp.zeros((R, 2 * HD), F32)
        square = jnp.zeros((R, 1), F32)
        for h in range(H):

            @pl.when(l != half)
            def _():
                arrived(xin.at[m, h], ag_rs.at[m, h])

            @pl.when(l == half)
            def _():
                arrived(xin.at[m, h, pl.ds(0, T - 1)], ag_rs.at[m, h])

            scaled = []
            for q in range(T):
                cols = slice(q * W + h * S, q * W + (h + 1) * S)
                xq = xin[m, h, q].astype(F32)
                square = square + jnp.sum(xq * xq, axis=-1, keepdims=True)
                scaled.append((xq * gain_v[:, cols]).astype(BF16))
            acc = acc + jnp.dot(
                jnp.concatenate(scaled, axis=1), kvw_v[h], preferred_element_type=F32)
        fresh = (acc * lax.rsqrt(square * (1.0 / width) + 1e-06)).astype(BF16).astype(F32)
        fresh_f[rows, :] = fresh

    def front(m):
        rows = pl.ds(pl.multiple_of(m * R, R), R)

        @pl.when(l > 0)
        def _():
            fresh_part(m)

        fresh = fresh_f[rows, :]
        key = fresh[:, 0:HD]
        value = fresh[:, HD:2 * HD]
        parts = []
        for a in range(heads):
            qa = qf_v[rows, a * HD:(a + 1) * HD]
            own = jnp.sum(qa * key, axis=-1, keepdims=True) * (HD ** -0.5)
            old_top = mc_ref[a, rows, :]
            top = jnp.maximum(old_top, own)
            old_scale = jnp.exp(old_top - top)
            own_weight = jnp.exp(own - top)
            total = sc_ref[a, rows, :] * old_scale + own_weight
            mixed = (ctx_ref[a, rows, :] * old_scale + own_weight * value) / total
            parts.append(mixed.astype(BF16))
        return jnp.concatenate(parts, axis=1)

    def project(m, context, h):
        for i, d in enumerate(order):
            part = jnp.dot(
                context, outw_v[h, :, i * S:(i + 1) * S], preferred_element_type=F32)
            rs_send[m, h, d - 1] = part.astype(BF16)
            rs_copy(m, h, d).start()

    def project_own(m, context, h):
        own_part[m, h] = jnp.dot(
            context, outw_v[h, :, (T - 1) * S:T * S], preferred_element_type=F32)

    def reduce(m, h):
        total = own_part[m, h] + xin[m, h, t].astype(F32)
        arrived(rs_recv.at[m, h], rs_rs.at[m, h])
        for d in order:
            total = total + rs_recv[m, h, d - 1].astype(F32)
        rounded = total.astype(BF16)
        xnew[m, h] = rounded
        xnew_f[pl.ds(pl.multiple_of(m * R, R), R), h * S:(h + 1) * S] = rounded.astype(F32)

        @pl.when((l < last) & (l != half - 1))
        def _():
            for d in order + (0,):
                ag_copy(m, h, d).start()

        @pl.when(l == half - 1)
        def _():
            hop_copy(m, h).start()

    def exchange():
        stacked = jnp.concatenate(
            [xnew_f[0:R, c * HD:(c + 1) * HD] for c in range(heads)]
            + [fresh_f[0:R, c * HD:(c + 1) * HD] for c in range(2)], axis=0).astype(BF16)
        leaving = jnp.dot(sel_ref[...], stacked, preferred_element_type=F32).astype(BF16)
        for d in range(1, G):
            row_pack[d - 1] = leaving[(d - 1) * 32:d * 32]
            row_copy(d).start()

    def collect():
        row_arr[G - 1] = jnp.zeros((32, HD), BF16)
        for d in range(1, G):
            row_copy(d).wait_recv()
        moved_ref[...] = jnp.dot(
            sel2_ref[...], row_arr[...].reshape(G * 32, HD), preferred_element_type=F32)

    lens_load.wait()
    moves_load.wait()
    arrange()
    query_load.wait()
    cache_load.wait()
    qf_v[...] = jnp.dot(pick_ref[...], q_v[...], preferred_element_type=F32)
    first = R // block
    attend(0, first)

    @pl.when(l > 0)
    def _():
        attend(first, blocks)
        depart()

    @pl.when(l == 0)
    def _():
        x_load.wait()
        gain_load.wait()
        arrived(kvw_v, load_sem.at[3])
        whole_fresh()

    @pl.when(l >= 3)
    def _():
        arrive()

    @pl.when(l > 0)
    def _():
        gain_load.wait()
        arrived(kvw_v, load_sem.at[3])

    forward(0)

    def batch(m, carry):
        context = front(m)

        @pl.when((l == 0) & (m == 0))
        def _():
            pl.semaphore_wait(barrier, T - 1 + G - 1 + T)

        @pl.when(m == 0)
        def _():
            for h in range(H):
                for d in order + (0,):
                    outw_load(h, d).wait()

        for h in range(H):
            project(m, context, h)

        @pl.when(m + 1 < micros)
        def _():
            forward(m + 1)

        for h in range(H):
            project_own(m, context, h)

        @pl.when((l == 0) & (m == 0))
        def _():
            attend(first, blocks)

        @pl.when((l == last) & (m == micros - 1))
        def _():
            collect()

        for h in range(H):
            reduce(m, h)

        @pl.when((l == last) & (m == 0))
        def _():
            exchange()

        return carry

    lax.fori_loop(0, micros, batch, 0)

    @pl.when(l == 0)
    def _():
        depart()

    @pl.when(l < 3)
    def _():
        arrive()

    @pl.when(l < last)
    def _():
        exchange()
        collect()

    back = back_ref[...]
    for c in range(pieces):
        piece = (xnew_f[:, c * HD:(c + 1) * HD] if c < heads
                 else fresh_f[:, (c - heads) * HD:(c - heads + 1) * HD])
        kept = jnp.dot(back, piece.astype(BF16), preferred_element_type=F32)
        result = (kept + moved_ref[c * slots:(c + 1) * slots, :]).astype(BF16)
        if c < heads:
            xout_ref[:, c * HD:(c + 1) * HD] = result
        else:
            fresh_out_ref[:, (c - heads) * HD:(c - heads + 1) * HD] = result

    for m in range(micros):
        for h in range(H):
            for d in order:
                rs_copy(m, h, d).wait_send()
    for d in range(1, G):
        info_copy(d).wait_send()
        gc_copy(d).wait_send()
        row_copy(d).wait_send()

    @pl.when((l < last) & (l != half - 1))
    def _():
        for m in range(micros):
            for h in range(H):
                for d in range(T):
                    ag_copy(m, h, d).wait_send()

    @pl.when(l == half - 1)
    def _():
        for m in range(micros):
            for h in range(H):
                hop_copy(m, h).wait_send()

    @pl.when(l == half)
    def _():
        for m in range(micros):
            for h in range(H):
                for d in order:
                    fwd_copy(m, h, d).wait_send()


def finish(chunks, xout, fresh_ref, count_ref, base, layer_out, new_cache, held, out_sem, x_sem):
    slots, ctx_len, kv = held.shape
    part = slots // chunks

    def store(c):
        rows = pl.ds(c * part, part)
        return pltpu.make_async_copy(held.at[rows], new_cache.at[0, rows], out_sem.at[c])

    rows_copy = pltpu.make_async_copy(xout, layer_out.at[0], x_sem.at[0])
    rows_copy.start()
    token = iota((ctx_len, HD), 0)
    for c in range(chunks):
        for j in range(c * part, (c + 1) * part):
            here = token == count_ref[j:j + 1, :]
            for k in range(kv // HD):
                cols = slice(k * HD, (k + 1) * HD)
                row = fresh_ref[j:j + 1, cols].astype(F32)
                held[j, :, cols] = jnp.where(here, row, base[j, :, cols].astype(F32)).astype(BF16)
        store(c).start()
    rows_copy.wait()
    for c in range(chunks):
        store(c).wait()


def per_device(sizes, hidden_in, queries, cache, lengths, moves, norm_gain, kv_weight, out_weight):
    G, L, T, micros, slots, width, ctx_len = sizes
    W = width // T
    heads = W // HD
    pieces = heads + 2
    R = ROWS
    H = HALVES
    S = W // H
    kv = 2 * HD
    movers = (G - 1) * PAIR
    any_spec = pl.BlockSpec(memory_space=pl.ANY)
    vmem = pl.BlockSpec(memory_space=pltpu.VMEM)
    dma = pltpu.SemaphoreType.DMA
    xout, fresh, count, base = pl.pallas_call(
        functools.partial(kernel, sizes),
        out_shape=(
            pltpu.VMEM((slots, W), BF16),
            pltpu.VMEM((slots, kv), BF16),
            pltpu.VMEM((slots, HD), jnp.int32),
            pltpu.VMEM((slots, ctx_len, kv), BF16),
        ),
        in_specs=[any_spec] * 8,
        out_specs=(vmem, vmem, vmem, vmem),
        scratch_shapes=[
            pltpu.SMEM(lengths.shape, jnp.int32),
            pltpu.SMEM(moves.shape[::-1], jnp.int32),
            pltpu.VMEM((micros, H, T, R, S), BF16),
            pltpu.VMEM((slots, width), BF16),
            pltpu.VMEM((slots, W), BF16),
            pltpu.VMEM((slots, W), F32),
            pltpu.VMEM((slots, ctx_len, kv), BF16),
            pltpu.VMEM((1, width), F32),
            pltpu.VMEM((H, T * S, kv), BF16),
            pltpu.VMEM((H, W, T * S), BF16),
            pltpu.VMEM((heads, slots, HD), F32),
            pltpu.VMEM((heads, slots, HD), F32),
            pltpu.VMEM((heads, slots, HD), F32),
            pltpu.VMEM((slots, kv), F32),
            pltpu.VMEM((micros, H, R, S), F32),
            pltpu.VMEM((micros, H, R, S), BF16),
            pltpu.VMEM((slots, W), F32),
            pltpu.VMEM((micros, H, T - 1, R, S), BF16),
            pltpu.VMEM((micros, H, T - 1, R, S), BF16),
            pltpu.VMEM((movers, ctx_len, kv), BF16),
            pltpu.VMEM((movers, ctx_len, kv), BF16),
            pltpu.VMEM((G - 1, 16, 256), jnp.int32),
            pltpu.VMEM((G - 1, 16, 256), jnp.int32),
            pltpu.VMEM((1, 8, 256), jnp.int32),
            pltpu.SMEM((8, 256), jnp.int32),
            pltpu.SMEM((slots,), jnp.int32),
            pltpu.VMEM((slots, slots), BF16),
            pltpu.VMEM((slots, slots), BF16),
            pltpu.VMEM(((G - 1) * 32, pieces * R), BF16),
            pltpu.VMEM((pieces * slots, 256), BF16),
            pltpu.VMEM((pieces * slots, HD), F32),
            pltpu.VMEM((G - 1, 32, HD), BF16),
            pltpu.VMEM((G, 32, HD), BF16),
            dma((7,)), dma((H, T)),
            dma((micros, H, T - 1)), dma((micros, H)),
            dma((micros, H, T)), dma((micros, H)), dma((micros, H)), dma((micros, H, T - 1)),
            dma((G - 1,)), dma((G - 1,)), dma((G - 1,)), dma((G - 1,)), dma((G - 1,)), dma((G - 1,)),
            dma((1,)),
        ],
        compiler_params=pltpu.CompilerParams(
            collective_id=0, has_side_effects=True, vmem_limit_bytes=56 * 1024 * 1024),
        name="chain",
    )(lengths, moves.T, hidden_in, queries, cache, norm_gain, kv_weight, out_weight)
    chunks = 4
    return pl.pallas_call(
        functools.partial(finish, chunks),
        out_shape=(
            jax.ShapeDtypeStruct((1, slots, W), BF16),
            jax.ShapeDtypeStruct((1, slots, ctx_len, kv), BF16),
        ),
        in_specs=[vmem] * 4,
        out_specs=(any_spec, any_spec),
        scratch_shapes=[pltpu.VMEM((slots, ctx_len, kv), BF16), dma((chunks,)), dma((1,))],
        compiler_params=pltpu.CompilerParams(vmem_limit_bytes=16 * 1024 * 1024),
        name="finish",
    )(*(pltpu.with_memory_space_constraint(part, pltpu.VMEM) for part in (xout, fresh, count, base)))


def solution(mesh):
    G, L, T = mesh.shape["group"], mesh.shape["section"], mesh.shape["tensor"]

    def whole(hidden_in, queries, cache, lengths, moves, norm_gain, kv_weight, out_weight):
        slots = hidden_in.shape[0] // G
        sizes = (G, L, T, slots // ROWS, slots, hidden_in.shape[1], cache.shape[2])
        return jax.shard_map(
            functools.partial(per_device, sizes),
            mesh=mesh,
            in_specs=(
                P("group", None),
                P("section", "group", "tensor"),
                P("section", "group", None, "tensor"),
                P("group"),
                P("group", None),
                P("section", None),
                P("section", None, "tensor"),
                P("section", "tensor", None),
            ),
            out_specs=(P("section", "group", "tensor"), P("section", "group", None, "tensor")),
            check_vma=False,
        )(hidden_in, queries, cache, lengths, moves, norm_gain, kv_weight, out_weight)

    return whole
```

```python
import functools

import jax
import jax.numpy as jnp
from jax import lax
from jax.experimental import pallas as pl
from jax.experimental.pallas import tpu as pltpu
from jax.sharding import PartitionSpec as P

HD = 128
PAIR = 2
ROWS = 16
HALVES = 2
MESH = pl.DeviceIdType.MESH
F32 = jnp.float32
BF16 = jnp.bfloat16
NONE = 255
LOW = -1e30


def iota(shape, axis):
    return lax.broadcasted_iota(jnp.int32, shape, axis)


def kernel(
    sizes,
    lens_in, moves_in, hidden, query, cache, gain, kvw, outw,
    xout_ref, base_v,
    count_ref, lens_ref, moves_ref, xin, x0_v, q_v, qf_v, cache_v, gain_v, kvw_v, outw_v,
    mc_ref, sc_ref, ctx_ref, fresh_f, own_part, xnew, xnew_f, rs_send, rs_recv,
    pack, arr, info_pack, info_arr, place_v, place_s,
    perm_s, pick_ref, back_ref, sel_ref, sel2_ref, moved_ref, row_pack, row_arr,
    load_sem, outw_sem,
    rs_ss, rs_rs, ag_ss, ag_rs, hop_rs, fwd_ss, gc_ss, gc_rs, info_ss, info_rs, row_ss, row_rs,
    local_sem,
):
    G, L, T, micros, slots, width, ctx_len = sizes
    W = width // T
    H = HALVES
    S = W // H
    heads = W // HD
    pieces = heads + 2
    g = lax.axis_index("group")
    l = lax.axis_index("section")
    t = lax.axis_index("tensor")
    R = ROWS
    last = L - 1
    half = L // 2

    order = tuple(sorted(range(1, T), key=lambda d: -min(d, T - d)))

    def rs_copy(m, h, d):
        return pltpu.make_async_remote_copy(
            src_ref=rs_send.at[m, h, d - 1], dst_ref=rs_recv.at[m, h, d - 1],
            send_sem=rs_ss.at[m, h, d - 1], recv_sem=rs_rs.at[m, h],
            device_id={"tensor": lax.rem(t + d, T)}, device_id_type=MESH)

    def ag_copy(m, h, d):
        return pltpu.make_async_remote_copy(
            src_ref=xnew.at[m, h], dst_ref=xin.at[m, h, t],
            send_sem=ag_ss.at[m, h, d], recv_sem=ag_rs.at[m, h],
            device_id={"section": l + 1, "tensor": lax.rem(t + d, T)}, device_id_type=MESH)

    def hop_copy(m, h):
        return pltpu.make_async_remote_copy(
            src_ref=xnew.at[m, h], dst_ref=xin.at[m, h, t],
            send_sem=ag_ss.at[m, h, 0], recv_sem=hop_rs.at[m, h],
            device_id={"section": l + 1}, device_id_type=MESH)

    def fwd_copy(m, h, d):
        return pltpu.make_async_remote_copy(
            src_ref=xin.at[m, h, t], dst_ref=xin.at[m, h, t],
            send_sem=fwd_ss.at[m, h, d - 1], recv_sem=ag_rs.at[m, h],
            device_id={"tensor": lax.rem(t + d, T)}, device_id_type=MESH)

    def arrived(ref, sem):
        pltpu.make_async_copy(ref, ref, sem).wait()

    def to_group(src, dst, ss, rs, d):
        return pltpu.make_async_remote_copy(
            src_ref=src, dst_ref=dst, send_sem=ss.at[d - 1], recv_sem=rs.at[d - 1],
            device_id={"group": lax.rem(g + d, G)}, device_id_type=MESH)

    def gc_copy(d):
        e = PAIR * (d - 1)
        return to_group(pack.at[pl.ds(e, PAIR)], arr.at[pl.ds(e, PAIR)], gc_ss, gc_rs, d)

    def info_copy(d):
        return to_group(info_pack.at[d - 1], info_arr.at[d - 1], info_ss, info_rs, d)

    def row_copy(d):
        return to_group(row_pack.at[d - 1], row_arr.at[d - 1], row_ss, row_rs, d)

    def outw_load(h, d):
        start = pl.multiple_of(lax.rem(t + d, T) * W + h * S, S)
        place = order.index(d) if d else T - 1
        return pltpu.make_async_copy(
            outw.at[0, :, pl.ds(start, S)], outw_v.at[h, :, pl.ds(place * S, S)], outw_sem.at[h, d])

    query_load = pltpu.make_async_copy(query.at[0], q_v, load_sem.at[0])
    cache_load = pltpu.make_async_copy(cache.at[0], cache_v, load_sem.at[1])
    lens_load = pltpu.make_async_copy(lens_in, lens_ref, load_sem.at[5])
    moves_load = pltpu.make_async_copy(moves_in, moves_ref, load_sem.at[6])
    x_load = pltpu.make_async_copy(hidden, x0_v, load_sem.at[4])
    gain_load = pltpu.make_async_copy(gain, gain_v, load_sem.at[2])
    movers = moves_ref.shape[1]
    place_load = pltpu.make_async_copy(place_v.at[0], place_s, local_sem.at[0])

    lens_load.start()
    moves_load.start()
    query_load.start()
    cache_load.start()

    @pl.when(l == 0)
    def _():
        x_load.start()

    gain_load.start()
    for h in range(H):
        for q in range(T):
            pltpu.make_async_copy(
                kvw.at[0, pl.ds(q * W + h * S, S)], kvw_v.at[h, pl.ds(q * S, S)],
                load_sem.at[3]).start()

    for h in range(H):
        for d in order:
            outw_load(h, d).start()
    for h in range(H):
        outw_load(h, 0).start()

    barrier = pltpu.get_barrier_semaphore()
    for d in range(1, T):
        pl.semaphore_signal(barrier, inc=1, device_id={"tensor": lax.rem(t + d, T)}, device_id_type=MESH)
    for d in range(1, G):
        pl.semaphore_signal(barrier, inc=1, device_id={"group": lax.rem(g + d, G)}, device_id_type=MESH)

    @pl.when(l > 0)
    def _():
        for k in range(T):
            pl.semaphore_signal(
                barrier, inc=1, device_id={"section": l - 1, "tensor": k}, device_id_type=MESH)

    @pl.when((l > 0) & (l < last))
    def _():
        pl.semaphore_wait(barrier, T - 1 + G - 1 + T)

    @pl.when(l == last)
    def _():
        pl.semaphore_wait(barrier, T - 1 + G - 1)

    def arrange():
        leaving = [moves_ref[0, i] for i in range(movers)]
        ranked = list(leaving)
        for end in range(movers - 1, 0, -1):
            for i in range(end):
                low = jnp.minimum(ranked[i], ranked[i + 1])
                high = jnp.maximum(ranked[i], ranked[i + 1])
                ranked[i], ranked[i + 1] = low, high

        def staying(position):
            slot = position - movers
            for k in range(movers):
                slot = slot + (slot >= ranked[k]).astype(jnp.int32)
            return slot

        def slot_of(position):
            slot = staying(position)
            for i in range(movers):
                slot = jnp.where(position == i, leaving[i], slot)
            return slot

        def place(p, carry):
            perm_s[p] = staying(p)
            return carry

        for i in range(movers):
            perm_s[i] = leaving[i]
        lax.fori_loop(movers, slots, place, 0)
        square = (slots, slots)
        row, col = iota(square, 0), iota(square, 1)
        pick_ref[...] = jnp.where(slot_of(row) == col, 1.0, 0.0).astype(BF16)
        back_ref[...] = jnp.where((staying(col) == row) & (col >= movers), 1.0, 0.0).astype(BF16)

    block = 8
    blocks = slots // block

    def attend(first, end):
        span = block * ctx_len
        scale = HD ** -0.5

        def one(b, carry):
            rows = pl.ds(pl.multiple_of(b * block, block), block)
            lens = jnp.zeros((block, span), jnp.int32)
            row = iota((block, span), 0)
            slot = [perm_s[b * block + n] for n in range(block)]
            for n in range(block):
                lens = jnp.where(row == n, lens_ref[slot[n]], lens)
            tokens = jnp.concatenate([cache_v[slot[n]] for n in range(block)], axis=0)
            col = iota((block, span), 1)
            ok = (col // ctx_len == row) & (col % ctx_len < lens)
            bias = jnp.where(ok, 0.0, LOW).astype(F32)
            stacked = jnp.concatenate(
                [qf_v[rows, a * HD:(a + 1) * HD] for a in range(heads)], axis=0).astype(BF16)
            keys = tokens[:, 0:HD]
            values = tokens[:, HD:2 * HD]
            score = lax.dot_general(
                stacked, keys, (((1,), (1,)), ((), ())), preferred_element_type=F32)
            score = score.reshape(heads, block, span) * scale + bias[None]
            top = jnp.max(score, axis=-1, keepdims=True)
            weight = jnp.exp(score - top)
            total = jnp.sum(weight, axis=-1, keepdims=True)
            mixed = jnp.dot(
                weight.reshape(heads * block, span).astype(BF16), values,
                preferred_element_type=F32)
            ctx_ref[:, rows, :] = mixed.reshape(heads, block, HD)
            mc_ref[:, rows, :] = jnp.broadcast_to(top, (heads, block, HD))
            sc_ref[:, rows, :] = jnp.broadcast_to(total, (heads, block, HD))
            return carry

        lax.fori_loop(first, end, one, 0)

    def depart():
        lane = iota((8, 256), 1)
        sel_row = iota(sel_ref.shape, 0)
        slot_at = jnp.full(sel_ref.shape, NONE, jnp.int32)
        for d in range(1, G):
            e = d - 1
            dest = lax.rem(g + d, G)
            place_vec = jnp.zeros((8, 256), jnp.int32)
            len_vec = jnp.zeros((8, 256), jnp.int32)
            for i in range(PAIR):
                slot = jnp.int32(NONE)
                place = jnp.int32(NONE)
                from_slot = jnp.int32(0)
                for k in range(movers // PAIR):
                    hit = moves_ref[1, PAIR * k] == dest
                    slot = jnp.where(hit, PAIR * k + i, slot)
                    place = jnp.where(hit, moves_ref[2, PAIR * k + i], place)
                    from_slot = jnp.where(hit, moves_ref[0, PAIR * k + i], from_slot)
                here = lane // 16 == e * PAIR + i
                place_vec = jnp.where(here, place, place_vec)
                len_vec = jnp.where(here, lens_ref[from_slot], len_vec)
                slot_at = jnp.where(sel_row // 16 == e * PAIR + i, slot, slot_at)
                pack[PAIR * e + i] = cache_v[from_slot]
            info_pack[e, 0:8, :] = place_vec
            info_pack[e, 8:16, :] = len_vec
            info_copy(d).start()
            gc_copy(d).start()
        sel_col = iota(sel_ref.shape, 1)
        chosen = (sel_row % 16 == sel_col // R) & (slot_at == sel_col % R)
        sel_ref[...] = jnp.where(chosen, 1.0, 0.0).astype(BF16)

    def arrive():
        for d in range(1, G):
            info_copy(d).wait_recv()
        place = info_arr[0, 0:8, :]
        length = info_arr[0, 8:16, :]
        for e in range(1, G - 1):
            place = place + info_arr[e, 0:8, :]
            length = length + info_arr[e, 8:16, :]
        lane8 = iota((8, 256), 1)
        place = jnp.where(lane8 < (G - 1) * PAIR * 16, place, NONE)
        place_v[0] = place
        place_load.start()
        wide = (slots, 256)
        spot = jnp.broadcast_to(place[0:1, :], wide)
        long = jnp.broadcast_to(length[0:1, :], wide)
        lane = iota(wide, 1)
        row = iota(wide, 0)
        match = spot == row
        first = match & (lane % 16 == 0)
        has = jnp.max(jnp.where(first, 1.0, 0.0), axis=-1, keepdims=True)
        moved_len = jnp.max(jnp.where(first, long.astype(F32), 0.0), axis=-1, keepdims=True)
        own_len = jnp.zeros((slots, HD), F32)
        narrow = iota((slots, HD), 0)
        for n in range(slots):
            own_len = jnp.where(narrow == n, lens_ref[n].astype(F32), own_len)
        count_ref[...] = jnp.where(has > 0.5, moved_len, own_len).astype(jnp.int32)
        for c in range(pieces):
            sel2_ref[c * slots:(c + 1) * slots, :] = jnp.where(
                match & (lane % 16 == c), 1.0, 0.0).astype(BF16)
        for d in range(1, G):
            gc_copy(d).wait_recv()
        place_load.wait()

        def fill(j, carry):
            index = jnp.int32(-1)
            for e in range((G - 1) * PAIR):
                index = jnp.where(place_s[0, e * 16] == j, e, index)
            moved = arr[jnp.maximum(index, 0)]
            kept = cache_v[j]
            base_v[j] = lax.select_n(index >= 0, kept, moved)
            return carry

        lax.fori_loop(0, slots, fill, 0)

    def pass_on(m, h):
        arrived(xin.at[m, h, t], hop_rs.at[m, h])
        for d in order:
            fwd_copy(m, h, d).start()

    def forward(m):
        @pl.when(l == half)
        def _():
            pass_on(m, 0)

    def whole_fresh():
        acc = jnp.zeros((slots, 2 * HD), F32)
        square = jnp.zeros((slots, 1), F32)
        for h in range(H):
            scaled = []
            for q in range(T):
                cols = slice(q * W + h * S, q * W + (h + 1) * S)
                xq = x0_v[:, cols].astype(F32)
                square = square + jnp.sum(xq * xq, axis=-1, keepdims=True)
                scaled.append((xq * gain_v[:, cols]).astype(BF16))
            acc = acc + jnp.dot(
                jnp.concatenate(scaled, axis=1), kvw_v[h], preferred_element_type=F32)
        fresh = (acc * lax.rsqrt(square * (1.0 / width) + 1e-06)).astype(BF16)
        fresh_f[...] = jnp.dot(pick_ref[...], fresh, preferred_element_type=F32)
        mine = x0_v[:, pl.ds(pl.multiple_of(t * W, W), W)]
        ordered = jnp.dot(pick_ref[...], mine, preferred_element_type=F32).astype(BF16)
        for m in range(micros):
            for h in range(H):
                xin[m, h, t] = ordered[m * R:(m + 1) * R, h * S:(h + 1) * S]

    def fresh_part(m):
        rows = pl.ds(pl.multiple_of(m * R, R), R)
        acc = jnp.zeros((R, 2 * HD), F32)
        square = jnp.zeros((R, 1), F32)
        for h in range(H):

            if h:
                arrived(xin.at[m, h], ag_rs.at[m, h])
            else:

                @pl.when(l != half)
                def _():
                    arrived(xin.at[m, h], ag_rs.at[m, h])

                @pl.when(l == half)
                def _():
                    arrived(xin.at[m, h, pl.ds(0, T - 1)], ag_rs.at[m, h])

            scaled = []
            for q in range(T):
                cols = slice(q * W + h * S, q * W + (h + 1) * S)
                xq = xin[m, h, q].astype(F32)
                square = square + jnp.sum(xq * xq, axis=-1, keepdims=True)
                scaled.append((xq * gain_v[:, cols]).astype(BF16))
            acc = acc + jnp.dot(
                jnp.concatenate(scaled, axis=1), kvw_v[h], preferred_element_type=F32)
        fresh = (acc * lax.rsqrt(square * (1.0 / width) + 1e-06)).astype(BF16).astype(F32)
        fresh_f[rows, :] = fresh

    def front(m):
        rows = pl.ds(pl.multiple_of(m * R, R), R)

        @pl.when(l > 0)
        def _():
            fresh_part(m)

        fresh = fresh_f[rows, :]
        key = fresh[:, 0:HD]
        value = fresh[:, HD:2 * HD]
        parts = []
        for a in range(heads):
            qa = qf_v[rows, a * HD:(a + 1) * HD]
            own = jnp.sum(qa * key, axis=-1, keepdims=True) * (HD ** -0.5)
            old_top = mc_ref[a, rows, :]
            top = jnp.maximum(old_top, own)
            old_scale = jnp.exp(old_top - top)
            own_weight = jnp.exp(own - top)
            total = sc_ref[a, rows, :] * old_scale + own_weight
            mixed = (ctx_ref[a, rows, :] * old_scale + own_weight * value) / total
            parts.append(mixed.astype(BF16))
        return jnp.concatenate(parts, axis=1)

    def project(m, context, h):
        for i, d in enumerate(order):
            part = jnp.dot(
                context, outw_v[h, :, i * S:(i + 1) * S], preferred_element_type=F32)
            if i or h:
                rs_copy(m, h if i else h - 1, order[i - 1]).start()
            rs_send[m, h, d - 1] = part.astype(BF16)
        if h == H - 1:
            rs_copy(m, h, order[-1]).start()

    def project_own(m, context, h):
        own_part[m, h] = jnp.dot(
            context, outw_v[h, :, (T - 1) * S:T * S], preferred_element_type=F32)

    def reduce(m, h):
        total = own_part[m, h] + xin[m, h, t].astype(F32)
        arrived(rs_recv.at[m, h], rs_rs.at[m, h])
        for d in order:
            total = total + rs_recv[m, h, d - 1].astype(F32)
        rounded = total.astype(BF16)
        xnew[m, h] = rounded
        xnew_f[pl.ds(pl.multiple_of(m * R, R), R), h * S:(h + 1) * S] = rounded.astype(F32)

        @pl.when((l < last) if h else (l < last) & (l != half - 1))
        def _():
            for d in order + (0,):
                ag_copy(m, h, d).start()

        if h == 0:

            @pl.when(l == half - 1)
            def _():
                hop_copy(m, h).start()

    def exchange():
        stacked = jnp.concatenate(
            [xnew_f[0:R, c * HD:(c + 1) * HD] for c in range(heads)]
            + [fresh_f[0:R, c * HD:(c + 1) * HD] for c in range(2)], axis=0).astype(BF16)
        leaving = jnp.dot(sel_ref[...], stacked, preferred_element_type=F32).astype(BF16)
        for d in range(1, G):
            row_pack[d - 1] = leaving[(d - 1) * 32:d * 32]
            row_copy(d).start()

    def collect():
        row_arr[G - 1] = jnp.zeros((32, HD), BF16)
        for d in range(1, G):
            row_copy(d).wait_recv()
        moved_ref[...] = jnp.dot(
            sel2_ref[...], row_arr[...].reshape(G * 32, HD), preferred_element_type=F32)

    def settle():
        kept = jnp.dot(back_ref[...], fresh_f[...].astype(BF16), preferred_element_type=F32)
        token = iota((ctx_len, HD), 0)
        for k in range(2):
            cols = slice(k * HD, (k + 1) * HD)
            c = heads + k
            fresh = kept[:, cols] + moved_ref[c * slots:(c + 1) * slots, :]
            for j in range(slots):
                here = token == count_ref[j:j + 1, :]
                base_v[j, :, cols] = jnp.where(
                    here, fresh[j:j + 1, :], base_v[j, :, cols].astype(F32)).astype(BF16)

    lens_load.wait()
    moves_load.wait()
    arrange()
    query_load.wait()
    cache_load.wait()
    qf_v[...] = jnp.dot(pick_ref[...], q_v[...], preferred_element_type=F32)
    first = R // block
    attend(0, first)

    @pl.when(l > 0)
    def _():
        attend(first, blocks)
        depart()

    @pl.when(l == 0)
    def _():
        x_load.wait()
        gain_load.wait()
        arrived(kvw_v, load_sem.at[3])
        whole_fresh()

    @pl.when(l >= 3)
    def _():
        arrive()

    @pl.when(l > 0)
    def _():
        gain_load.wait()
        arrived(kvw_v, load_sem.at[3])

    forward(0)

    def batch(m, carry):
        context = front(m)

        @pl.when((l == 0) & (m == 0))
        def _():
            pl.semaphore_wait(barrier, T - 1 + G - 1 + T)

        @pl.when(m == 0)
        def _():
            for h in range(H):
                for d in order + (0,):
                    outw_load(h, d).wait()

        for h in range(H):
            project(m, context, h)

        @pl.when(m + 1 < micros)
        def _():
            forward(m + 1)

        for h in range(H):
            project_own(m, context, h)

        @pl.when((l == 0) & (m == 0))
        def _():
            attend(first, blocks)

        @pl.when((l == last) & (m == micros - 1))
        def _():
            collect()
            settle()

        for h in range(H):
            reduce(m, h)

        @pl.when((l == last) & (m == 0))
        def _():
            exchange()

        return carry

    lax.fori_loop(0, micros, batch, 0)

    @pl.when(l == 0)
    def _():
        depart()

    @pl.when(l < 3)
    def _():
        arrive()

    @pl.when(l < last)
    def _():
        exchange()
        collect()
        settle()

    kept = jnp.dot(back_ref[...], xnew_f[...].astype(BF16), preferred_element_type=F32)
    for c in range(heads):
        cols = slice(c * HD, (c + 1) * HD)
        xout_ref[:, cols] = (kept[:, cols] + moved_ref[c * slots:(c + 1) * slots, :]).astype(BF16)

    for m in range(micros):
        for h in range(H):
            for d in order:
                rs_copy(m, h, d).wait_send()
    for d in range(1, G):
        info_copy(d).wait_send()
        gc_copy(d).wait_send()
        row_copy(d).wait_send()

    @pl.when((l < last) & (l != half - 1))
    def _():
        for m in range(micros):
            for d in range(T):
                ag_copy(m, 0, d).wait_send()

    @pl.when(l < last)
    def _():
        for m in range(micros):
            for h in range(1, H):
                for d in range(T):
                    ag_copy(m, h, d).wait_send()

    @pl.when(l == half - 1)
    def _():
        for m in range(micros):
            hop_copy(m, 0).wait_send()

    @pl.when(l == half)
    def _():
        for m in range(micros):
            for d in order:
                fwd_copy(m, 0, d).wait_send()


def finish(chunks, xout, base, layer_out, new_cache, out_sem, x_sem):
    part = base.shape[0] // chunks

    def store(c):
        rows = pl.ds(c * part, part)
        return pltpu.make_async_copy(base.at[rows], new_cache.at[0, rows], out_sem.at[c])

    rows_copy = pltpu.make_async_copy(xout, layer_out.at[0], x_sem.at[0])
    for c in range(chunks):
        store(c).start()
    rows_copy.start()
    for c in range(chunks):
        store(c).wait()
    rows_copy.wait()


def per_device(sizes, hidden_in, queries, cache, lengths, moves, norm_gain, kv_weight, out_weight):
    G, L, T, micros, slots, width, ctx_len = sizes
    W = width // T
    heads = W // HD
    pieces = heads + 2
    R = ROWS
    H = HALVES
    S = W // H
    kv = 2 * HD
    movers = (G - 1) * PAIR
    any_spec = pl.BlockSpec(memory_space=pl.ANY)
    vmem = pl.BlockSpec(memory_space=pltpu.VMEM)
    dma = pltpu.SemaphoreType.DMA
    xout, base = pl.pallas_call(
        functools.partial(kernel, sizes),
        out_shape=(
            pltpu.VMEM((slots, W), BF16),
            pltpu.VMEM((slots, ctx_len, kv), BF16),
        ),
        in_specs=[any_spec] * 8,
        out_specs=(vmem, vmem),
        scratch_shapes=[
            pltpu.VMEM((slots, HD), jnp.int32),
            pltpu.SMEM(lengths.shape, jnp.int32),
            pltpu.SMEM(moves.shape[::-1], jnp.int32),
            pltpu.VMEM((micros, H, T, R, S), BF16),
            pltpu.VMEM((slots, width), BF16),
            pltpu.VMEM((slots, W), BF16),
            pltpu.VMEM((slots, W), F32),
            pltpu.VMEM((slots, ctx_len, kv), BF16),
            pltpu.VMEM((1, width), F32),
            pltpu.VMEM((H, T * S, kv), BF16),
            pltpu.VMEM((H, W, T * S), BF16),
            pltpu.VMEM((heads, slots, HD), F32),
            pltpu.VMEM((heads, slots, HD), F32),
            pltpu.VMEM((heads, slots, HD), F32),
            pltpu.VMEM((slots, kv), F32),
            pltpu.VMEM((micros, H, R, S), F32),
            pltpu.VMEM((micros, H, R, S), BF16),
            pltpu.VMEM((slots, W), F32),
            pltpu.VMEM((micros, H, T - 1, R, S), BF16),
            pltpu.VMEM((micros, H, T - 1, R, S), BF16),
            pltpu.VMEM((movers, ctx_len, kv), BF16),
            pltpu.VMEM((movers, ctx_len, kv), BF16),
            pltpu.VMEM((G - 1, 16, 256), jnp.int32),
            pltpu.VMEM((G - 1, 16, 256), jnp.int32),
            pltpu.VMEM((1, 8, 256), jnp.int32),
            pltpu.SMEM((8, 256), jnp.int32),
            pltpu.SMEM((slots,), jnp.int32),
            pltpu.VMEM((slots, slots), BF16),
            pltpu.VMEM((slots, slots), BF16),
            pltpu.VMEM(((G - 1) * 32, pieces * R), BF16),
            pltpu.VMEM((pieces * slots, 256), BF16),
            pltpu.VMEM((pieces * slots, HD), F32),
            pltpu.VMEM((G - 1, 32, HD), BF16),
            pltpu.VMEM((G, 32, HD), BF16),
            dma((7,)), dma((H, T)),
            dma((micros, H, T - 1)), dma((micros, H)),
            dma((micros, H, T)), dma((micros, H)), dma((micros, H)), dma((micros, H, T - 1)),
            dma((G - 1,)), dma((G - 1,)), dma((G - 1,)), dma((G - 1,)), dma((G - 1,)), dma((G - 1,)),
            dma((1,)),
        ],
        compiler_params=pltpu.CompilerParams(
            collective_id=0, has_side_effects=True, vmem_limit_bytes=56 * 1024 * 1024),
        name="chain",
    )(lengths, moves.T, hidden_in, queries, cache, norm_gain, kv_weight, out_weight)
    chunks = 4
    return pl.pallas_call(
        functools.partial(finish, chunks),
        out_shape=(
            jax.ShapeDtypeStruct((1, slots, W), BF16),
            jax.ShapeDtypeStruct((1, slots, ctx_len, kv), BF16),
        ),
        in_specs=[vmem] * 2,
        out_specs=(any_spec, any_spec),
        scratch_shapes=[dma((chunks,)), dma((1,))],
        compiler_params=pltpu.CompilerParams(vmem_limit_bytes=16 * 1024 * 1024),
        name="finish",
    )(*(pltpu.with_memory_space_constraint(part, pltpu.VMEM) for part in (xout, base)))


def solution(mesh):
    G, L, T = mesh.shape["group"], mesh.shape["section"], mesh.shape["tensor"]

    def whole(hidden_in, queries, cache, lengths, moves, norm_gain, kv_weight, out_weight):
        slots = hidden_in.shape[0] // G
        sizes = (G, L, T, slots // ROWS, slots, hidden_in.shape[1], cache.shape[2])
        return jax.shard_map(
            functools.partial(per_device, sizes),
            mesh=mesh,
            in_specs=(
                P("group", None),
                P("section", "group", "tensor"),
                P("section", "group", None, "tensor"),
                P("group"),
                P("group", None),
                P("section", None),
                P("section", None, "tensor"),
                P("section", "tensor", None),
            ),
            out_specs=(P("section", "group", "tensor"), P("section", "group", None, "tensor")),
            check_vma=False,
        )(hidden_in, queries, cache, lengths, moves, norm_gain, kv_weight, out_weight)

    return whole
```

```python
import functools

import jax
import jax.numpy as jnp
from jax import lax
from jax.experimental import pallas as pl
from jax.experimental.pallas import tpu as pltpu
from jax.sharding import PartitionSpec as P

HD = 128
PAIR = 2
ROWS = 16
HALVES = 2
MESH = pl.DeviceIdType.MESH
F32 = jnp.float32
BF16 = jnp.bfloat16
NONE = 255
LOW = -1e30


def iota(shape, axis):
    return lax.broadcasted_iota(jnp.int32, shape, axis)


def kernel(
    sizes,
    lens_in, moves_in, hidden, query, cache, gain, kvw, outw,
    xout_ref, base_v,
    count_ref, lens_ref, moves_ref, xin, x0_v, q_v, qf_v, cache_v, gain_v, kvw_v, outw_v,
    mc_ref, sc_ref, ctx_ref, fresh_f, own_part, xnew, xnew_f, rs_send, rs_recv,
    pack, arr, info_pack, info_arr, place_v, place_s,
    perm_s, pick_ref, back_ref, sel_ref, sel2_ref, moved_ref, row_pack, row_arr,
    load_sem, outw_sem,
    rs_ss, rs_rs, ag_ss, ag_rs, hop_rs, fwd_ss, gc_ss, gc_rs, info_ss, info_rs, row_ss, row_rs,
    local_sem,
):
    G, L, T, micros, slots, width, ctx_len = sizes
    W = width // T
    H = HALVES
    S = W // H
    heads = W // HD
    pieces = heads + 2
    g = lax.axis_index("group")
    l = lax.axis_index("section")
    t = lax.axis_index("tensor")
    R = ROWS
    last = L - 1
    half = L // 2

    order = tuple(sorted(range(1, T), key=lambda d: -min(d, T - d)))

    def rs_copy(m, h, d):
        return pltpu.make_async_remote_copy(
            src_ref=rs_send.at[m, h, d - 1], dst_ref=rs_recv.at[m, h, d - 1],
            send_sem=rs_ss.at[m, h, d - 1], recv_sem=rs_rs.at[m, h],
            device_id={"tensor": lax.rem(t + d, T)}, device_id_type=MESH)

    def ag_copy(m, h, d):
        return pltpu.make_async_remote_copy(
            src_ref=xnew.at[m, h], dst_ref=xin.at[m, h, t],
            send_sem=ag_ss.at[m, h, d], recv_sem=ag_rs.at[m, h],
            device_id={"section": l + 1, "tensor": lax.rem(t + d, T)}, device_id_type=MESH)

    def hop_copy(m, h):
        return pltpu.make_async_remote_copy(
            src_ref=xnew.at[m, h], dst_ref=xin.at[m, h, t],
            send_sem=ag_ss.at[m, h, 0], recv_sem=hop_rs.at[m, h],
            device_id={"section": l + 1}, device_id_type=MESH)

    def fwd_copy(m, h, d):
        return pltpu.make_async_remote_copy(
            src_ref=xin.at[m, h, t], dst_ref=xin.at[m, h, t],
            send_sem=fwd_ss.at[m, h, d - 1], recv_sem=ag_rs.at[m, h],
            device_id={"tensor": lax.rem(t + d, T)}, device_id_type=MESH)

    def arrived(ref, sem):
        pltpu.make_async_copy(ref, ref, sem).wait()

    def to_group(src, dst, ss, rs, d):
        return pltpu.make_async_remote_copy(
            src_ref=src, dst_ref=dst, send_sem=ss.at[d - 1], recv_sem=rs.at[d - 1],
            device_id={"group": lax.rem(g + d, G)}, device_id_type=MESH)

    def gc_copy(d):
        e = PAIR * (d - 1)
        return to_group(pack.at[pl.ds(e, PAIR)], arr.at[pl.ds(e, PAIR)], gc_ss, gc_rs, d)

    def info_copy(d):
        return to_group(info_pack.at[d - 1], info_arr.at[d - 1], info_ss, info_rs, d)

    def row_copy(d):
        return to_group(row_pack.at[d - 1], row_arr.at[d - 1], row_ss, row_rs, d)

    def outw_load(h, d):
        start = pl.multiple_of(lax.rem(t + d, T) * W + h * S, S)
        place = order.index(d) if d else T - 1
        return pltpu.make_async_copy(
            outw.at[0, :, pl.ds(start, S)], outw_v.at[h, :, pl.ds(place * S, S)], outw_sem.at[h, d])

    query_load = pltpu.make_async_copy(query.at[0], q_v, load_sem.at[0])
    cache_load = pltpu.make_async_copy(cache.at[0], cache_v, load_sem.at[1])
    lens_load = pltpu.make_async_copy(lens_in, lens_ref, load_sem.at[5])
    moves_load = pltpu.make_async_copy(moves_in, moves_ref, load_sem.at[6])
    x_load = pltpu.make_async_copy(hidden, x0_v, load_sem.at[4])
    gain_load = pltpu.make_async_copy(gain, gain_v, load_sem.at[2])
    movers = moves_ref.shape[1]
    place_load = pltpu.make_async_copy(place_v.at[0], place_s, local_sem.at[0])

    lens_load.start()
    moves_load.start()
    query_load.start()
    cache_load.start()

    @pl.when(l == 0)
    def _():
        x_load.start()

    gain_load.start()
    for h in range(H):
        for q in range(T):
            pltpu.make_async_copy(
                kvw.at[0, pl.ds(q * W + h * S, S)], kvw_v.at[h, pl.ds(q * S, S)],
                load_sem.at[3]).start()

    for h in range(H):
        for d in order:
            outw_load(h, d).start()
    for h in range(H):
        outw_load(h, 0).start()

    barrier = pltpu.get_barrier_semaphore()
    for d in range(1, T):
        pl.semaphore_signal(barrier, inc=1, device_id={"tensor": lax.rem(t + d, T)}, device_id_type=MESH)
    for d in range(1, G):
        pl.semaphore_signal(barrier, inc=1, device_id={"group": lax.rem(g + d, G)}, device_id_type=MESH)

    @pl.when(l > 0)
    def _():
        for k in range(T):
            pl.semaphore_signal(
                barrier, inc=1, device_id={"section": l - 1, "tensor": k}, device_id_type=MESH)

    @pl.when((l > 0) & (l < last))
    def _():
        pl.semaphore_wait(barrier, T - 1 + G - 1 + T)

    @pl.when(l == last)
    def _():
        pl.semaphore_wait(barrier, T - 1 + G - 1)

    def arrange():
        leaving = [moves_ref[0, i] for i in range(movers)]
        ranked = list(leaving)
        for end in range(movers - 1, 0, -1):
            for i in range(end):
                low = jnp.minimum(ranked[i], ranked[i + 1])
                high = jnp.maximum(ranked[i], ranked[i + 1])
                ranked[i], ranked[i + 1] = low, high

        def staying(position):
            slot = position - movers
            for k in range(movers):
                slot = slot + (slot >= ranked[k]).astype(jnp.int32)
            return slot

        def slot_of(position):
            slot = staying(position)
            for i in range(movers):
                slot = jnp.where(position == i, leaving[i], slot)
            return slot

        def place(p, carry):
            perm_s[p] = staying(p)
            return carry

        for i in range(movers):
            perm_s[i] = leaving[i]
        lax.fori_loop(movers, slots, place, 0)
        square = (slots, slots)
        row, col = iota(square, 0), iota(square, 1)
        pick_ref[...] = jnp.where(slot_of(row) == col, 1.0, 0.0).astype(BF16)
        back_ref[...] = jnp.where((staying(col) == row) & (col >= movers), 1.0, 0.0).astype(BF16)

    block = 8
    blocks = slots // block

    def attend(first, end):
        span = block * ctx_len
        scale = HD ** -0.5

        def one(b, carry):
            rows = pl.ds(pl.multiple_of(b * block, block), block)
            lens = jnp.zeros((block, span), jnp.int32)
            row = iota((block, span), 0)
            slot = [perm_s[b * block + n] for n in range(block)]
            for n in range(block):
                lens = jnp.where(row == n, lens_ref[slot[n]], lens)
            tokens = jnp.concatenate([cache_v[slot[n]] for n in range(block)], axis=0)
            col = iota((block, span), 1)
            ok = (col // ctx_len == row) & (col % ctx_len < lens)
            bias = jnp.where(ok, 0.0, LOW).astype(F32)
            stacked = jnp.concatenate(
                [qf_v[rows, a * HD:(a + 1) * HD] for a in range(heads)], axis=0).astype(BF16)
            keys = tokens[:, 0:HD]
            values = tokens[:, HD:2 * HD]
            score = lax.dot_general(
                stacked, keys, (((1,), (1,)), ((), ())), preferred_element_type=F32)
            score = score.reshape(heads, block, span) * scale + bias[None]
            top = jnp.max(score, axis=-1, keepdims=True)
            weight = jnp.exp(score - top)
            total = jnp.sum(weight, axis=-1, keepdims=True)
            mixed = jnp.dot(
                weight.reshape(heads * block, span).astype(BF16), values,
                preferred_element_type=F32)
            ctx_ref[:, rows, :] = mixed.reshape(heads, block, HD)
            mc_ref[:, rows, :] = jnp.broadcast_to(top, (heads, block, HD))
            sc_ref[:, rows, :] = jnp.broadcast_to(total, (heads, block, HD))
            return carry

        lax.fori_loop(first, end, one, 0)

    def depart():
        lane = iota((8, 256), 1)
        sel_row = iota(sel_ref.shape, 0)
        slot_at = jnp.full(sel_ref.shape, NONE, jnp.int32)
        for d in range(1, G):
            e = d - 1
            dest = lax.rem(g + d, G)
            place_vec = jnp.zeros((8, 256), jnp.int32)
            len_vec = jnp.zeros((8, 256), jnp.int32)
            for i in range(PAIR):
                slot = jnp.int32(NONE)
                place = jnp.int32(NONE)
                from_slot = jnp.int32(0)
                for k in range(movers // PAIR):
                    hit = moves_ref[1, PAIR * k] == dest
                    slot = jnp.where(hit, PAIR * k + i, slot)
                    place = jnp.where(hit, moves_ref[2, PAIR * k + i], place)
                    from_slot = jnp.where(hit, moves_ref[0, PAIR * k + i], from_slot)
                here = lane // 16 == e * PAIR + i
                place_vec = jnp.where(here, place, place_vec)
                len_vec = jnp.where(here, lens_ref[from_slot], len_vec)
                slot_at = jnp.where(sel_row // 16 == e * PAIR + i, slot, slot_at)
                pack[PAIR * e + i] = cache_v[from_slot]
            info_pack[e, 0:8, :] = place_vec
            info_pack[e, 8:16, :] = len_vec
            info_copy(d).start()
            gc_copy(d).start()
        sel_col = iota(sel_ref.shape, 1)
        chosen = (sel_row % 16 == sel_col // R) & (slot_at == sel_col % R)
        sel_ref[...] = jnp.where(chosen, 1.0, 0.0).astype(BF16)

    def arrive():
        for d in range(1, G):
            info_copy(d).wait_recv()
        place = info_arr[0, 0:8, :]
        length = info_arr[0, 8:16, :]
        for e in range(1, G - 1):
            place = place + info_arr[e, 0:8, :]
            length = length + info_arr[e, 8:16, :]
        lane8 = iota((8, 256), 1)
        place = jnp.where(lane8 < (G - 1) * PAIR * 16, place, NONE)
        place_v[0] = place
        place_load.start()
        wide = (slots, 256)
        spot = jnp.broadcast_to(place[0:1, :], wide)
        long = jnp.broadcast_to(length[0:1, :], wide)
        lane = iota(wide, 1)
        row = iota(wide, 0)
        match = spot == row
        first = match & (lane % 16 == 0)
        has = jnp.max(jnp.where(first, 1.0, 0.0), axis=-1, keepdims=True)
        moved_len = jnp.max(jnp.where(first, long.astype(F32), 0.0), axis=-1, keepdims=True)
        own_len = jnp.zeros((slots, HD), F32)
        narrow = iota((slots, HD), 0)
        for n in range(slots):
            own_len = jnp.where(narrow == n, lens_ref[n].astype(F32), own_len)
        count_ref[...] = jnp.where(has > 0.5, moved_len, own_len).astype(jnp.int32)
        for c in range(pieces):
            sel2_ref[c * slots:(c + 1) * slots, :] = jnp.where(
                match & (lane % 16 == c), 1.0, 0.0).astype(BF16)
        for d in range(1, G):
            gc_copy(d).wait_recv()
        place_load.wait()

        def fill(j, carry):
            index = jnp.int32(-1)
            for e in range((G - 1) * PAIR):
                index = jnp.where(place_s[0, e * 16] == j, e, index)
            moved = arr[jnp.maximum(index, 0)]
            kept = cache_v[j]
            base_v[j] = lax.select_n(index >= 0, kept, moved)
            return carry

        lax.fori_loop(0, slots, fill, 0)

    def pass_on(m, h):
        arrived(xin.at[m, h, t], hop_rs.at[m, h])
        for d in order:
            fwd_copy(m, h, d).start()

    def forward(m):
        @pl.when(l == half)
        def _():
            pass_on(m, 0)

    def whole_fresh():
        acc = jnp.zeros((slots, 2 * HD), F32)
        square = jnp.zeros((slots, 1), F32)
        for h in range(H):
            scaled = []
            for q in range(T):
                cols = slice(q * W + h * S, q * W + (h + 1) * S)
                xq = x0_v[:, cols].astype(F32)
                square = square + jnp.sum(xq * xq, axis=-1, keepdims=True)
                scaled.append((xq * gain_v[:, cols]).astype(BF16))
            acc = acc + jnp.dot(
                jnp.concatenate(scaled, axis=1), kvw_v[h], preferred_element_type=F32)
        fresh = (acc * lax.rsqrt(square * (1.0 / width) + 1e-06)).astype(BF16)
        fresh_f[...] = jnp.dot(pick_ref[...], fresh, preferred_element_type=F32)
        mine = x0_v[:, pl.ds(pl.multiple_of(t * W, W), W)]
        ordered = jnp.dot(pick_ref[...], mine, preferred_element_type=F32).astype(BF16)
        for m in range(micros):
            for h in range(H):
                xin[m, h, t] = ordered[m * R:(m + 1) * R, h * S:(h + 1) * S]

    def fresh_part(m):
        rows = pl.ds(pl.multiple_of(m * R, R), R)
        acc = jnp.zeros((R, 2 * HD), F32)
        square = jnp.zeros((R, 1), F32)
        for h in range(H):

            if h:
                arrived(xin.at[m, h], ag_rs.at[m, h])
            else:

                @pl.when(l != half)
                def _():
                    arrived(xin.at[m, h], ag_rs.at[m, h])

                @pl.when(l == half)
                def _():
                    arrived(xin.at[m, h, pl.ds(0, T - 1)], ag_rs.at[m, h])

            scaled = []
            for q in range(T):
                cols = slice(q * W + h * S, q * W + (h + 1) * S)
                xq = xin[m, h, q].astype(F32)
                square = square + jnp.sum(xq * xq, axis=-1, keepdims=True)
                scaled.append((xq * gain_v[:, cols]).astype(BF16))
            acc = acc + jnp.dot(
                jnp.concatenate(scaled, axis=1), kvw_v[h], preferred_element_type=F32)
        fresh = (acc * lax.rsqrt(square * (1.0 / width) + 1e-06)).astype(BF16).astype(F32)
        fresh_f[rows, :] = fresh
        return fresh

    def front(m, head):
        rows = pl.ds(pl.multiple_of(m * R, R), R)
        fresh = fresh_f[rows, :] if head else fresh_part(m)
        key = fresh[:, 0:HD]
        value = fresh[:, HD:2 * HD]
        parts = []
        for a in range(heads):
            qa = qf_v[rows, a * HD:(a + 1) * HD]
            own = jnp.sum(qa * key, axis=-1, keepdims=True) * (HD ** -0.5)
            old_top = mc_ref[a, rows, :]
            top = jnp.maximum(old_top, own)
            old_scale = jnp.exp(old_top - top)
            own_weight = jnp.exp(own - top)
            total = sc_ref[a, rows, :] * old_scale + own_weight
            mixed = (ctx_ref[a, rows, :] * old_scale + own_weight * value) / total
            parts.append(mixed.astype(BF16))
        return jnp.concatenate(parts, axis=1)

    def project(m, context, h):
        for i, d in enumerate(order):
            part = jnp.dot(
                context, outw_v[h, :, i * S:(i + 1) * S], preferred_element_type=F32)
            if i or h:
                rs_copy(m, h if i else h - 1, order[i - 1]).start()
            rs_send[m, h, d - 1] = part.astype(BF16)
        if h == H - 1:
            rs_copy(m, h, order[-1]).start()

    def project_own(m, context, h):
        own_part[m, h] = jnp.dot(
            context, outw_v[h, :, (T - 1) * S:T * S], preferred_element_type=F32)

    def reduce(m, h):
        total = own_part[m, h] + xin[m, h, t].astype(F32)
        arrived(rs_recv.at[m, h], rs_rs.at[m, h])
        for d in order:
            total = total + rs_recv[m, h, d - 1].astype(F32)
        rounded = total.astype(BF16)
        xnew[m, h] = rounded
        xnew_f[pl.ds(pl.multiple_of(m * R, R), R), h * S:(h + 1) * S] = rounded.astype(F32)

        @pl.when((l < last) if h else (l < last) & (l != half - 1))
        def _():
            for d in order + (0,):
                ag_copy(m, h, d).start()

        if h == 0:

            @pl.when(l == half - 1)
            def _():
                hop_copy(m, h).start()

    def exchange():
        stacked = jnp.concatenate(
            [xnew_f[0:R, c * HD:(c + 1) * HD] for c in range(heads)]
            + [fresh_f[0:R, c * HD:(c + 1) * HD] for c in range(2)], axis=0).astype(BF16)
        leaving = jnp.dot(sel_ref[...], stacked, preferred_element_type=F32).astype(BF16)
        for d in range(1, G):
            row_pack[d - 1] = leaving[(d - 1) * 32:d * 32]
            row_copy(d).start()

    def collect():
        row_arr[G - 1] = jnp.zeros((32, HD), BF16)
        for d in range(1, G):
            row_copy(d).wait_recv()
        moved_ref[...] = jnp.dot(
            sel2_ref[...], row_arr[...].reshape(G * 32, HD), preferred_element_type=F32)

    def settle():
        kept = jnp.dot(back_ref[...], fresh_f[...].astype(BF16), preferred_element_type=F32)
        token = iota((ctx_len, HD), 0)
        for k in range(2):
            cols = slice(k * HD, (k + 1) * HD)
            c = heads + k
            fresh = kept[:, cols] + moved_ref[c * slots:(c + 1) * slots, :]
            for j in range(slots):
                here = token == count_ref[j:j + 1, :]
                base_v[j, :, cols] = jnp.where(
                    here, fresh[j:j + 1, :], base_v[j, :, cols].astype(F32)).astype(BF16)

    lens_load.wait()
    moves_load.wait()
    arrange()
    query_load.wait()
    cache_load.wait()
    qf_v[...] = jnp.dot(pick_ref[...], q_v[...], preferred_element_type=F32)
    first = R // block
    attend(0, first)

    @pl.when(l > 0)
    def _():
        attend(first, blocks)
        depart()

    @pl.when(l == 0)
    def _():
        x_load.wait()
        gain_load.wait()
        arrived(kvw_v, load_sem.at[3])
        whole_fresh()

    @pl.when(l >= 3)
    def _():
        arrive()

    def weights_wait():
        for h in range(H):
            for d in order + (0,):
                outw_load(h, d).wait()

    def batch(m, head):
        context = front(m, head)

        if head:

            @pl.when(m == 0)
            def _():
                weights_wait()
                pl.semaphore_wait(barrier, T - 1 + G - 1 + T)

        for h in range(H):
            project(m, context, h)
        for h in range(H):
            project_own(m, context, h)

        if head:

            @pl.when(m == 0)
            def _():
                attend(first, blocks)

        else:

            @pl.when(m + 1 < micros)
            def _():
                forward(m + 1)

            @pl.when((l == last) & (m == micros - 1))
            def _():
                collect()
                settle()

        for h in range(H):
            reduce(m, h)

        if not head:

            @pl.when((l == last) & (m == 0))
            def _():
                exchange()

    @pl.when(l == 0)
    def _():
        lax.fori_loop(0, micros, lambda m, carry: batch(m, True) or carry, 0)

    @pl.when(l > 0)
    def _():
        gain_load.wait()
        arrived(kvw_v, load_sem.at[3])
        weights_wait()
        forward(0)
        lax.fori_loop(0, micros, lambda m, carry: batch(m, False) or carry, 0)

    @pl.when(l == 0)
    def _():
        depart()

    @pl.when(l < 3)
    def _():
        arrive()

    @pl.when(l < last)
    def _():
        exchange()
        collect()
        settle()

    kept = jnp.dot(back_ref[...], xnew_f[...].astype(BF16), preferred_element_type=F32)
    for c in range(heads):
        cols = slice(c * HD, (c + 1) * HD)
        xout_ref[:, cols] = (kept[:, cols] + moved_ref[c * slots:(c + 1) * slots, :]).astype(BF16)

    for m in range(micros):
        for h in range(H):
            for d in order:
                rs_copy(m, h, d).wait_send()
    for d in range(1, G):
        info_copy(d).wait_send()
        gc_copy(d).wait_send()
        row_copy(d).wait_send()

    @pl.when((l < last) & (l != half - 1))
    def _():
        for m in range(micros):
            for d in range(T):
                ag_copy(m, 0, d).wait_send()

    @pl.when(l < last)
    def _():
        for m in range(micros):
            for h in range(1, H):
                for d in range(T):
                    ag_copy(m, h, d).wait_send()

    @pl.when(l == half - 1)
    def _():
        for m in range(micros):
            hop_copy(m, 0).wait_send()

    @pl.when(l == half)
    def _():
        for m in range(micros):
            for d in order:
                fwd_copy(m, 0, d).wait_send()


def finish(chunks, xout, base, layer_out, new_cache, out_sem, x_sem):
    part = base.shape[0] // chunks

    def store(c):
        rows = pl.ds(c * part, part)
        return pltpu.make_async_copy(base.at[rows], new_cache.at[0, rows], out_sem.at[c])

    rows_copy = pltpu.make_async_copy(xout, layer_out.at[0], x_sem.at[0])
    for c in range(chunks):
        store(c).start()
    rows_copy.start()
    for c in range(chunks):
        store(c).wait()
    rows_copy.wait()


def per_device(sizes, hidden_in, queries, cache, lengths, moves, norm_gain, kv_weight, out_weight):
    G, L, T, micros, slots, width, ctx_len = sizes
    W = width // T
    heads = W // HD
    pieces = heads + 2
    R = ROWS
    H = HALVES
    S = W // H
    kv = 2 * HD
    movers = (G - 1) * PAIR
    any_spec = pl.BlockSpec(memory_space=pl.ANY)
    vmem = pl.BlockSpec(memory_space=pltpu.VMEM)
    dma = pltpu.SemaphoreType.DMA
    xout, base = pl.pallas_call(
        functools.partial(kernel, sizes),
        out_shape=(
            pltpu.VMEM((slots, W), BF16),
            pltpu.VMEM((slots, ctx_len, kv), BF16),
        ),
        in_specs=[any_spec] * 8,
        out_specs=(vmem, vmem),
        scratch_shapes=[
            pltpu.VMEM((slots, HD), jnp.int32),
            pltpu.SMEM(lengths.shape, jnp.int32),
            pltpu.SMEM(moves.shape[::-1], jnp.int32),
            pltpu.VMEM((micros, H, T, R, S), BF16),
            pltpu.VMEM((slots, width), BF16),
            pltpu.VMEM((slots, W), BF16),
            pltpu.VMEM((slots, W), F32),
            pltpu.VMEM((slots, ctx_len, kv), BF16),
            pltpu.VMEM((1, width), F32),
            pltpu.VMEM((H, T * S, kv), BF16),
            pltpu.VMEM((H, W, T * S), BF16),
            pltpu.VMEM((heads, slots, HD), F32),
            pltpu.VMEM((heads, slots, HD), F32),
            pltpu.VMEM((heads, slots, HD), F32),
            pltpu.VMEM((slots, kv), F32),
            pltpu.VMEM((micros, H, R, S), F32),
            pltpu.VMEM((micros, H, R, S), BF16),
            pltpu.VMEM((slots, W), F32),
            pltpu.VMEM((micros, H, T - 1, R, S), BF16),
            pltpu.VMEM((micros, H, T - 1, R, S), BF16),
            pltpu.VMEM((movers, ctx_len, kv), BF16),
            pltpu.VMEM((movers, ctx_len, kv), BF16),
            pltpu.VMEM((G - 1, 16, 256), jnp.int32),
            pltpu.VMEM((G - 1, 16, 256), jnp.int32),
            pltpu.VMEM((1, 8, 256), jnp.int32),
            pltpu.SMEM((8, 256), jnp.int32),
            pltpu.SMEM((slots,), jnp.int32),
            pltpu.VMEM((slots, slots), BF16),
            pltpu.VMEM((slots, slots), BF16),
            pltpu.VMEM(((G - 1) * 32, pieces * R), BF16),
            pltpu.VMEM((pieces * slots, 256), BF16),
            pltpu.VMEM((pieces * slots, HD), F32),
            pltpu.VMEM((G - 1, 32, HD), BF16),
            pltpu.VMEM((G, 32, HD), BF16),
            dma((7,)), dma((H, T)),
            dma((micros, H, T - 1)), dma((micros, H)),
            dma((micros, H, T)), dma((micros, H)), dma((micros, H)), dma((micros, H, T - 1)),
            dma((G - 1,)), dma((G - 1,)), dma((G - 1,)), dma((G - 1,)), dma((G - 1,)), dma((G - 1,)),
            dma((1,)),
        ],
        compiler_params=pltpu.CompilerParams(
            collective_id=0, has_side_effects=True, vmem_limit_bytes=56 * 1024 * 1024),
        name="chain",
    )(lengths, moves.T, hidden_in, queries, cache, norm_gain, kv_weight, out_weight)
    chunks = 4
    return pl.pallas_call(
        functools.partial(finish, chunks),
        out_shape=(
            jax.ShapeDtypeStruct((1, slots, W), BF16),
            jax.ShapeDtypeStruct((1, slots, ctx_len, kv), BF16),
        ),
        in_specs=[vmem] * 2,
        out_specs=(any_spec, any_spec),
        scratch_shapes=[dma((chunks,)), dma((1,))],
        compiler_params=pltpu.CompilerParams(vmem_limit_bytes=16 * 1024 * 1024),
        name="finish",
    )(*(pltpu.with_memory_space_constraint(part, pltpu.VMEM) for part in (xout, base)))


def solution(mesh):
    G, L, T = mesh.shape["group"], mesh.shape["section"], mesh.shape["tensor"]

    def whole(hidden_in, queries, cache, lengths, moves, norm_gain, kv_weight, out_weight):
        slots = hidden_in.shape[0] // G
        sizes = (G, L, T, slots // ROWS, slots, hidden_in.shape[1], cache.shape[2])
        return jax.shard_map(
            functools.partial(per_device, sizes),
            mesh=mesh,
            in_specs=(
                P("group", None),
                P("section", "group", "tensor"),
                P("section", "group", None, "tensor"),
                P("group"),
                P("group", None),
                P("section", None),
                P("section", None, "tensor"),
                P("section", "tensor", None),
            ),
            out_specs=(P("section", "group", "tensor"), P("section", "group", None, "tensor")),
            check_vma=False,
        )(hidden_in, queries, cache, lengths, moves, norm_gain, kv_weight, out_weight)

    return whole
```

```python
import functools

import jax
import jax.numpy as jnp
from jax import lax
from jax.experimental import pallas as pl
from jax.experimental.pallas import tpu as pltpu
from jax.sharding import PartitionSpec as P

HD = 128
PAIR = 2
ROWS = 16
HALVES = 2
MESH = pl.DeviceIdType.MESH
F32 = jnp.float32
BF16 = jnp.bfloat16
NONE = 255
LOW = -1e30


def iota(shape, axis):
    return lax.broadcasted_iota(jnp.int32, shape, axis)


def kernel(
    sizes,
    lens_in, moves_in, hidden, query, cache, gain, kvw, outw,
    xout_ref, base_v,
    count_ref, lens_ref, moves_ref, xin, x0_v, q_v, qf_v, cache_v, gain_v, kvw_v, outw_v,
    mc_ref, sc_ref, ctx_ref, fresh_f, own_part, xnew, xnew_f, rs_send, rs_recv,
    pack, arr, info_pack, info_arr, place_v, place_s,
    perm_s, pick_ref, back_ref, sel_ref, sel2_ref, moved_ref, row_pack, row_arr,
    load_sem, outw_sem,
    rs_ss, rs_rs, ag_ss, ag_rs, hop_rs, fwd_ss, gc_ss, gc_rs, info_ss, info_rs, row_ss, row_rs,
    local_sem,
):
    G, L, T, micros, slots, width, ctx_len = sizes
    W = width // T
    H = HALVES
    S = W // H
    heads = W // HD
    pieces = heads + 2
    g = lax.axis_index("group")
    l = lax.axis_index("section")
    t = lax.axis_index("tensor")
    R = ROWS
    last = L - 1
    half = L // 2

    order = tuple(sorted(range(1, T), key=lambda d: -min(d, T - d)))

    def rs_copy(m, h, d):
        return pltpu.make_async_remote_copy(
            src_ref=rs_send.at[m, h, d - 1], dst_ref=rs_recv.at[m, h, d - 1],
            send_sem=rs_ss.at[m, h, d - 1], recv_sem=rs_rs.at[m, h],
            device_id={"tensor": lax.rem(t + d, T)}, device_id_type=MESH)

    def ag_copy(m, h, d):
        return pltpu.make_async_remote_copy(
            src_ref=xnew.at[m, h], dst_ref=xin.at[m, h, t],
            send_sem=ag_ss.at[m, h, d], recv_sem=ag_rs.at[m, h],
            device_id={"section": l + 1, "tensor": lax.rem(t + d, T)}, device_id_type=MESH)

    def hop_copy(m, h):
        return pltpu.make_async_remote_copy(
            src_ref=xnew.at[m, h], dst_ref=xin.at[m, h, t],
            send_sem=ag_ss.at[m, h, 0], recv_sem=hop_rs.at[m, h],
            device_id={"section": l + 1}, device_id_type=MESH)

    def fwd_copy(m, h, d):
        return pltpu.make_async_remote_copy(
            src_ref=xin.at[m, h, t], dst_ref=xin.at[m, h, t],
            send_sem=fwd_ss.at[m, h, d - 1], recv_sem=ag_rs.at[m, h],
            device_id={"tensor": lax.rem(t + d, T)}, device_id_type=MESH)

    def arrived(ref, sem):
        pltpu.make_async_copy(ref, ref, sem).wait()

    def to_group(src, dst, ss, rs, d):
        return pltpu.make_async_remote_copy(
            src_ref=src, dst_ref=dst, send_sem=ss.at[d - 1], recv_sem=rs.at[d - 1],
            device_id={"group": lax.rem(g + d, G)}, device_id_type=MESH)

    def gc_copy(d):
        e = PAIR * (d - 1)
        return to_group(pack.at[pl.ds(e, PAIR)], arr.at[pl.ds(e, PAIR)], gc_ss, gc_rs, d)

    def info_copy(d):
        return to_group(info_pack.at[d - 1], info_arr.at[d - 1], info_ss, info_rs, d)

    def row_copy(d):
        return to_group(row_pack.at[d - 1], row_arr.at[d - 1], row_ss, row_rs, d)

    def outw_load(h, d):
        start = pl.multiple_of(lax.rem(t + d, T) * W + h * S, S)
        place = order.index(d) if d else T - 1
        return pltpu.make_async_copy(
            outw.at[0, :, pl.ds(start, S)], outw_v.at[h, :, pl.ds(place * S, S)], outw_sem.at[h, d])

    query_load = pltpu.make_async_copy(query.at[0], q_v, load_sem.at[0])
    cache_load = pltpu.make_async_copy(cache.at[0], cache_v, load_sem.at[1])
    lens_load = pltpu.make_async_copy(lens_in, lens_ref, load_sem.at[5])
    moves_load = pltpu.make_async_copy(moves_in, moves_ref, load_sem.at[6])
    x_load = pltpu.make_async_copy(hidden, x0_v, load_sem.at[4])
    gain_load = pltpu.make_async_copy(gain, gain_v, load_sem.at[2])
    movers = moves_ref.shape[1]
    place_load = pltpu.make_async_copy(place_v.at[0], place_s, local_sem.at[0])

    lens_load.start()
    moves_load.start()
    query_load.start()
    cache_load.start()

    @pl.when(l == 0)
    def _():
        x_load.start()

    gain_load.start()
    for h in range(H):
        for q in range(T):
            pltpu.make_async_copy(
                kvw.at[0, pl.ds(q * W + h * S, S)], kvw_v.at[h, pl.ds(q * S, S)],
                load_sem.at[3]).start()

    barrier = pltpu.get_barrier_semaphore()
    for d in range(1, T):
        pl.semaphore_signal(barrier, inc=1, device_id={"tensor": lax.rem(t + d, T)}, device_id_type=MESH)
    for d in range(1, G):
        pl.semaphore_signal(barrier, inc=1, device_id={"group": lax.rem(g + d, G)}, device_id_type=MESH)

    @pl.when(l > 0)
    def _():
        for k in range(T):
            pl.semaphore_signal(
                barrier, inc=1, device_id={"section": l - 1, "tensor": k}, device_id_type=MESH)

    @pl.when((l > 0) & (l < last))
    def _():
        pl.semaphore_wait(barrier, T - 1 + G - 1 + T)

    @pl.when(l == last)
    def _():
        pl.semaphore_wait(barrier, T - 1 + G - 1)

    def arrange():
        leaving = [moves_ref[0, i] for i in range(movers)]
        ranked = list(leaving)
        for end in range(movers - 1, 0, -1):
            for i in range(end):
                low = jnp.minimum(ranked[i], ranked[i + 1])
                high = jnp.maximum(ranked[i], ranked[i + 1])
                ranked[i], ranked[i + 1] = low, high

        def staying(position):
            slot = position - movers
            for k in range(movers):
                slot = slot + (slot >= ranked[k]).astype(jnp.int32)
            return slot

        def slot_of(position):
            slot = staying(position)
            for i in range(movers):
                slot = jnp.where(position == i, leaving[i], slot)
            return slot

        def place(p, carry):
            perm_s[p] = staying(p)
            return carry

        for i in range(movers):
            perm_s[i] = leaving[i]
        lax.fori_loop(movers, slots, place, 0)
        square = (slots, slots)
        row, col = iota(square, 0), iota(square, 1)
        pick_ref[...] = jnp.where(slot_of(row) == col, 1.0, 0.0).astype(BF16)
        back_ref[...] = jnp.where((staying(col) == row) & (col >= movers), 1.0, 0.0).astype(BF16)

    block = 8
    blocks = slots // block

    def attend(first, end):
        span = block * ctx_len
        scale = HD ** -0.5

        def one(b, carry):
            rows = pl.ds(pl.multiple_of(b * block, block), block)
            lens = jnp.zeros((block, span), jnp.int32)
            row = iota((block, span), 0)
            slot = [perm_s[b * block + n] for n in range(block)]
            for n in range(block):
                lens = jnp.where(row == n, lens_ref[slot[n]], lens)
            tokens = jnp.concatenate([cache_v[slot[n]] for n in range(block)], axis=0)
            col = iota((block, span), 1)
            ok = (col // ctx_len == row) & (col % ctx_len < lens)
            bias = jnp.where(ok, 0.0, LOW).astype(F32)
            stacked = jnp.concatenate(
                [qf_v[rows, a * HD:(a + 1) * HD] for a in range(heads)], axis=0).astype(BF16)
            keys = tokens[:, 0:HD]
            values = tokens[:, HD:2 * HD]
            score = lax.dot_general(
                stacked, keys, (((1,), (1,)), ((), ())), preferred_element_type=F32)
            score = score.reshape(heads, block, span) * scale + bias[None]
            top = jnp.max(score, axis=-1, keepdims=True)
            weight = jnp.exp(score - top)
            total = jnp.sum(weight, axis=-1, keepdims=True)
            mixed = jnp.dot(
                weight.reshape(heads * block, span).astype(BF16), values,
                preferred_element_type=F32)
            ctx_ref[:, rows, :] = mixed.reshape(heads, block, HD)
            mc_ref[:, rows, :] = jnp.broadcast_to(top, (heads, block, HD))
            sc_ref[:, rows, :] = jnp.broadcast_to(total, (heads, block, HD))
            return carry

        lax.fori_loop(first, end, one, 0)

    def depart():
        lane = iota((8, 256), 1)
        sel_row = iota(sel_ref.shape, 0)
        slot_at = jnp.full(sel_ref.shape, NONE, jnp.int32)
        for d in range(1, G):
            e = d - 1
            dest = lax.rem(g + d, G)
            place_vec = jnp.zeros((8, 256), jnp.int32)
            len_vec = jnp.zeros((8, 256), jnp.int32)
            for i in range(PAIR):
                slot = jnp.int32(NONE)
                place = jnp.int32(NONE)
                from_slot = jnp.int32(0)
                for k in range(movers // PAIR):
                    hit = moves_ref[1, PAIR * k] == dest
                    slot = jnp.where(hit, PAIR * k + i, slot)
                    place = jnp.where(hit, moves_ref[2, PAIR * k + i], place)
                    from_slot = jnp.where(hit, moves_ref[0, PAIR * k + i], from_slot)
                here = lane // 16 == e * PAIR + i
                place_vec = jnp.where(here, place, place_vec)
                len_vec = jnp.where(here, lens_ref[from_slot], len_vec)
                slot_at = jnp.where(sel_row // 16 == e * PAIR + i, slot, slot_at)
                pack[PAIR * e + i] = cache_v[from_slot]
            info_pack[e, 0:8, :] = place_vec
            info_pack[e, 8:16, :] = len_vec
            info_copy(d).start()
            gc_copy(d).start()
        sel_col = iota(sel_ref.shape, 1)
        chosen = (sel_row % 16 == sel_col // R) & (slot_at == sel_col % R)
        sel_ref[...] = jnp.where(chosen, 1.0, 0.0).astype(BF16)

    def arrive():
        for d in range(1, G):
            info_copy(d).wait_recv()
        place = info_arr[0, 0:8, :]
        length = info_arr[0, 8:16, :]
        for e in range(1, G - 1):
            place = place + info_arr[e, 0:8, :]
            length = length + info_arr[e, 8:16, :]
        lane8 = iota((8, 256), 1)
        place = jnp.where(lane8 < (G - 1) * PAIR * 16, place, NONE)
        place_v[0] = place
        place_load.start()
        wide = (slots, 256)
        spot = jnp.broadcast_to(place[0:1, :], wide)
        long = jnp.broadcast_to(length[0:1, :], wide)
        lane = iota(wide, 1)
        row = iota(wide, 0)
        match = spot == row
        first = match & (lane % 16 == 0)
        has = jnp.max(jnp.where(first, 1.0, 0.0), axis=-1, keepdims=True)
        moved_len = jnp.max(jnp.where(first, long.astype(F32), 0.0), axis=-1, keepdims=True)
        own_len = jnp.zeros((slots, HD), F32)
        narrow = iota((slots, HD), 0)
        for n in range(slots):
            own_len = jnp.where(narrow == n, lens_ref[n].astype(F32), own_len)
        count_ref[...] = jnp.where(has > 0.5, moved_len, own_len).astype(jnp.int32)
        for c in range(pieces):
            sel2_ref[c * slots:(c + 1) * slots, :] = jnp.where(
                match & (lane % 16 == c), 1.0, 0.0).astype(BF16)
        for d in range(1, G):
            gc_copy(d).wait_recv()
        place_load.wait()

        def fill(j, carry):
            index = jnp.int32(-1)
            for e in range((G - 1) * PAIR):
                index = jnp.where(place_s[0, e * 16] == j, e, index)
            moved = arr[jnp.maximum(index, 0)]
            kept = cache_v[j]
            base_v[j] = lax.select_n(index >= 0, kept, moved)
            return carry

        lax.fori_loop(0, slots, fill, 0)

    def pass_on(m, h):
        arrived(xin.at[m, h, t], hop_rs.at[m, h])
        for d in order:
            fwd_copy(m, h, d).start()

    def forward(m):
        @pl.when(l == half)
        def _():
            pass_on(m, 0)

    def whole_fresh():
        acc = jnp.zeros((slots, 2 * HD), F32)
        square = jnp.zeros((slots, 1), F32)
        for h in range(H):
            scaled = []
            for q in range(T):
                cols = slice(q * W + h * S, q * W + (h + 1) * S)
                xq = x0_v[:, cols].astype(F32)
                square = square + jnp.sum(xq * xq, axis=-1, keepdims=True)
                scaled.append((xq * gain_v[:, cols]).astype(BF16))
            acc = acc + jnp.dot(
                jnp.concatenate(scaled, axis=1), kvw_v[h], preferred_element_type=F32)
        fresh = (acc * lax.rsqrt(square * (1.0 / width) + 1e-06)).astype(BF16)
        fresh_f[...] = jnp.dot(pick_ref[...], fresh, preferred_element_type=F32)
        mine = x0_v[:, pl.ds(pl.multiple_of(t * W, W), W)]
        ordered = jnp.dot(pick_ref[...], mine, preferred_element_type=F32).astype(BF16)
        for m in range(micros):
            for h in range(H):
                xin[m, h, t] = ordered[m * R:(m + 1) * R, h * S:(h + 1) * S]

    def fresh_part(m):
        rows = pl.ds(pl.multiple_of(m * R, R), R)
        acc = jnp.zeros((R, 2 * HD), F32)
        square = jnp.zeros((R, 1), F32)
        for h in range(H):

            if h:
                arrived(xin.at[m, h], ag_rs.at[m, h])
            else:

                @pl.when(l != half)
                def _():
                    arrived(xin.at[m, h], ag_rs.at[m, h])

                @pl.when(l == half)
                def _():
                    arrived(xin.at[m, h, pl.ds(0, T - 1)], ag_rs.at[m, h])

            scaled = []
            for q in range(T):
                cols = slice(q * W + h * S, q * W + (h + 1) * S)
                xq = xin[m, h, q].astype(F32)
                square = square + jnp.sum(xq * xq, axis=-1, keepdims=True)
                scaled.append((xq * gain_v[:, cols]).astype(BF16))
            acc = acc + jnp.dot(
                jnp.concatenate(scaled, axis=1), kvw_v[h], preferred_element_type=F32)
        fresh = (acc * lax.rsqrt(square * (1.0 / width) + 1e-06)).astype(BF16).astype(F32)
        fresh_f[rows, :] = fresh

    def front(m):
        rows = pl.ds(pl.multiple_of(m * R, R), R)

        @pl.when(l > 0)
        def _():
            fresh_part(m)

        fresh = fresh_f[rows, :]
        key = fresh[:, 0:HD]
        value = fresh[:, HD:2 * HD]
        parts = []
        for a in range(heads):
            qa = qf_v[rows, a * HD:(a + 1) * HD]
            own = jnp.sum(qa * key, axis=-1, keepdims=True) * (HD ** -0.5)
            old_top = mc_ref[a, rows, :]
            top = jnp.maximum(old_top, own)
            old_scale = jnp.exp(old_top - top)
            own_weight = jnp.exp(own - top)
            total = sc_ref[a, rows, :] * old_scale + own_weight
            mixed = (ctx_ref[a, rows, :] * old_scale + own_weight * value) / total
            parts.append(mixed.astype(BF16))
        return jnp.concatenate(parts, axis=1)

    def project(m, context, h):
        for i, d in enumerate(order):
            part = jnp.dot(
                context, outw_v[h, :, i * S:(i + 1) * S], preferred_element_type=F32)
            if i or h:
                rs_copy(m, h if i else h - 1, order[i - 1]).start()
            rs_send[m, h, d - 1] = part.astype(BF16)
        if h == H - 1:
            rs_copy(m, h, order[-1]).start()

    def project_own(m, context, h):
        own_part[m, h] = jnp.dot(
            context, outw_v[h, :, (T - 1) * S:T * S], preferred_element_type=F32)

    def reduce(m, h):
        total = own_part[m, h] + xin[m, h, t].astype(F32)
        arrived(rs_recv.at[m, h], rs_rs.at[m, h])
        for d in order:
            total = total + rs_recv[m, h, d - 1].astype(F32)
        rounded = total.astype(BF16)
        xnew[m, h] = rounded
        xnew_f[pl.ds(pl.multiple_of(m * R, R), R), h * S:(h + 1) * S] = rounded.astype(F32)

        @pl.when((l < last) if h else (l < last) & (l != half - 1))
        def _():
            for d in order + (0,):
                ag_copy(m, h, d).start()

        if h == 0:

            @pl.when(l == half - 1)
            def _():
                hop_copy(m, h).start()

    def exchange():
        stacked = jnp.concatenate(
            [xnew_f[0:R, c * HD:(c + 1) * HD] for c in range(heads)]
            + [fresh_f[0:R, c * HD:(c + 1) * HD] for c in range(2)], axis=0).astype(BF16)
        leaving = jnp.dot(sel_ref[...], stacked, preferred_element_type=F32).astype(BF16)
        for d in range(1, G):
            row_pack[d - 1] = leaving[(d - 1) * 32:d * 32]
            row_copy(d).start()

    def collect():
        row_arr[G - 1] = jnp.zeros((32, HD), BF16)
        for d in range(1, G):
            row_copy(d).wait_recv()
        moved_ref[...] = jnp.dot(
            sel2_ref[...], row_arr[...].reshape(G * 32, HD), preferred_element_type=F32)

    def settle():
        kept = jnp.dot(back_ref[...], fresh_f[...].astype(BF16), preferred_element_type=F32)
        token = iota((ctx_len, HD), 0)
        for k in range(2):
            cols = slice(k * HD, (k + 1) * HD)
            c = heads + k
            fresh = kept[:, cols] + moved_ref[c * slots:(c + 1) * slots, :]
            for j in range(slots):
                here = token == count_ref[j:j + 1, :]
                base_v[j, :, cols] = jnp.where(
                    here, fresh[j:j + 1, :], base_v[j, :, cols].astype(F32)).astype(BF16)

    lens_load.wait()
    moves_load.wait()
    arrange()
    for h in range(H):
        for d in order:
            outw_load(h, d).start()
    query_load.wait()
    cache_load.wait()
    qf_v[...] = jnp.dot(pick_ref[...], q_v[...], preferred_element_type=F32)
    first = R // block
    attend(0, first)
    for h in range(H):
        outw_load(h, 0).start()

    @pl.when(l > 0)
    def _():
        attend(first, blocks)
        depart()

    @pl.when(l == 0)
    def _():
        x_load.wait()
        gain_load.wait()
        arrived(kvw_v, load_sem.at[3])
        whole_fresh()

    @pl.when(l >= 3)
    def _():
        arrive()

    @pl.when(l > 0)
    def _():
        gain_load.wait()
        arrived(kvw_v, load_sem.at[3])

    forward(0)

    def batch(m, carry):
        context = front(m)

        @pl.when((l == 0) & (m == 0))
        def _():
            pl.semaphore_wait(barrier, T - 1 + G - 1 + T)

        @pl.when(m == 0)
        def _():
            for h in range(H):
                for d in order + (0,):
                    outw_load(h, d).wait()

        for h in range(H):
            project(m, context, h)

        @pl.when(m + 1 < micros)
        def _():
            forward(m + 1)

        for h in range(H):
            project_own(m, context, h)

        @pl.when((l == 0) & (m == 0))
        def _():
            attend(first, blocks)

        @pl.when((l == last) & (m == micros - 1))
        def _():
            collect()
            settle()

        for h in range(H):
            reduce(m, h)

        @pl.when((l == last) & (m == 0))
        def _():
            exchange()

        return carry

    lax.fori_loop(0, micros, batch, 0)

    @pl.when(l == 0)
    def _():
        depart()

    @pl.when(l < 3)
    def _():
        arrive()

    @pl.when(l < last)
    def _():
        exchange()
        collect()
        settle()

    kept = jnp.dot(back_ref[...], xnew_f[...].astype(BF16), preferred_element_type=F32)
    for c in range(heads):
        cols = slice(c * HD, (c + 1) * HD)
        xout_ref[:, cols] = (kept[:, cols] + moved_ref[c * slots:(c + 1) * slots, :]).astype(BF16)

    for m in range(micros):
        for h in range(H):
            for d in order:
                rs_copy(m, h, d).wait_send()
    for d in range(1, G):
        info_copy(d).wait_send()
        gc_copy(d).wait_send()
        row_copy(d).wait_send()

    @pl.when((l < last) & (l != half - 1))
    def _():
        for m in range(micros):
            for d in range(T):
                ag_copy(m, 0, d).wait_send()

    @pl.when(l < last)
    def _():
        for m in range(micros):
            for h in range(1, H):
                for d in range(T):
                    ag_copy(m, h, d).wait_send()

    @pl.when(l == half - 1)
    def _():
        for m in range(micros):
            hop_copy(m, 0).wait_send()

    @pl.when(l == half)
    def _():
        for m in range(micros):
            for d in order:
                fwd_copy(m, 0, d).wait_send()


def finish(chunks, xout, base, layer_out, new_cache, out_sem, x_sem):
    part = base.shape[0] // chunks

    def store(c):
        rows = pl.ds(c * part, part)
        return pltpu.make_async_copy(base.at[rows], new_cache.at[0, rows], out_sem.at[c])

    rows_copy = pltpu.make_async_copy(xout, layer_out.at[0], x_sem.at[0])
    for c in range(chunks):
        store(c).start()
    rows_copy.start()
    for c in range(chunks):
        store(c).wait()
    rows_copy.wait()


def per_device(sizes, hidden_in, queries, cache, lengths, moves, norm_gain, kv_weight, out_weight):
    G, L, T, micros, slots, width, ctx_len = sizes
    W = width // T
    heads = W // HD
    pieces = heads + 2
    R = ROWS
    H = HALVES
    S = W // H
    kv = 2 * HD
    movers = (G - 1) * PAIR
    any_spec = pl.BlockSpec(memory_space=pl.ANY)
    vmem = pl.BlockSpec(memory_space=pltpu.VMEM)
    dma = pltpu.SemaphoreType.DMA
    xout, base = pl.pallas_call(
        functools.partial(kernel, sizes),
        out_shape=(
            pltpu.VMEM((slots, W), BF16),
            pltpu.VMEM((slots, ctx_len, kv), BF16),
        ),
        in_specs=[any_spec] * 8,
        out_specs=(vmem, vmem),
        scratch_shapes=[
            pltpu.VMEM((slots, HD), jnp.int32),
            pltpu.SMEM(lengths.shape, jnp.int32),
            pltpu.SMEM(moves.shape[::-1], jnp.int32),
            pltpu.VMEM((micros, H, T, R, S), BF16),
            pltpu.VMEM((slots, width), BF16),
            pltpu.VMEM((slots, W), BF16),
            pltpu.VMEM((slots, W), F32),
            pltpu.VMEM((slots, ctx_len, kv), BF16),
            pltpu.VMEM((1, width), F32),
            pltpu.VMEM((H, T * S, kv), BF16),
            pltpu.VMEM((H, W, T * S), BF16),
            pltpu.VMEM((heads, slots, HD), F32),
            pltpu.VMEM((heads, slots, HD), F32),
            pltpu.VMEM((heads, slots, HD), F32),
            pltpu.VMEM((slots, kv), F32),
            pltpu.VMEM((micros, H, R, S), F32),
            pltpu.VMEM((micros, H, R, S), BF16),
            pltpu.VMEM((slots, W), F32),
            pltpu.VMEM((micros, H, T - 1, R, S), BF16),
            pltpu.VMEM((micros, H, T - 1, R, S), BF16),
            pltpu.VMEM((movers, ctx_len, kv), BF16),
            pltpu.VMEM((movers, ctx_len, kv), BF16),
            pltpu.VMEM((G - 1, 16, 256), jnp.int32),
            pltpu.VMEM((G - 1, 16, 256), jnp.int32),
            pltpu.VMEM((1, 8, 256), jnp.int32),
            pltpu.SMEM((8, 256), jnp.int32),
            pltpu.SMEM((slots,), jnp.int32),
            pltpu.VMEM((slots, slots), BF16),
            pltpu.VMEM((slots, slots), BF16),
            pltpu.VMEM(((G - 1) * 32, pieces * R), BF16),
            pltpu.VMEM((pieces * slots, 256), BF16),
            pltpu.VMEM((pieces * slots, HD), F32),
            pltpu.VMEM((G - 1, 32, HD), BF16),
            pltpu.VMEM((G, 32, HD), BF16),
            dma((7,)), dma((H, T)),
            dma((micros, H, T - 1)), dma((micros, H)),
            dma((micros, H, T)), dma((micros, H)), dma((micros, H)), dma((micros, H, T - 1)),
            dma((G - 1,)), dma((G - 1,)), dma((G - 1,)), dma((G - 1,)), dma((G - 1,)), dma((G - 1,)),
            dma((1,)),
        ],
        compiler_params=pltpu.CompilerParams(
            collective_id=0, has_side_effects=True, vmem_limit_bytes=56 * 1024 * 1024),
        name="chain",
    )(lengths, moves.T, hidden_in, queries, cache, norm_gain, kv_weight, out_weight)
    chunks = 4
    return pl.pallas_call(
        functools.partial(finish, chunks),
        out_shape=(
            jax.ShapeDtypeStruct((1, slots, W), BF16),
            jax.ShapeDtypeStruct((1, slots, ctx_len, kv), BF16),
        ),
        in_specs=[vmem] * 2,
        out_specs=(any_spec, any_spec),
        scratch_shapes=[dma((chunks,)), dma((1,))],
        compiler_params=pltpu.CompilerParams(vmem_limit_bytes=16 * 1024 * 1024),
        name="finish",
    )(*(pltpu.with_memory_space_constraint(part, pltpu.VMEM) for part in (xout, base)))


def solution(mesh):
    G, L, T = mesh.shape["group"], mesh.shape["section"], mesh.shape["tensor"]

    def whole(hidden_in, queries, cache, lengths, moves, norm_gain, kv_weight, out_weight):
        slots = hidden_in.shape[0] // G
        sizes = (G, L, T, slots // ROWS, slots, hidden_in.shape[1], cache.shape[2])
        return jax.shard_map(
            functools.partial(per_device, sizes),
            mesh=mesh,
            in_specs=(
                P("group", None),
                P("section", "group", "tensor"),
                P("section", "group", None, "tensor"),
                P("group"),
                P("group", None),
                P("section", None),
                P("section", None, "tensor"),
                P("section", "tensor", None),
            ),
            out_specs=(P("section", "group", "tensor"), P("section", "group", None, "tensor")),
            check_vma=False,
        )(hidden_in, queries, cache, lengths, moves, norm_gain, kv_weight, out_weight)

    return whole
```

```python
import functools

import jax
import jax.numpy as jnp
from jax import lax
from jax.experimental import pallas as pl
from jax.experimental.pallas import tpu as pltpu
from jax.sharding import PartitionSpec as P

HD = 128
PAIR = 2
ROWS = 16
HALVES = 2
MESH = pl.DeviceIdType.MESH
F32 = jnp.float32
BF16 = jnp.bfloat16
NONE = 255
LOW = -1e30


def iota(shape, axis):
    return lax.broadcasted_iota(jnp.int32, shape, axis)


def kernel(
    sizes,
    lens_in, moves_in, hidden, query, cache, gain, kvw, outw,
    xout_ref, base_v,
    count_ref, lens_ref, moves_ref, xin, x0_v, q_v, qf_v, cache_v, gain_v, kvw_v, outw_v,
    mc_ref, sc_ref, ctx_ref, fresh_f, own_part, xnew, xnew_f, rs_send, rs_recv,
    pack, arr, info_pack, info_arr, place_v, place_s,
    perm_s, pick_ref, back_ref, sel_ref, sel2_ref, moved_ref, row_pack, row_arr,
    load_sem, outw_sem,
    rs_ss, rs_rs, ag_ss, ag_rs, hop_rs, fwd_ss, gc_ss, gc_rs, info_ss, info_rs, row_ss, row_rs,
    local_sem,
):
    G, L, T, micros, slots, width, ctx_len = sizes
    W = width // T
    H = HALVES
    S = W // H
    heads = W // HD
    pieces = heads + 2
    g = lax.axis_index("group")
    l = lax.axis_index("section")
    t = lax.axis_index("tensor")
    R = ROWS
    last = L - 1
    half = L // 2

    order = tuple(sorted(range(1, T), key=lambda d: -min(d, T - d)))

    def rs_copy(m, h, d):
        return pltpu.make_async_remote_copy(
            src_ref=rs_send.at[m, h, d - 1], dst_ref=rs_recv.at[m, h, d - 1],
            send_sem=rs_ss.at[m, h, d - 1], recv_sem=rs_rs.at[m, h],
            device_id={"tensor": lax.rem(t + d, T)}, device_id_type=MESH)

    def ag_copy(m, h, d):
        return pltpu.make_async_remote_copy(
            src_ref=xnew.at[m, h], dst_ref=xin.at[m, h, t],
            send_sem=ag_ss.at[m, h, d], recv_sem=ag_rs.at[m, h],
            device_id={"section": l + 1, "tensor": lax.rem(t + d, T)}, device_id_type=MESH)

    def hop_copy(m, h):
        return pltpu.make_async_remote_copy(
            src_ref=xnew.at[m, h], dst_ref=xin.at[m, h, t],
            send_sem=ag_ss.at[m, h, 0], recv_sem=hop_rs.at[m, h],
            device_id={"section": l + 1}, device_id_type=MESH)

    def fwd_copy(m, h, d):
        return pltpu.make_async_remote_copy(
            src_ref=xin.at[m, h, t], dst_ref=xin.at[m, h, t],
            send_sem=fwd_ss.at[m, h, d - 1], recv_sem=ag_rs.at[m, h],
            device_id={"tensor": lax.rem(t + d, T)}, device_id_type=MESH)

    def arrived(ref, sem):
        pltpu.make_async_copy(ref, ref, sem).wait()

    def to_group(src, dst, ss, rs, d):
        return pltpu.make_async_remote_copy(
            src_ref=src, dst_ref=dst, send_sem=ss.at[d - 1], recv_sem=rs.at[d - 1],
            device_id={"group": lax.rem(g + d, G)}, device_id_type=MESH)

    def gc_copy(d):
        e = PAIR * (d - 1)
        return to_group(pack.at[pl.ds(e, PAIR)], arr.at[pl.ds(e, PAIR)], gc_ss, gc_rs, d)

    def info_copy(d):
        return to_group(info_pack.at[d - 1], info_arr.at[d - 1], info_ss, info_rs, d)

    def row_copy(d):
        return to_group(row_pack.at[d - 1], row_arr.at[d - 1], row_ss, row_rs, d)

    def outw_load(h, d):
        start = pl.multiple_of(lax.rem(t + d, T) * W + h * S, S)
        place = order.index(d) if d else T - 1
        return pltpu.make_async_copy(
            outw.at[0, :, pl.ds(start, S)], outw_v.at[h, :, pl.ds(place * S, S)], outw_sem.at[h, d])

    query_load = pltpu.make_async_copy(query.at[0], q_v, load_sem.at[0])
    cache_load = pltpu.make_async_copy(cache.at[0], cache_v, load_sem.at[1])
    lens_load = pltpu.make_async_copy(lens_in, lens_ref, load_sem.at[5])
    moves_load = pltpu.make_async_copy(moves_in, moves_ref, load_sem.at[6])
    x_load = pltpu.make_async_copy(hidden, x0_v, load_sem.at[4])
    gain_load = pltpu.make_async_copy(gain, gain_v, load_sem.at[2])
    movers = moves_ref.shape[1]
    place_load = pltpu.make_async_copy(place_v.at[0], place_s, local_sem.at[0])

    lens_load.start()
    moves_load.start()
    query_load.start()
    cache_load.start()

    @pl.when(l == 0)
    def _():
        x_load.start()

    gain_load.start()
    for h in range(H):
        for q in range(T):
            pltpu.make_async_copy(
                kvw.at[0, pl.ds(q * W + h * S, S)], kvw_v.at[h, pl.ds(q * S, S)],
                load_sem.at[3]).start()

    barrier = pltpu.get_barrier_semaphore()
    for d in range(1, T):
        pl.semaphore_signal(barrier, inc=1, device_id={"tensor": lax.rem(t + d, T)}, device_id_type=MESH)
    for d in range(1, G):
        pl.semaphore_signal(barrier, inc=1, device_id={"group": lax.rem(g + d, G)}, device_id_type=MESH)

    @pl.when(l > 0)
    def _():
        for k in range(T):
            pl.semaphore_signal(
                barrier, inc=1, device_id={"section": l - 1, "tensor": k}, device_id_type=MESH)

    @pl.when((l > 0) & (l < last))
    def _():
        pl.semaphore_wait(barrier, T - 1 + G - 1 + T)

    @pl.when(l == last)
    def _():
        pl.semaphore_wait(barrier, T - 1 + G - 1)

    def arrange():
        leaving = [moves_ref[0, i] for i in range(movers)]
        ranked = list(leaving)
        for end in range(movers - 1, 0, -1):
            for i in range(end):
                low = jnp.minimum(ranked[i], ranked[i + 1])
                high = jnp.maximum(ranked[i], ranked[i + 1])
                ranked[i], ranked[i + 1] = low, high

        def staying(position):
            slot = position - movers
            for k in range(movers):
                slot = slot + (slot >= ranked[k]).astype(jnp.int32)
            return slot

        def slot_of(position):
            slot = staying(position)
            for i in range(movers):
                slot = jnp.where(position == i, leaving[i], slot)
            return slot

        def place(p, carry):
            perm_s[p] = staying(p)
            return carry

        for i in range(movers):
            perm_s[i] = leaving[i]
        lax.fori_loop(movers, slots, place, 0)
        square = (slots, slots)
        row, col = iota(square, 0), iota(square, 1)
        pick_ref[...] = jnp.where(slot_of(row) == col, 1.0, 0.0).astype(BF16)
        back_ref[...] = jnp.where((staying(col) == row) & (col >= movers), 1.0, 0.0).astype(BF16)

    block = 8
    blocks = slots // block

    def attend(first, end):
        span = block * ctx_len
        scale = HD ** -0.5

        def one(b, carry):
            rows = pl.ds(pl.multiple_of(b * block, block), block)
            lens = jnp.zeros((block, span), jnp.int32)
            row = iota((block, span), 0)
            slot = [perm_s[b * block + n] for n in range(block)]
            for n in range(block):
                lens = jnp.where(row == n, lens_ref[slot[n]], lens)
            tokens = jnp.concatenate([cache_v[slot[n]] for n in range(block)], axis=0)
            col = iota((block, span), 1)
            ok = (col // ctx_len == row) & (col % ctx_len < lens)
            bias = jnp.where(ok, 0.0, LOW).astype(F32)
            stacked = jnp.concatenate(
                [qf_v[rows, a * HD:(a + 1) * HD] for a in range(heads)], axis=0).astype(BF16)
            keys = tokens[:, 0:HD]
            values = tokens[:, HD:2 * HD]
            score = lax.dot_general(
                stacked, keys, (((1,), (1,)), ((), ())), preferred_element_type=F32)
            score = score.reshape(heads, block, span) * scale + bias[None]
            top = jnp.max(score, axis=-1, keepdims=True)
            weight = jnp.exp(score - top)
            total = jnp.sum(weight, axis=-1, keepdims=True)
            mixed = jnp.dot(
                weight.reshape(heads * block, span).astype(BF16), values,
                preferred_element_type=F32)
            ctx_ref[:, rows, :] = mixed.reshape(heads, block, HD)
            mc_ref[:, rows, :] = jnp.broadcast_to(top, (heads, block, HD))
            sc_ref[:, rows, :] = jnp.broadcast_to(total, (heads, block, HD))
            return carry

        lax.fori_loop(first, end, one, 0)

    def depart():
        lane = iota((8, 256), 1)
        sel_row = iota(sel_ref.shape, 0)
        slot_at = jnp.full(sel_ref.shape, NONE, jnp.int32)
        for d in range(1, G):
            e = d - 1
            dest = lax.rem(g + d, G)
            place_vec = jnp.zeros((8, 256), jnp.int32)
            len_vec = jnp.zeros((8, 256), jnp.int32)
            for i in range(PAIR):
                slot = jnp.int32(NONE)
                place = jnp.int32(NONE)
                from_slot = jnp.int32(0)
                for k in range(movers // PAIR):
                    hit = moves_ref[1, PAIR * k] == dest
                    slot = jnp.where(hit, PAIR * k + i, slot)
                    place = jnp.where(hit, moves_ref[2, PAIR * k + i], place)
                    from_slot = jnp.where(hit, moves_ref[0, PAIR * k + i], from_slot)
                here = lane // 16 == e * PAIR + i
                place_vec = jnp.where(here, place, place_vec)
                len_vec = jnp.where(here, lens_ref[from_slot], len_vec)
                slot_at = jnp.where(sel_row // 16 == e * PAIR + i, slot, slot_at)
                pack[PAIR * e + i] = cache_v[from_slot]
            info_pack[e, 0:8, :] = place_vec
            info_pack[e, 8:16, :] = len_vec
            info_copy(d).start()
            gc_copy(d).start()
        sel_col = iota(sel_ref.shape, 1)
        chosen = (sel_row % 16 == sel_col // R) & (slot_at == sel_col % R)
        sel_ref[...] = jnp.where(chosen, 1.0, 0.0).astype(BF16)

    def arrive():
        for d in range(1, G):
            info_copy(d).wait_recv()
        place = info_arr[0, 0:8, :]
        length = info_arr[0, 8:16, :]
        for e in range(1, G - 1):
            place = place + info_arr[e, 0:8, :]
            length = length + info_arr[e, 8:16, :]
        lane8 = iota((8, 256), 1)
        place = jnp.where(lane8 < (G - 1) * PAIR * 16, place, NONE)
        place_v[0] = place
        place_load.start()
        wide = (slots, 256)
        spot = jnp.broadcast_to(place[0:1, :], wide)
        long = jnp.broadcast_to(length[0:1, :], wide)
        lane = iota(wide, 1)
        row = iota(wide, 0)
        match = spot == row
        first = match & (lane % 16 == 0)
        has = jnp.max(jnp.where(first, 1.0, 0.0), axis=-1, keepdims=True)
        moved_len = jnp.max(jnp.where(first, long.astype(F32), 0.0), axis=-1, keepdims=True)
        own_len = jnp.zeros((slots, HD), F32)
        narrow = iota((slots, HD), 0)
        for n in range(slots):
            own_len = jnp.where(narrow == n, lens_ref[n].astype(F32), own_len)
        count_ref[...] = jnp.where(has > 0.5, moved_len, own_len).astype(jnp.int32)
        for c in range(pieces):
            sel2_ref[c * slots:(c + 1) * slots, :] = jnp.where(
                match & (lane % 16 == c), 1.0, 0.0).astype(BF16)
        for d in range(1, G):
            gc_copy(d).wait_recv()
        place_load.wait()

        def fill(j, carry):
            index = jnp.int32(-1)
            for e in range((G - 1) * PAIR):
                index = jnp.where(place_s[0, e * 16] == j, e, index)
            moved = arr[jnp.maximum(index, 0)]
            kept = cache_v[j]
            base_v[j] = lax.select_n(index >= 0, kept, moved)
            return carry

        lax.fori_loop(0, slots, fill, 0)

    def pass_on(m, h):
        arrived(xin.at[m, h, t], hop_rs.at[m, h])
        for d in order:
            fwd_copy(m, h, d).start()

    def forward(m):
        @pl.when(l == half)
        def _():
            pass_on(m, 0)

    def whole_fresh():
        acc = jnp.zeros((slots, 2 * HD), F32)
        square = jnp.zeros((slots, 1), F32)
        for h in range(H):
            scaled = []
            for q in range(T):
                cols = slice(q * W + h * S, q * W + (h + 1) * S)
                xq = x0_v[:, cols].astype(F32)
                square = square + jnp.sum(xq * xq, axis=-1, keepdims=True)
                scaled.append((xq * gain_v[:, cols]).astype(BF16))
            acc = acc + jnp.dot(
                jnp.concatenate(scaled, axis=1), kvw_v[h], preferred_element_type=F32)
        fresh = (acc * lax.rsqrt(square * (1.0 / width) + 1e-06)).astype(BF16)
        fresh_f[...] = jnp.dot(pick_ref[...], fresh, preferred_element_type=F32)
        mine = x0_v[:, pl.ds(pl.multiple_of(t * W, W), W)]
        ordered = jnp.dot(pick_ref[...], mine, preferred_element_type=F32).astype(BF16)
        for m in range(micros):
            for h in range(H):
                xin[m, h, t] = ordered[m * R:(m + 1) * R, h * S:(h + 1) * S]

    def fresh_part(m):
        rows = pl.ds(pl.multiple_of(m * R, R), R)
        acc = jnp.zeros((R, 2 * HD), F32)
        square = jnp.zeros((R, 1), F32)
        for h in range(H):

            if h:
                arrived(xin.at[m, h], ag_rs.at[m, h])
            else:

                @pl.when(l != half)
                def _():
                    arrived(xin.at[m, h], ag_rs.at[m, h])

                @pl.when(l == half)
                def _():
                    arrived(xin.at[m, h, pl.ds(0, T - 1)], ag_rs.at[m, h])

            scaled = []
            for q in range(T):
                cols = slice(q * W + h * S, q * W + (h + 1) * S)
                xq = xin[m, h, q].astype(F32)
                square = square + jnp.sum(xq * xq, axis=-1, keepdims=True)
                scaled.append((xq * gain_v[:, cols]).astype(BF16))
            acc = acc + jnp.dot(
                jnp.concatenate(scaled, axis=1), kvw_v[h], preferred_element_type=F32)
        fresh = (acc * lax.rsqrt(square * (1.0 / width) + 1e-06)).astype(BF16).astype(F32)
        fresh_f[rows, :] = fresh

    def front(m):
        rows = pl.ds(pl.multiple_of(m * R, R), R)

        @pl.when(l > 0)
        def _():
            fresh_part(m)

        fresh = fresh_f[rows, :]
        key = fresh[:, 0:HD]
        value = fresh[:, HD:2 * HD]
        parts = []
        for a in range(heads):
            qa = qf_v[rows, a * HD:(a + 1) * HD]
            own = jnp.sum(qa * key, axis=-1, keepdims=True) * (HD ** -0.5)
            old_top = mc_ref[a, rows, :]
            top = jnp.maximum(old_top, own)
            old_scale = jnp.exp(old_top - top)
            own_weight = jnp.exp(own - top)
            total = sc_ref[a, rows, :] * old_scale + own_weight
            mixed = (ctx_ref[a, rows, :] * old_scale + own_weight * value) / total
            parts.append(mixed.astype(BF16))
        return jnp.concatenate(parts, axis=1)

    def project(m, context, h):
        for i, d in enumerate(order):
            part = jnp.dot(
                context, outw_v[h, :, i * S:(i + 1) * S], preferred_element_type=F32)
            if i or h:
                rs_copy(m, h if i else h - 1, order[i - 1]).start()
            rs_send[m, h, d - 1] = part.astype(BF16)
        if h == H - 1:
            rs_copy(m, h, order[-1]).start()

    def project_own(m, context, h):
        own_part[m, h] = jnp.dot(
            context, outw_v[h, :, (T - 1) * S:T * S], preferred_element_type=F32)

    def reduce(m, h):
        total = own_part[m, h] + xin[m, h, t].astype(F32)
        arrived(rs_recv.at[m, h], rs_rs.at[m, h])
        for d in order:
            total = total + rs_recv[m, h, d - 1].astype(F32)
        rounded = total.astype(BF16)
        xnew[m, h] = rounded
        xnew_f[pl.ds(pl.multiple_of(m * R, R), R), h * S:(h + 1) * S] = rounded.astype(F32)

        @pl.when((l < last) if h else (l < last) & (l != half - 1))
        def _():
            for d in order + (0,):
                ag_copy(m, h, d).start()

        if h == 0:

            @pl.when(l == half - 1)
            def _():
                hop_copy(m, h).start()

    def exchange():
        stacked = jnp.concatenate(
            [xnew_f[0:R, c * HD:(c + 1) * HD] for c in range(heads)]
            + [fresh_f[0:R, c * HD:(c + 1) * HD] for c in range(2)], axis=0).astype(BF16)
        leaving = jnp.dot(sel_ref[...], stacked, preferred_element_type=F32).astype(BF16)
        for d in range(1, G):
            row_pack[d - 1] = leaving[(d - 1) * 32:d * 32]
            row_copy(d).start()

    def collect():
        row_arr[G - 1] = jnp.zeros((32, HD), BF16)
        for d in range(1, G):
            row_copy(d).wait_recv()
        moved_ref[...] = jnp.dot(
            sel2_ref[...], row_arr[...].reshape(G * 32, HD), preferred_element_type=F32)

    def settle():
        kept = jnp.dot(back_ref[...], fresh_f[...].astype(BF16), preferred_element_type=F32)
        token = iota((ctx_len, HD), 0)
        for k in range(2):
            cols = slice(k * HD, (k + 1) * HD)
            c = heads + k
            fresh = kept[:, cols] + moved_ref[c * slots:(c + 1) * slots, :]
            for j in range(slots):
                here = token == count_ref[j:j + 1, :]
                base_v[j, :, cols] = jnp.where(
                    here, fresh[j:j + 1, :], base_v[j, :, cols].astype(F32)).astype(BF16)

    def emit(h):
        cols = slice(h * S, (h + 1) * S)
        kept = jnp.dot(
            back_ref[...], xnew_f[:, cols].astype(BF16), preferred_element_type=F32)
        for k in range(S // HD):
            c = h * (S // HD) + k
            xout_ref[:, c * HD:(c + 1) * HD] = (
                kept[:, k * HD:(k + 1) * HD] + moved_ref[c * slots:(c + 1) * slots, :]).astype(BF16)

    def rs_sent(m):
        for h in range(H):
            for d in order:
                rs_copy(m, h, d).wait_send()

    def sent():
        for m in range(micros - 1):
            rs_sent(m)
        for d in range(1, G):
            info_copy(d).wait_send()
            gc_copy(d).wait_send()
            row_copy(d).wait_send()

    lens_load.wait()
    moves_load.wait()
    arrange()
    for h in range(H):
        for d in order:
            outw_load(h, d).start()
    query_load.wait()
    cache_load.wait()
    qf_v[...] = jnp.dot(pick_ref[...], q_v[...], preferred_element_type=F32)
    first = R // block
    attend(0, first)
    for h in range(H):
        outw_load(h, 0).start()

    @pl.when(l > 0)
    def _():
        attend(first, blocks)
        depart()

    @pl.when(l == 0)
    def _():
        x_load.wait()
        gain_load.wait()
        arrived(kvw_v, load_sem.at[3])
        whole_fresh()

    @pl.when(l >= 3)
    def _():
        arrive()

    @pl.when(l > 0)
    def _():
        gain_load.wait()
        arrived(kvw_v, load_sem.at[3])

    forward(0)

    def batch(m, carry):
        context = front(m)

        @pl.when((l == 0) & (m == 0))
        def _():
            pl.semaphore_wait(barrier, T - 1 + G - 1 + T)

        @pl.when(m == 0)
        def _():
            for h in range(H):
                for d in order + (0,):
                    outw_load(h, d).wait()

        for h in range(H):
            project(m, context, h)

        @pl.when(m + 1 < micros)
        def _():
            forward(m + 1)

        for h in range(H):
            project_own(m, context, h)

        @pl.when((l == 0) & (m == 0))
        def _():
            attend(first, blocks)

        @pl.when((l == last) & (m == micros - 1))
        def _():
            collect()
            settle()
            sent()

        for h in range(H):
            reduce(m, h)
            if h < H - 1:

                @pl.when((l == last) & (m == micros - 1))
                def _():
                    emit(h)

        @pl.when((l == last) & (m == 0))
        def _():
            exchange()

        return carry

    lax.fori_loop(0, micros, batch, 0)

    @pl.when(l == 0)
    def _():
        depart()

    @pl.when(l < 3)
    def _():
        arrive()

    @pl.when(l < last)
    def _():
        exchange()
        collect()
        settle()

    @pl.when(l < last)
    def _():
        for h in range(H - 1):
            emit(h)

    emit(H - 1)

    @pl.when(l < last)
    def _():
        sent()

    rs_sent(micros - 1)

    @pl.when((l < last) & (l != half - 1))
    def _():
        for m in range(micros):
            for d in range(T):
                ag_copy(m, 0, d).wait_send()

    @pl.when(l < last)
    def _():
        for m in range(micros):
            for h in range(1, H):
                for d in range(T):
                    ag_copy(m, h, d).wait_send()

    @pl.when(l == half - 1)
    def _():
        for m in range(micros):
            hop_copy(m, 0).wait_send()

    @pl.when(l == half)
    def _():
        for m in range(micros):
            for d in order:
                fwd_copy(m, 0, d).wait_send()


def finish(chunks, xout, base, layer_out, new_cache, out_sem, x_sem):
    part = base.shape[0] // chunks

    def store(c):
        rows = pl.ds(c * part, part)
        return pltpu.make_async_copy(base.at[rows], new_cache.at[0, rows], out_sem.at[c])

    rows_copy = pltpu.make_async_copy(xout, layer_out.at[0], x_sem.at[0])
    for c in range(chunks):
        store(c).start()
    rows_copy.start()
    for c in range(chunks):
        store(c).wait()
    rows_copy.wait()


def per_device(sizes, hidden_in, queries, cache, lengths, moves, norm_gain, kv_weight, out_weight):
    G, L, T, micros, slots, width, ctx_len = sizes
    W = width // T
    heads = W // HD
    pieces = heads + 2
    R = ROWS
    H = HALVES
    S = W // H
    kv = 2 * HD
    movers = (G - 1) * PAIR
    any_spec = pl.BlockSpec(memory_space=pl.ANY)
    vmem = pl.BlockSpec(memory_space=pltpu.VMEM)
    dma = pltpu.SemaphoreType.DMA
    xout, base = pl.pallas_call(
        functools.partial(kernel, sizes),
        out_shape=(
            pltpu.VMEM((slots, W), BF16),
            pltpu.VMEM((slots, ctx_len, kv), BF16),
        ),
        in_specs=[any_spec] * 8,
        out_specs=(vmem, vmem),
        scratch_shapes=[
            pltpu.VMEM((slots, HD), jnp.int32),
            pltpu.SMEM(lengths.shape, jnp.int32),
            pltpu.SMEM(moves.shape[::-1], jnp.int32),
            pltpu.VMEM((micros, H, T, R, S), BF16),
            pltpu.VMEM((slots, width), BF16),
            pltpu.VMEM((slots, W), BF16),
            pltpu.VMEM((slots, W), F32),
            pltpu.VMEM((slots, ctx_len, kv), BF16),
            pltpu.VMEM((1, width), F32),
            pltpu.VMEM((H, T * S, kv), BF16),
            pltpu.VMEM((H, W, T * S), BF16),
            pltpu.VMEM((heads, slots, HD), F32),
            pltpu.VMEM((heads, slots, HD), F32),
            pltpu.VMEM((heads, slots, HD), F32),
            pltpu.VMEM((slots, kv), F32),
            pltpu.VMEM((micros, H, R, S), F32),
            pltpu.VMEM((micros, H, R, S), BF16),
            pltpu.VMEM((slots, W), F32),
            pltpu.VMEM((micros, H, T - 1, R, S), BF16),
            pltpu.VMEM((micros, H, T - 1, R, S), BF16),
            pltpu.VMEM((movers, ctx_len, kv), BF16),
            pltpu.VMEM((movers, ctx_len, kv), BF16),
            pltpu.VMEM((G - 1, 16, 256), jnp.int32),
            pltpu.VMEM((G - 1, 16, 256), jnp.int32),
            pltpu.VMEM((1, 8, 256), jnp.int32),
            pltpu.SMEM((8, 256), jnp.int32),
            pltpu.SMEM((slots,), jnp.int32),
            pltpu.VMEM((slots, slots), BF16),
            pltpu.VMEM((slots, slots), BF16),
            pltpu.VMEM(((G - 1) * 32, pieces * R), BF16),
            pltpu.VMEM((pieces * slots, 256), BF16),
            pltpu.VMEM((pieces * slots, HD), F32),
            pltpu.VMEM((G - 1, 32, HD), BF16),
            pltpu.VMEM((G, 32, HD), BF16),
            dma((7,)), dma((H, T)),
            dma((micros, H, T - 1)), dma((micros, H)),
            dma((micros, H, T)), dma((micros, H)), dma((micros, H)), dma((micros, H, T - 1)),
            dma((G - 1,)), dma((G - 1,)), dma((G - 1,)), dma((G - 1,)), dma((G - 1,)), dma((G - 1,)),
            dma((1,)),
        ],
        compiler_params=pltpu.CompilerParams(
            collective_id=0, has_side_effects=True, vmem_limit_bytes=56 * 1024 * 1024),
        name="chain",
    )(lengths, moves.T, hidden_in, queries, cache, norm_gain, kv_weight, out_weight)
    chunks = 4
    return pl.pallas_call(
        functools.partial(finish, chunks),
        out_shape=(
            jax.ShapeDtypeStruct((1, slots, W), BF16),
            jax.ShapeDtypeStruct((1, slots, ctx_len, kv), BF16),
        ),
        in_specs=[vmem] * 2,
        out_specs=(any_spec, any_spec),
        scratch_shapes=[dma((chunks,)), dma((1,))],
        compiler_params=pltpu.CompilerParams(vmem_limit_bytes=16 * 1024 * 1024),
        name="finish",
    )(*(pltpu.with_memory_space_constraint(part, pltpu.VMEM) for part in (xout, base)))


def solution(mesh):
    G, L, T = mesh.shape["group"], mesh.shape["section"], mesh.shape["tensor"]

    def whole(hidden_in, queries, cache, lengths, moves, norm_gain, kv_weight, out_weight):
        slots = hidden_in.shape[0] // G
        sizes = (G, L, T, slots // ROWS, slots, hidden_in.shape[1], cache.shape[2])
        return jax.shard_map(
            functools.partial(per_device, sizes),
            mesh=mesh,
            in_specs=(
                P("group", None),
                P("section", "group", "tensor"),
                P("section", "group", None, "tensor"),
                P("group"),
                P("group", None),
                P("section", None),
                P("section", None, "tensor"),
                P("section", "tensor", None),
            ),
            out_specs=(P("section", "group", "tensor"), P("section", "group", None, "tensor")),
            check_vma=False,
        )(hidden_in, queries, cache, lengths, moves, norm_gain, kv_weight, out_weight)

    return whole
```

```python
import functools

import jax
import jax.numpy as jnp
from jax import lax
from jax.experimental import pallas as pl
from jax.experimental.pallas import tpu as pltpu
from jax.sharding import PartitionSpec as P

HD = 128
PAIR = 2
ROWS = 16
HALVES = 2
MESH = pl.DeviceIdType.MESH
F32 = jnp.float32
BF16 = jnp.bfloat16
NONE = 255
LOW = -1e30


def iota(shape, axis):
    return lax.broadcasted_iota(jnp.int32, shape, axis)


def kernel(
    sizes,
    lens_in, moves_in, hidden, query, cache, gain, kvw, outw,
    xout_ref, base_v,
    count_ref, lens_ref, moves_ref, xin, x0_v, q_v, qf_v, cache_v, gain_v, kvw_v, outw_v,
    mc_ref, sc_ref, ctx_ref, fresh_f, own_part, xnew, xnew_f, rs_send, rs_recv,
    pack, arr, info_pack, info_arr, place_v, place_s,
    perm_s, pick_ref, back_ref, sel_ref, sel2_ref, moved_ref, row_pack, row_arr,
    load_sem, outw_sem,
    rs_ss, rs_rs, ag_ss, ag_rs, hop_rs, fwd_ss, gc_ss, gc_rs, info_ss, info_rs, row_ss, row_rs,
    local_sem,
):
    G, L, T, micros, slots, width, ctx_len = sizes
    W = width // T
    H = HALVES
    S = W // H
    heads = W // HD
    pieces = heads + 2
    g = lax.axis_index("group")
    l = lax.axis_index("section")
    t = lax.axis_index("tensor")
    R = ROWS
    last = L - 1
    half = L // 2

    order = tuple(sorted(range(1, T), key=lambda d: -min(d, T - d)))

    def rs_copy(m, h, d):
        return pltpu.make_async_remote_copy(
            src_ref=rs_send.at[m, h, d - 1], dst_ref=rs_recv.at[m, h, d - 1],
            send_sem=rs_ss.at[m, h, d - 1], recv_sem=rs_rs.at[m, h],
            device_id={"tensor": lax.rem(t + d, T)}, device_id_type=MESH)

    def ag_copy(m, h, d):
        return pltpu.make_async_remote_copy(
            src_ref=xnew.at[m, h], dst_ref=xin.at[m, h, t],
            send_sem=ag_ss.at[m, h, d], recv_sem=ag_rs.at[m, h],
            device_id={"section": l + 1, "tensor": lax.rem(t + d, T)}, device_id_type=MESH)

    def hop_copy(m, h):
        return pltpu.make_async_remote_copy(
            src_ref=xnew.at[m, h], dst_ref=xin.at[m, h, t],
            send_sem=ag_ss.at[m, h, 0], recv_sem=hop_rs.at[m, h],
            device_id={"section": l + 1}, device_id_type=MESH)

    def fwd_copy(m, h, d):
        return pltpu.make_async_remote_copy(
            src_ref=xin.at[m, h, t], dst_ref=xin.at[m, h, t],
            send_sem=fwd_ss.at[m, h, d - 1], recv_sem=ag_rs.at[m, h],
            device_id={"tensor": lax.rem(t + d, T)}, device_id_type=MESH)

    def arrived(ref, sem):
        pltpu.make_async_copy(ref, ref, sem).wait()

    def to_group(src, dst, ss, rs, d):
        return pltpu.make_async_remote_copy(
            src_ref=src, dst_ref=dst, send_sem=ss.at[d - 1], recv_sem=rs.at[d - 1],
            device_id={"group": lax.rem(g + d, G)}, device_id_type=MESH)

    def gc_copy(d):
        e = PAIR * (d - 1)
        return to_group(pack.at[pl.ds(e, PAIR)], arr.at[pl.ds(e, PAIR)], gc_ss, gc_rs, d)

    def info_copy(d):
        return to_group(info_pack.at[d - 1], info_arr.at[d - 1], info_ss, info_rs, d)

    def row_copy(d):
        return to_group(row_pack.at[d - 1], row_arr.at[d - 1], row_ss, row_rs, d)

    def outw_load(h, d):
        start = pl.multiple_of(lax.rem(t + d, T) * W + h * S, S)
        place = order.index(d) if d else T - 1
        return pltpu.make_async_copy(
            outw.at[0, :, pl.ds(start, S)], outw_v.at[h, :, pl.ds(place * S, S)], outw_sem.at[h, d])

    query_load = pltpu.make_async_copy(query.at[0], q_v, load_sem.at[0])
    cache_load = pltpu.make_async_copy(cache.at[0], cache_v, load_sem.at[1])
    lens_load = pltpu.make_async_copy(lens_in, lens_ref, load_sem.at[5])
    moves_load = pltpu.make_async_copy(moves_in, moves_ref, load_sem.at[6])
    x_load = pltpu.make_async_copy(hidden, x0_v, load_sem.at[4])
    gain_load = pltpu.make_async_copy(gain, gain_v, load_sem.at[2])
    movers = moves_ref.shape[1]
    place_load = pltpu.make_async_copy(place_v.at[0], place_s, local_sem.at[0])

    lens_load.start()
    moves_load.start()
    query_load.start()
    cache_load.start()

    @pl.when(l == 0)
    def _():
        x_load.start()

    gain_load.start()
    for h in range(H):
        for q in range(T):
            pltpu.make_async_copy(
                kvw.at[0, pl.ds(q * W + h * S, S)], kvw_v.at[h, pl.ds(q * S, S)],
                load_sem.at[3]).start()

    barrier = pltpu.get_barrier_semaphore()
    for d in range(1, T):
        pl.semaphore_signal(barrier, inc=1, device_id={"tensor": lax.rem(t + d, T)}, device_id_type=MESH)
    for d in range(1, G):
        pl.semaphore_signal(barrier, inc=1, device_id={"group": lax.rem(g + d, G)}, device_id_type=MESH)

    @pl.when(l > 0)
    def _():
        for k in range(T):
            pl.semaphore_signal(
                barrier, inc=1, device_id={"section": l - 1, "tensor": k}, device_id_type=MESH)

    @pl.when((l > 0) & (l < last))
    def _():
        pl.semaphore_wait(barrier, T - 1 + G - 1 + T)

    @pl.when(l == last)
    def _():
        pl.semaphore_wait(barrier, T - 1 + G - 1)

    def arrange():
        leaving = [moves_ref[0, i] for i in range(movers)]
        ranked = list(leaving)
        for end in range(movers - 1, 0, -1):
            for i in range(end):
                low = jnp.minimum(ranked[i], ranked[i + 1])
                high = jnp.maximum(ranked[i], ranked[i + 1])
                ranked[i], ranked[i + 1] = low, high

        def staying(position):
            slot = position - movers
            for k in range(movers):
                slot = slot + (slot >= ranked[k]).astype(jnp.int32)
            return slot

        def slot_of(position):
            slot = staying(position)
            for i in range(movers):
                slot = jnp.where(position == i, leaving[i], slot)
            return slot

        def place(p, carry):
            perm_s[p] = staying(p)
            return carry

        for i in range(movers):
            perm_s[i] = leaving[i]
        lax.fori_loop(movers, slots, place, 0)
        square = (slots, slots)
        row, col = iota(square, 0), iota(square, 1)
        pick_ref[...] = jnp.where(slot_of(row) == col, 1.0, 0.0).astype(BF16)
        back_ref[...] = jnp.where((staying(col) == row) & (col >= movers), 1.0, 0.0).astype(BF16)

    block = 8
    blocks = slots // block

    def attend(first, end):
        span = block * ctx_len
        scale = HD ** -0.5

        def one(b, carry):
            rows = pl.ds(pl.multiple_of(b * block, block), block)
            lens = jnp.zeros((block, span), jnp.int32)
            row = iota((block, span), 0)
            slot = [perm_s[b * block + n] for n in range(block)]
            for n in range(block):
                lens = jnp.where(row == n, lens_ref[slot[n]], lens)
            tokens = jnp.concatenate([cache_v[slot[n]] for n in range(block)], axis=0)
            col = iota((block, span), 1)
            ok = (col // ctx_len == row) & (col % ctx_len < lens)
            bias = jnp.where(ok, 0.0, LOW).astype(F32)
            stacked = jnp.concatenate(
                [qf_v[rows, a * HD:(a + 1) * HD] for a in range(heads)], axis=0).astype(BF16)
            keys = tokens[:, 0:HD]
            values = tokens[:, HD:2 * HD]
            score = lax.dot_general(
                stacked, keys, (((1,), (1,)), ((), ())), preferred_element_type=F32)
            score = score.reshape(heads, block, span) * scale + bias[None]
            top = jnp.max(score, axis=-1, keepdims=True)
            weight = jnp.exp(score - top)
            total = jnp.sum(weight, axis=-1, keepdims=True)
            mixed = jnp.dot(
                weight.reshape(heads * block, span).astype(BF16), values,
                preferred_element_type=F32)
            ctx_ref[:, rows, :] = mixed.reshape(heads, block, HD)
            mc_ref[:, rows, :] = jnp.broadcast_to(top, (heads, block, HD))
            sc_ref[:, rows, :] = jnp.broadcast_to(total, (heads, block, HD))
            return carry

        lax.fori_loop(first, end, one, 0)

    def depart():
        lane = iota((8, 256), 1)
        sel_row = iota(sel_ref.shape, 0)
        slot_at = jnp.full(sel_ref.shape, NONE, jnp.int32)
        for d in range(1, G):
            e = d - 1
            dest = lax.rem(g + d, G)
            place_vec = jnp.zeros((8, 256), jnp.int32)
            len_vec = jnp.zeros((8, 256), jnp.int32)
            for i in range(PAIR):
                slot = jnp.int32(NONE)
                place = jnp.int32(NONE)
                from_slot = jnp.int32(0)
                for k in range(movers // PAIR):
                    hit = moves_ref[1, PAIR * k] == dest
                    slot = jnp.where(hit, PAIR * k + i, slot)
                    place = jnp.where(hit, moves_ref[2, PAIR * k + i], place)
                    from_slot = jnp.where(hit, moves_ref[0, PAIR * k + i], from_slot)
                here = lane // 16 == e * PAIR + i
                place_vec = jnp.where(here, place, place_vec)
                len_vec = jnp.where(here, lens_ref[from_slot], len_vec)
                slot_at = jnp.where(sel_row // 16 == e * PAIR + i, slot, slot_at)
                pack[PAIR * e + i] = cache_v[from_slot]
            info_pack[e, 0:8, :] = place_vec
            info_pack[e, 8:16, :] = len_vec
            info_copy(d).start()
            gc_copy(d).start()
        sel_col = iota(sel_ref.shape, 1)
        chosen = (sel_row % 16 == sel_col // R) & (slot_at == sel_col % R)
        sel_ref[...] = jnp.where(chosen, 1.0, 0.0).astype(BF16)

    def arrive():
        for d in range(1, G):
            info_copy(d).wait_recv()
        place = info_arr[0, 0:8, :]
        length = info_arr[0, 8:16, :]
        for e in range(1, G - 1):
            place = place + info_arr[e, 0:8, :]
            length = length + info_arr[e, 8:16, :]
        lane8 = iota((8, 256), 1)
        place = jnp.where(lane8 < (G - 1) * PAIR * 16, place, NONE)
        place_v[0] = place
        place_load.start()
        wide = (slots, 256)
        spot = jnp.broadcast_to(place[0:1, :], wide)
        long = jnp.broadcast_to(length[0:1, :], wide)
        lane = iota(wide, 1)
        row = iota(wide, 0)
        match = spot == row
        first = match & (lane % 16 == 0)
        has = jnp.max(jnp.where(first, 1.0, 0.0), axis=-1, keepdims=True)
        moved_len = jnp.max(jnp.where(first, long.astype(F32), 0.0), axis=-1, keepdims=True)
        own_len = jnp.zeros((slots, HD), F32)
        narrow = iota((slots, HD), 0)
        for n in range(slots):
            own_len = jnp.where(narrow == n, lens_ref[n].astype(F32), own_len)
        count_ref[...] = jnp.where(has > 0.5, moved_len, own_len).astype(jnp.int32)
        for c in range(pieces):
            sel2_ref[c * slots:(c + 1) * slots, :] = jnp.where(
                match & (lane % 16 == c), 1.0, 0.0).astype(BF16)
        for d in range(1, G):
            gc_copy(d).wait_recv()
        place_load.wait()

        def fill(j, carry):
            index = jnp.int32(-1)
            for e in range((G - 1) * PAIR):
                index = jnp.where(place_s[0, e * 16] == j, e, index)
            moved = arr[jnp.maximum(index, 0)]
            kept = cache_v[j]
            base_v[j] = lax.select_n(index >= 0, kept, moved)
            return carry

        lax.fori_loop(0, slots, fill, 0)

    def pass_on(m, h):
        arrived(xin.at[m, h, t], hop_rs.at[m, h])
        for d in order:
            fwd_copy(m, h, d).start()

    def forward(m):
        @pl.when(l == half)
        def _():
            pass_on(m, 0)

    def whole_fresh():
        acc = jnp.zeros((slots, 2 * HD), F32)
        square = jnp.zeros((slots, 1), F32)
        for h in range(H):
            scaled = []
            for q in range(T):
                cols = slice(q * W + h * S, q * W + (h + 1) * S)
                xq = x0_v[:, cols].astype(F32)
                square = square + jnp.sum(xq * xq, axis=-1, keepdims=True)
                scaled.append((xq * gain_v[:, cols]).astype(BF16))
            acc = acc + jnp.dot(
                jnp.concatenate(scaled, axis=1), kvw_v[h], preferred_element_type=F32)
        fresh = (acc * lax.rsqrt(square * (1.0 / width) + 1e-06)).astype(BF16)
        fresh_f[...] = jnp.dot(pick_ref[...], fresh, preferred_element_type=F32)
        mine = x0_v[:, pl.ds(pl.multiple_of(t * W, W), W)]
        ordered = jnp.dot(pick_ref[...], mine, preferred_element_type=F32).astype(BF16)
        for m in range(micros):
            for h in range(H):
                xin[m, h, t] = ordered[m * R:(m + 1) * R, h * S:(h + 1) * S]

    def fresh_part(m):
        rows = pl.ds(pl.multiple_of(m * R, R), R)
        acc = jnp.zeros((R, 2 * HD), F32)
        square = jnp.zeros((R, 1), F32)
        for h in range(H):

            if h:
                arrived(xin.at[m, h], ag_rs.at[m, h])
            else:

                @pl.when(l != half)
                def _():
                    arrived(xin.at[m, h], ag_rs.at[m, h])

                @pl.when(l == half)
                def _():
                    arrived(xin.at[m, h, pl.ds(0, T - 1)], ag_rs.at[m, h])

            scaled = []
            for q in range(T):
                cols = slice(q * W + h * S, q * W + (h + 1) * S)
                xq = xin[m, h, q].astype(F32)
                square = square + jnp.sum(xq * xq, axis=-1, keepdims=True)
                scaled.append((xq * gain_v[:, cols]).astype(BF16))
            acc = acc + jnp.dot(
                jnp.concatenate(scaled, axis=1), kvw_v[h], preferred_element_type=F32)
        fresh = (acc * lax.rsqrt(square * (1.0 / width) + 1e-06)).astype(BF16).astype(F32)
        fresh_f[rows, :] = fresh

    def front(m):
        rows = pl.ds(pl.multiple_of(m * R, R), R)

        @pl.when(l > 0)
        def _():
            fresh_part(m)

        fresh = fresh_f[rows, :]
        key = fresh[:, 0:HD]
        value = fresh[:, HD:2 * HD]
        parts = []
        for a in range(heads):
            qa = qf_v[rows, a * HD:(a + 1) * HD]
            own = jnp.sum(qa * key, axis=-1, keepdims=True) * (HD ** -0.5)
            old_top = mc_ref[a, rows, :]
            top = jnp.maximum(old_top, own)
            old_scale = jnp.exp(old_top - top)
            own_weight = jnp.exp(own - top)
            total = sc_ref[a, rows, :] * old_scale + own_weight
            mixed = (ctx_ref[a, rows, :] * old_scale + own_weight * value) / total
            parts.append(mixed.astype(BF16))
        return jnp.concatenate(parts, axis=1)

    def project(m, context, h):
        for i, d in enumerate(order):
            part = jnp.dot(
                context, outw_v[h, :, i * S:(i + 1) * S], preferred_element_type=F32)
            rs_send[m, h, d - 1] = part.astype(BF16)
            rs_copy(m, h, d).start()

    def project_own(m, context, h):
        own_part[m, h] = jnp.dot(
            context, outw_v[h, :, (T - 1) * S:T * S], preferred_element_type=F32)

    def reduce(m, h):
        total = own_part[m, h] + xin[m, h, t].astype(F32)
        arrived(rs_recv.at[m, h], rs_rs.at[m, h])
        for d in order:
            total = total + rs_recv[m, h, d - 1].astype(F32)
        rounded = total.astype(BF16)
        xnew[m, h] = rounded
        xnew_f[pl.ds(pl.multiple_of(m * R, R), R), h * S:(h + 1) * S] = rounded.astype(F32)

        @pl.when((l < last) if h else (l < last) & (l != half - 1))
        def _():
            for d in order + (0,):
                ag_copy(m, h, d).start()

        if h == 0:

            @pl.when(l == half - 1)
            def _():
                hop_copy(m, h).start()

    def exchange():
        stacked = jnp.concatenate(
            [xnew_f[0:R, c * HD:(c + 1) * HD] for c in range(heads)]
            + [fresh_f[0:R, c * HD:(c + 1) * HD] for c in range(2)], axis=0).astype(BF16)
        leaving = jnp.dot(sel_ref[...], stacked, preferred_element_type=F32).astype(BF16)
        for d in range(1, G):
            row_pack[d - 1] = leaving[(d - 1) * 32:d * 32]
            row_copy(d).start()

    def collect():
        row_arr[G - 1] = jnp.zeros((32, HD), BF16)
        for d in range(1, G):
            row_copy(d).wait_recv()
        moved_ref[...] = jnp.dot(
            sel2_ref[...], row_arr[...].reshape(G * 32, HD), preferred_element_type=F32)

    def settle():
        kept = jnp.dot(back_ref[...], fresh_f[...].astype(BF16), preferred_element_type=F32)
        token = iota((ctx_len, HD), 0)
        for k in range(2):
            cols = slice(k * HD, (k + 1) * HD)
            c = heads + k
            fresh = kept[:, cols] + moved_ref[c * slots:(c + 1) * slots, :]
            for j in range(slots):
                here = token == count_ref[j:j + 1, :]
                base_v[j, :, cols] = jnp.where(
                    here, fresh[j:j + 1, :], base_v[j, :, cols].astype(F32)).astype(BF16)

    def emit(h):
        cols = slice(h * S, (h + 1) * S)
        kept = jnp.dot(
            back_ref[...], xnew_f[:, cols].astype(BF16), preferred_element_type=F32)
        for k in range(S // HD):
            c = h * (S // HD) + k
            xout_ref[:, c * HD:(c + 1) * HD] = (
                kept[:, k * HD:(k + 1) * HD] + moved_ref[c * slots:(c + 1) * slots, :]).astype(BF16)

    def rs_sent(m):
        for h in range(H):
            for d in order:
                rs_copy(m, h, d).wait_send()

    def sent():
        for m in range(micros - 1):
            rs_sent(m)
        for d in range(1, G):
            info_copy(d).wait_send()
            gc_copy(d).wait_send()
            row_copy(d).wait_send()

    lens_load.wait()
    moves_load.wait()
    arrange()
    for h in range(H):
        for d in order:
            outw_load(h, d).start()
    query_load.wait()
    cache_load.wait()
    qf_v[...] = jnp.dot(pick_ref[...], q_v[...], preferred_element_type=F32)
    first = R // block
    attend(0, first)
    for h in range(H):
        outw_load(h, 0).start()

    @pl.when(l > 0)
    def _():
        attend(first, blocks)
        depart()

    @pl.when(l == 0)
    def _():
        x_load.wait()
        gain_load.wait()
        arrived(kvw_v, load_sem.at[3])
        whole_fresh()

    @pl.when(l >= 3)
    def _():
        arrive()

    @pl.when(l > 0)
    def _():
        gain_load.wait()
        arrived(kvw_v, load_sem.at[3])

    forward(0)

    def batch(m, carry):
        context = front(m)

        @pl.when((l == 0) & (m == 0))
        def _():
            pl.semaphore_wait(barrier, T - 1 + G - 1 + T)

        @pl.when(m == 0)
        def _():
            for h in range(H):
                for d in order + (0,):
                    outw_load(h, d).wait()

        for h in range(H):
            project(m, context, h)

        @pl.when(m + 1 < micros)
        def _():
            forward(m + 1)

        for h in range(H):
            project_own(m, context, h)

        @pl.when((l == 0) & (m == 0))
        def _():
            attend(first, blocks)

        @pl.when((l == last) & (m == micros - 1))
        def _():
            collect()
            settle()
            sent()

        for h in range(H):
            reduce(m, h)
            if h < H - 1:

                @pl.when((l == last) & (m == micros - 1))
                def _():
                    emit(h)

        @pl.when((l == last) & (m == 0))
        def _():
            exchange()

        return carry

    lax.fori_loop(0, micros, batch, 0)

    @pl.when(l == 0)
    def _():
        depart()

    @pl.when(l < 3)
    def _():
        arrive()

    @pl.when(l < last)
    def _():
        exchange()
        collect()
        settle()

    @pl.when(l < last)
    def _():
        for h in range(H - 1):
            emit(h)

    emit(H - 1)

    @pl.when(l < last)
    def _():
        sent()

    rs_sent(micros - 1)

    @pl.when((l < last) & (l != half - 1))
    def _():
        for m in range(micros):
            for d in range(T):
                ag_copy(m, 0, d).wait_send()

    @pl.when(l < last)
    def _():
        for m in range(micros):
            for h in range(1, H):
                for d in range(T):
                    ag_copy(m, h, d).wait_send()

    @pl.when(l == half - 1)
    def _():
        for m in range(micros):
            hop_copy(m, 0).wait_send()

    @pl.when(l == half)
    def _():
        for m in range(micros):
            for d in order:
                fwd_copy(m, 0, d).wait_send()


def finish(chunks, xout, base, layer_out, new_cache, out_sem, x_sem):
    part = base.shape[0] // chunks

    def store(c):
        rows = pl.ds(c * part, part)
        return pltpu.make_async_copy(base.at[rows], new_cache.at[0, rows], out_sem.at[c])

    rows_copy = pltpu.make_async_copy(xout, layer_out.at[0], x_sem.at[0])
    for c in range(chunks):
        store(c).start()
    rows_copy.start()
    for c in range(chunks):
        store(c).wait()
    rows_copy.wait()


def per_device(sizes, hidden_in, queries, cache, lengths, moves, norm_gain, kv_weight, out_weight):
    G, L, T, micros, slots, width, ctx_len = sizes
    W = width // T
    heads = W // HD
    pieces = heads + 2
    R = ROWS
    H = HALVES
    S = W // H
    kv = 2 * HD
    movers = (G - 1) * PAIR
    any_spec = pl.BlockSpec(memory_space=pl.ANY)
    vmem = pl.BlockSpec(memory_space=pltpu.VMEM)
    dma = pltpu.SemaphoreType.DMA
    xout, base = pl.pallas_call(
        functools.partial(kernel, sizes),
        out_shape=(
            pltpu.VMEM((slots, W), BF16),
            pltpu.VMEM((slots, ctx_len, kv), BF16),
        ),
        in_specs=[any_spec] * 8,
        out_specs=(vmem, vmem),
        scratch_shapes=[
            pltpu.VMEM((slots, HD), jnp.int32),
            pltpu.SMEM(lengths.shape, jnp.int32),
            pltpu.SMEM(moves.shape[::-1], jnp.int32),
            pltpu.VMEM((micros, H, T, R, S), BF16),
            pltpu.VMEM((slots, width), BF16),
            pltpu.VMEM((slots, W), BF16),
            pltpu.VMEM((slots, W), F32),
            pltpu.VMEM((slots, ctx_len, kv), BF16),
            pltpu.VMEM((1, width), F32),
            pltpu.VMEM((H, T * S, kv), BF16),
            pltpu.VMEM((H, W, T * S), BF16),
            pltpu.VMEM((heads, slots, HD), F32),
            pltpu.VMEM((heads, slots, HD), F32),
            pltpu.VMEM((heads, slots, HD), F32),
            pltpu.VMEM((slots, kv), F32),
            pltpu.VMEM((micros, H, R, S), F32),
            pltpu.VMEM((micros, H, R, S), BF16),
            pltpu.VMEM((slots, W), F32),
            pltpu.VMEM((micros, H, T - 1, R, S), BF16),
            pltpu.VMEM((micros, H, T - 1, R, S), BF16),
            pltpu.VMEM((movers, ctx_len, kv), BF16),
            pltpu.VMEM((movers, ctx_len, kv), BF16),
            pltpu.VMEM((G - 1, 16, 256), jnp.int32),
            pltpu.VMEM((G - 1, 16, 256), jnp.int32),
            pltpu.VMEM((1, 8, 256), jnp.int32),
            pltpu.SMEM((8, 256), jnp.int32),
            pltpu.SMEM((slots,), jnp.int32),
            pltpu.VMEM((slots, slots), BF16),
            pltpu.VMEM((slots, slots), BF16),
            pltpu.VMEM(((G - 1) * 32, pieces * R), BF16),
            pltpu.VMEM((pieces * slots, 256), BF16),
            pltpu.VMEM((pieces * slots, HD), F32),
            pltpu.VMEM((G - 1, 32, HD), BF16),
            pltpu.VMEM((G, 32, HD), BF16),
            dma((7,)), dma((H, T)),
            dma((micros, H, T - 1)), dma((micros, H)),
            dma((micros, H, T)), dma((micros, H)), dma((micros, H)), dma((micros, H, T - 1)),
            dma((G - 1,)), dma((G - 1,)), dma((G - 1,)), dma((G - 1,)), dma((G - 1,)), dma((G - 1,)),
            dma((1,)),
        ],
        compiler_params=pltpu.CompilerParams(
            collective_id=0, has_side_effects=True, vmem_limit_bytes=56 * 1024 * 1024),
        name="chain",
    )(lengths, moves.T, hidden_in, queries, cache, norm_gain, kv_weight, out_weight)
    chunks = 4
    return pl.pallas_call(
        functools.partial(finish, chunks),
        out_shape=(
            jax.ShapeDtypeStruct((1, slots, W), BF16),
            jax.ShapeDtypeStruct((1, slots, ctx_len, kv), BF16),
        ),
        in_specs=[vmem] * 2,
        out_specs=(any_spec, any_spec),
        scratch_shapes=[dma((chunks,)), dma((1,))],
        compiler_params=pltpu.CompilerParams(vmem_limit_bytes=16 * 1024 * 1024),
        name="finish",
    )(*(pltpu.with_memory_space_constraint(part, pltpu.VMEM) for part in (xout, base)))


def solution(mesh):
    G, L, T = mesh.shape["group"], mesh.shape["section"], mesh.shape["tensor"]

    def whole(hidden_in, queries, cache, lengths, moves, norm_gain, kv_weight, out_weight):
        slots = hidden_in.shape[0] // G
        sizes = (G, L, T, slots // ROWS, slots, hidden_in.shape[1], cache.shape[2])
        return jax.shard_map(
            functools.partial(per_device, sizes),
            mesh=mesh,
            in_specs=(
                P("group", None),
                P("section", "group", "tensor"),
                P("section", "group", None, "tensor"),
                P("group"),
                P("group", None),
                P("section", None),
                P("section", None, "tensor"),
                P("section", "tensor", None),
            ),
            out_specs=(P("section", "group", "tensor"), P("section", "group", None, "tensor")),
            check_vma=False,
        )(hidden_in, queries, cache, lengths, moves, norm_gain, kv_weight, out_weight)

    return whole
```

```python
import functools

import jax
import jax.numpy as jnp
from jax import lax
from jax.experimental import pallas as pl
from jax.experimental.pallas import tpu as pltpu
from jax.sharding import PartitionSpec as P

HD = 128
PAIR = 2
ROWS = 16
HALVES = 2
MESH = pl.DeviceIdType.MESH
F32 = jnp.float32
BF16 = jnp.bfloat16
NONE = 255
LOW = -1e30


def iota(shape, axis):
    return lax.broadcasted_iota(jnp.int32, shape, axis)


def kernel(
    sizes,
    lens_in, moves_in, hidden, query, cache, gain, kvw, outw,
    xout_ref, base_v,
    count_ref, lens_ref, moves_ref, xin, x0_v, q_v, qf_v, cache_v, gain_v, kvw_v, outw_v,
    mc_ref, sc_ref, ctx_ref, fresh_f, own_part, xnew, xnew_f, rs_send, rs_recv,
    pack, arr, info_pack, info_arr, place_v, place_s,
    perm_s, pick_ref, back_ref, sel_ref, sel2_ref, moved_ref, row_pack, row_arr,
    load_sem, outw_sem,
    rs_ss, rs_rs, ag_ss, ag_rs, hop_rs, fwd_ss, gc_ss, gc_rs, info_ss, info_rs, row_ss, row_rs,
    local_sem,
):
    G, L, T, micros, slots, width, ctx_len = sizes
    W = width // T
    H = HALVES
    S = W // H
    heads = W // HD
    pieces = heads + 2
    g = lax.axis_index("group")
    l = lax.axis_index("section")
    t = lax.axis_index("tensor")
    R = ROWS
    last = L - 1
    half = L // 2

    order = tuple(sorted(range(1, T), key=lambda d: -min(d, T - d)))

    def rs_copy(m, h, d):
        return pltpu.make_async_remote_copy(
            src_ref=rs_send.at[m, h, d - 1], dst_ref=rs_recv.at[m, h, d - 1],
            send_sem=rs_ss.at[m, h, d - 1], recv_sem=rs_rs.at[m, h],
            device_id={"tensor": lax.rem(t + d, T)}, device_id_type=MESH)

    def ag_copy(m, h, d):
        return pltpu.make_async_remote_copy(
            src_ref=xnew.at[m, h], dst_ref=xin.at[m, h, t],
            send_sem=ag_ss.at[m, h, d], recv_sem=ag_rs.at[m, h],
            device_id={"section": l + 1, "tensor": lax.rem(t + d, T)}, device_id_type=MESH)

    def hop_copy(m, h):
        return pltpu.make_async_remote_copy(
            src_ref=xnew.at[m, h], dst_ref=xin.at[m, h, t],
            send_sem=ag_ss.at[m, h, 0], recv_sem=hop_rs.at[m, h],
            device_id={"section": l + 1}, device_id_type=MESH)

    def fwd_copy(m, h, d):
        return pltpu.make_async_remote_copy(
            src_ref=xin.at[m, h, t], dst_ref=xin.at[m, h, t],
            send_sem=fwd_ss.at[m, h, d - 1], recv_sem=ag_rs.at[m, h],
            device_id={"tensor": lax.rem(t + d, T)}, device_id_type=MESH)

    def arrived(ref, sem):
        pltpu.make_async_copy(ref, ref, sem).wait()

    def to_group(src, dst, ss, rs, d):
        return pltpu.make_async_remote_copy(
            src_ref=src, dst_ref=dst, send_sem=ss.at[d - 1], recv_sem=rs.at[d - 1],
            device_id={"group": lax.rem(g + d, G)}, device_id_type=MESH)

    def gc_copy(d):
        e = PAIR * (d - 1)
        return to_group(pack.at[pl.ds(e, PAIR)], arr.at[pl.ds(e, PAIR)], gc_ss, gc_rs, d)

    def info_copy(d):
        return to_group(info_pack.at[d - 1], info_arr.at[d - 1], info_ss, info_rs, d)

    def row_copy(d):
        return to_group(row_pack.at[d - 1], row_arr.at[d - 1], row_ss, row_rs, d)

    def outw_load(h, d):
        start = pl.multiple_of(lax.rem(t + d, T) * W + h * S, S)
        place = order.index(d) if d else T - 1
        return pltpu.make_async_copy(
            outw.at[0, :, pl.ds(start, S)], outw_v.at[h, :, pl.ds(place * S, S)], outw_sem.at[h, d])

    query_load = pltpu.make_async_copy(query.at[0], q_v, load_sem.at[0])
    cache_load = pltpu.make_async_copy(cache.at[0], cache_v, load_sem.at[1])
    lens_load = pltpu.make_async_copy(lens_in, lens_ref, load_sem.at[5])
    moves_load = pltpu.make_async_copy(moves_in, moves_ref, load_sem.at[6])
    x_load = pltpu.make_async_copy(hidden, x0_v, load_sem.at[4])
    gain_load = pltpu.make_async_copy(gain, gain_v, load_sem.at[2])
    movers = moves_ref.shape[1]
    place_load = pltpu.make_async_copy(place_v.at[0], place_s, local_sem.at[0])

    lens_load.start(priority=1)
    moves_load.start(priority=1)
    query_load.start(priority=1)
    cache_load.start(priority=1)

    @pl.when(l == 0)
    def _():
        x_load.start(priority=1)

    gain_load.start(priority=1)
    for h in range(H):
        for q in range(T):
            pltpu.make_async_copy(
                kvw.at[0, pl.ds(q * W + h * S, S)], kvw_v.at[h, pl.ds(q * S, S)],
                load_sem.at[3]).start(priority=1)

    barrier = pltpu.get_barrier_semaphore()
    for d in range(1, T):
        pl.semaphore_signal(barrier, inc=1, device_id={"tensor": lax.rem(t + d, T)}, device_id_type=MESH)
    for d in range(1, G):
        pl.semaphore_signal(barrier, inc=1, device_id={"group": lax.rem(g + d, G)}, device_id_type=MESH)

    @pl.when(l > 0)
    def _():
        for k in range(T):
            pl.semaphore_signal(
                barrier, inc=1, device_id={"section": l - 1, "tensor": k}, device_id_type=MESH)

    @pl.when((l > 0) & (l < last))
    def _():
        pl.semaphore_wait(barrier, T - 1 + G - 1 + T)

    @pl.when(l == last)
    def _():
        pl.semaphore_wait(barrier, T - 1 + G - 1)

    def arrange():
        leaving = [moves_ref[0, i] for i in range(movers)]
        ranked = list(leaving)
        for end in range(movers - 1, 0, -1):
            for i in range(end):
                low = jnp.minimum(ranked[i], ranked[i + 1])
                high = jnp.maximum(ranked[i], ranked[i + 1])
                ranked[i], ranked[i + 1] = low, high

        def staying(position):
            slot = position - movers
            for k in range(movers):
                slot = slot + (slot >= ranked[k]).astype(jnp.int32)
            return slot

        def slot_of(position):
            slot = staying(position)
            for i in range(movers):
                slot = jnp.where(position == i, leaving[i], slot)
            return slot

        def place(p, carry):
            perm_s[p] = staying(p)
            return carry

        for i in range(movers):
            perm_s[i] = leaving[i]
        lax.fori_loop(movers, slots, place, 0)
        square = (slots, slots)
        row, col = iota(square, 0), iota(square, 1)
        pick_ref[...] = jnp.where(slot_of(row) == col, 1.0, 0.0).astype(BF16)
        back_ref[...] = jnp.where((staying(col) == row) & (col >= movers), 1.0, 0.0).astype(BF16)

    block = 8
    blocks = slots // block

    def attend(first, end):
        span = block * ctx_len
        scale = HD ** -0.5

        def one(b, carry):
            rows = pl.ds(pl.multiple_of(b * block, block), block)
            lens = jnp.zeros((block, span), jnp.int32)
            row = iota((block, span), 0)
            slot = [perm_s[b * block + n] for n in range(block)]
            for n in range(block):
                lens = jnp.where(row == n, lens_ref[slot[n]], lens)
            tokens = jnp.concatenate([cache_v[slot[n]] for n in range(block)], axis=0)
            col = iota((block, span), 1)
            ok = (col // ctx_len == row) & (col % ctx_len < lens)
            bias = jnp.where(ok, 0.0, LOW).astype(F32)
            stacked = jnp.concatenate(
                [qf_v[rows, a * HD:(a + 1) * HD] for a in range(heads)], axis=0).astype(BF16)
            keys = tokens[:, 0:HD]
            values = tokens[:, HD:2 * HD]
            score = lax.dot_general(
                stacked, keys, (((1,), (1,)), ((), ())), preferred_element_type=F32)
            score = score.reshape(heads, block, span) * scale + bias[None]
            top = jnp.max(score, axis=-1, keepdims=True)
            weight = jnp.exp(score - top)
            total = jnp.sum(weight, axis=-1, keepdims=True)
            mixed = jnp.dot(
                weight.reshape(heads * block, span).astype(BF16), values,
                preferred_element_type=F32)
            ctx_ref[:, rows, :] = mixed.reshape(heads, block, HD)
            mc_ref[:, rows, :] = jnp.broadcast_to(top, (heads, block, HD))
            sc_ref[:, rows, :] = jnp.broadcast_to(total, (heads, block, HD))
            return carry

        lax.fori_loop(first, end, one, 0)

    def depart():
        lane = iota((8, 256), 1)
        sel_row = iota(sel_ref.shape, 0)
        slot_at = jnp.full(sel_ref.shape, NONE, jnp.int32)
        for d in range(1, G):
            e = d - 1
            dest = lax.rem(g + d, G)
            place_vec = jnp.zeros((8, 256), jnp.int32)
            len_vec = jnp.zeros((8, 256), jnp.int32)
            for i in range(PAIR):
                slot = jnp.int32(NONE)
                place = jnp.int32(NONE)
                from_slot = jnp.int32(0)
                for k in range(movers // PAIR):
                    hit = moves_ref[1, PAIR * k] == dest
                    slot = jnp.where(hit, PAIR * k + i, slot)
                    place = jnp.where(hit, moves_ref[2, PAIR * k + i], place)
                    from_slot = jnp.where(hit, moves_ref[0, PAIR * k + i], from_slot)
                here = lane // 16 == e * PAIR + i
                place_vec = jnp.where(here, place, place_vec)
                len_vec = jnp.where(here, lens_ref[from_slot], len_vec)
                slot_at = jnp.where(sel_row // 16 == e * PAIR + i, slot, slot_at)
                pack[PAIR * e + i] = cache_v[from_slot]
            info_pack[e, 0:8, :] = place_vec
            info_pack[e, 8:16, :] = len_vec
            info_copy(d).start()
            gc_copy(d).start()
        sel_col = iota(sel_ref.shape, 1)
        chosen = (sel_row % 16 == sel_col // R) & (slot_at == sel_col % R)
        sel_ref[...] = jnp.where(chosen, 1.0, 0.0).astype(BF16)

    def arrive():
        for d in range(1, G):
            info_copy(d).wait_recv()
        place = info_arr[0, 0:8, :]
        length = info_arr[0, 8:16, :]
        for e in range(1, G - 1):
            place = place + info_arr[e, 0:8, :]
            length = length + info_arr[e, 8:16, :]
        lane8 = iota((8, 256), 1)
        place = jnp.where(lane8 < (G - 1) * PAIR * 16, place, NONE)
        place_v[0] = place
        place_load.start()
        wide = (slots, 256)
        spot = jnp.broadcast_to(place[0:1, :], wide)
        long = jnp.broadcast_to(length[0:1, :], wide)
        lane = iota(wide, 1)
        row = iota(wide, 0)
        match = spot == row
        first = match & (lane % 16 == 0)
        has = jnp.max(jnp.where(first, 1.0, 0.0), axis=-1, keepdims=True)
        moved_len = jnp.max(jnp.where(first, long.astype(F32), 0.0), axis=-1, keepdims=True)
        own_len = jnp.zeros((slots, HD), F32)
        narrow = iota((slots, HD), 0)
        for n in range(slots):
            own_len = jnp.where(narrow == n, lens_ref[n].astype(F32), own_len)
        count_ref[...] = jnp.where(has > 0.5, moved_len, own_len).astype(jnp.int32)
        for c in range(pieces):
            sel2_ref[c * slots:(c + 1) * slots, :] = jnp.where(
                match & (lane % 16 == c), 1.0, 0.0).astype(BF16)
        for d in range(1, G):
            gc_copy(d).wait_recv()
        place_load.wait()

        def fill(j, carry):
            index = jnp.int32(-1)
            for e in range((G - 1) * PAIR):
                index = jnp.where(place_s[0, e * 16] == j, e, index)
            moved = arr[jnp.maximum(index, 0)]
            kept = cache_v[j]
            base_v[j] = lax.select_n(index >= 0, kept, moved)
            return carry

        lax.fori_loop(0, slots, fill, 0)

    def pass_on(m, h):
        arrived(xin.at[m, h, t], hop_rs.at[m, h])
        for d in order:
            fwd_copy(m, h, d).start()

    def forward(m):
        @pl.when(l == half)
        def _():
            pass_on(m, 0)

    def whole_fresh():
        acc = jnp.zeros((slots, 2 * HD), F32)
        square = jnp.zeros((slots, 1), F32)
        for h in range(H):
            scaled = []
            for q in range(T):
                cols = slice(q * W + h * S, q * W + (h + 1) * S)
                xq = x0_v[:, cols].astype(F32)
                square = square + jnp.sum(xq * xq, axis=-1, keepdims=True)
                scaled.append((xq * gain_v[:, cols]).astype(BF16))
            acc = acc + jnp.dot(
                jnp.concatenate(scaled, axis=1), kvw_v[h], preferred_element_type=F32)
        fresh = (acc * lax.rsqrt(square * (1.0 / width) + 1e-06)).astype(BF16)
        fresh_f[...] = jnp.dot(pick_ref[...], fresh, preferred_element_type=F32)
        mine = x0_v[:, pl.ds(pl.multiple_of(t * W, W), W)]
        ordered = jnp.dot(pick_ref[...], mine, preferred_element_type=F32).astype(BF16)
        for m in range(micros):
            for h in range(H):
                xin[m, h, t] = ordered[m * R:(m + 1) * R, h * S:(h + 1) * S]

    def fresh_part(m):
        rows = pl.ds(pl.multiple_of(m * R, R), R)
        acc = jnp.zeros((R, 2 * HD), F32)
        square = jnp.zeros((R, 1), F32)
        for h in range(H):

            if h:
                arrived(xin.at[m, h], ag_rs.at[m, h])
            else:

                @pl.when(l != half)
                def _():
                    arrived(xin.at[m, h], ag_rs.at[m, h])

                @pl.when(l == half)
                def _():
                    arrived(xin.at[m, h, pl.ds(0, T - 1)], ag_rs.at[m, h])

            scaled = []
            for q in range(T):
                cols = slice(q * W + h * S, q * W + (h + 1) * S)
                xq = xin[m, h, q].astype(F32)
                square = square + jnp.sum(xq * xq, axis=-1, keepdims=True)
                scaled.append((xq * gain_v[:, cols]).astype(BF16))
            acc = acc + jnp.dot(
                jnp.concatenate(scaled, axis=1), kvw_v[h], preferred_element_type=F32)
        fresh = (acc * lax.rsqrt(square * (1.0 / width) + 1e-06)).astype(BF16).astype(F32)
        fresh_f[rows, :] = fresh

    def front(m):
        rows = pl.ds(pl.multiple_of(m * R, R), R)

        @pl.when(l > 0)
        def _():
            fresh_part(m)

        fresh = fresh_f[rows, :]
        key = fresh[:, 0:HD]
        value = fresh[:, HD:2 * HD]
        parts = []
        for a in range(heads):
            qa = qf_v[rows, a * HD:(a + 1) * HD]
            own = jnp.sum(qa * key, axis=-1, keepdims=True) * (HD ** -0.5)
            old_top = mc_ref[a, rows, :]
            top = jnp.maximum(old_top, own)
            old_scale = jnp.exp(old_top - top)
            own_weight = jnp.exp(own - top)
            total = sc_ref[a, rows, :] * old_scale + own_weight
            mixed = (ctx_ref[a, rows, :] * old_scale + own_weight * value) / total
            parts.append(mixed.astype(BF16))
        return jnp.concatenate(parts, axis=1)

    def project(m, context, h):
        for i, d in enumerate(order):
            part = jnp.dot(
                context, outw_v[h, :, i * S:(i + 1) * S], preferred_element_type=F32)
            if i or h:
                rs_copy(m, h if i else h - 1, order[i - 1]).start()
            rs_send[m, h, d - 1] = part.astype(BF16)
        if h == H - 1:
            rs_copy(m, h, order[-1]).start()

    def project_own(m, context, h):
        own_part[m, h] = jnp.dot(
            context, outw_v[h, :, (T - 1) * S:T * S], preferred_element_type=F32)

    def reduce(m, h):
        total = own_part[m, h] + xin[m, h, t].astype(F32)
        arrived(rs_recv.at[m, h], rs_rs.at[m, h])
        for d in order:
            total = total + rs_recv[m, h, d - 1].astype(F32)
        rounded = total.astype(BF16)
        xnew[m, h] = rounded
        xnew_f[pl.ds(pl.multiple_of(m * R, R), R), h * S:(h + 1) * S] = rounded.astype(F32)

        @pl.when((l < last) if h else (l < last) & (l != half - 1))
        def _():
            for d in order + (0,):
                ag_copy(m, h, d).start()

        if h == 0:

            @pl.when(l == half - 1)
            def _():
                hop_copy(m, h).start()

    def exchange():
        stacked = jnp.concatenate(
            [xnew_f[0:R, c * HD:(c + 1) * HD] for c in range(heads)]
            + [fresh_f[0:R, c * HD:(c + 1) * HD] for c in range(2)], axis=0).astype(BF16)
        leaving = jnp.dot(sel_ref[...], stacked, preferred_element_type=F32).astype(BF16)
        for d in range(1, G):
            row_pack[d - 1] = leaving[(d - 1) * 32:d * 32]
            row_copy(d).start()

    def collect():
        row_arr[G - 1] = jnp.zeros((32, HD), BF16)
        for d in range(1, G):
            row_copy(d).wait_recv()
        moved_ref[...] = jnp.dot(
            sel2_ref[...], row_arr[...].reshape(G * 32, HD), preferred_element_type=F32)

    def settle():
        kept = jnp.dot(back_ref[...], fresh_f[...].astype(BF16), preferred_element_type=F32)
        token = iota((ctx_len, HD), 0)
        for k in range(2):
            cols = slice(k * HD, (k + 1) * HD)
            c = heads + k
            fresh = kept[:, cols] + moved_ref[c * slots:(c + 1) * slots, :]
            for j in range(slots):
                here = token == count_ref[j:j + 1, :]
                base_v[j, :, cols] = jnp.where(
                    here, fresh[j:j + 1, :], base_v[j, :, cols].astype(F32)).astype(BF16)

    def emit(h):
        cols = slice(h * S, (h + 1) * S)
        kept = jnp.dot(
            back_ref[...], xnew_f[:, cols].astype(BF16), preferred_element_type=F32)
        for k in range(S // HD):
            c = h * (S // HD) + k
            xout_ref[:, c * HD:(c + 1) * HD] = (
                kept[:, k * HD:(k + 1) * HD] + moved_ref[c * slots:(c + 1) * slots, :]).astype(BF16)

    def rs_sent(m):
        for h in range(H):
            for d in order:
                rs_copy(m, h, d).wait_send()

    def sent():
        for m in range(micros - 1):
            rs_sent(m)
        for d in range(1, G):
            info_copy(d).wait_send()
            gc_copy(d).wait_send()
            row_copy(d).wait_send()

    lens_load.wait()
    moves_load.wait()
    arrange()
    for h in range(H):
        for d in order:
            outw_load(h, d).start()
    query_load.wait()
    cache_load.wait()
    qf_v[...] = jnp.dot(pick_ref[...], q_v[...], preferred_element_type=F32)
    first = R // block
    attend(0, first)
    for h in range(H):
        outw_load(h, 0).start()

    @pl.when(l > 0)
    def _():
        attend(first, blocks)
        depart()

    @pl.when(l == 0)
    def _():
        x_load.wait()
        gain_load.wait()
        arrived(kvw_v, load_sem.at[3])
        whole_fresh()

    @pl.when(l >= 3)
    def _():
        arrive()

    @pl.when(l > 0)
    def _():
        gain_load.wait()
        arrived(kvw_v, load_sem.at[3])

    forward(0)

    def batch(m, carry):
        context = front(m)

        @pl.when((l == 0) & (m == 0))
        def _():
            pl.semaphore_wait(barrier, T - 1 + G - 1 + T)

        @pl.when(m == 0)
        def _():
            for h in range(H):
                for d in order + (0,):
                    outw_load(h, d).wait()

        for h in range(H):
            project(m, context, h)

        @pl.when(m + 1 < micros)
        def _():
            forward(m + 1)

        for h in range(H):
            project_own(m, context, h)

        @pl.when((l == 0) & (m == 0))
        def _():
            attend(first, blocks)

        @pl.when((l == last) & (m == micros - 1))
        def _():
            collect()
            settle()
            sent()

        for h in range(H):
            reduce(m, h)
            if h < H - 1:

                @pl.when((l == last) & (m == micros - 1))
                def _():
                    emit(h)

        @pl.when((l == last) & (m == 0))
        def _():
            exchange()

        return carry

    lax.fori_loop(0, micros, batch, 0)

    @pl.when(l == 0)
    def _():
        depart()

    @pl.when(l < 3)
    def _():
        arrive()

    @pl.when(l < last)
    def _():
        exchange()
        collect()
        settle()

    @pl.when(l < last)
    def _():
        for h in range(H - 1):
            emit(h)

    emit(H - 1)

    @pl.when(l < last)
    def _():
        sent()

    rs_sent(micros - 1)

    @pl.when((l < last) & (l != half - 1))
    def _():
        for m in range(micros):
            for d in range(T):
                ag_copy(m, 0, d).wait_send()

    @pl.when(l < last)
    def _():
        for m in range(micros):
            for h in range(1, H):
                for d in range(T):
                    ag_copy(m, h, d).wait_send()

    @pl.when(l == half - 1)
    def _():
        for m in range(micros):
            hop_copy(m, 0).wait_send()

    @pl.when(l == half)
    def _():
        for m in range(micros):
            for d in order:
                fwd_copy(m, 0, d).wait_send()


def finish(chunks, xout, base, layer_out, new_cache, out_sem, x_sem):
    part = base.shape[0] // chunks

    def store(c):
        rows = pl.ds(c * part, part)
        return pltpu.make_async_copy(base.at[rows], new_cache.at[0, rows], out_sem.at[c])

    rows_copy = pltpu.make_async_copy(xout, layer_out.at[0], x_sem.at[0])
    for c in range(chunks):
        store(c).start()
    rows_copy.start()
    for c in range(chunks):
        store(c).wait()
    rows_copy.wait()


def per_device(sizes, hidden_in, queries, cache, lengths, moves, norm_gain, kv_weight, out_weight):
    G, L, T, micros, slots, width, ctx_len = sizes
    W = width // T
    heads = W // HD
    pieces = heads + 2
    R = ROWS
    H = HALVES
    S = W // H
    kv = 2 * HD
    movers = (G - 1) * PAIR
    any_spec = pl.BlockSpec(memory_space=pl.ANY)
    vmem = pl.BlockSpec(memory_space=pltpu.VMEM)
    dma = pltpu.SemaphoreType.DMA
    xout, base = pl.pallas_call(
        functools.partial(kernel, sizes),
        out_shape=(
            pltpu.VMEM((slots, W), BF16),
            pltpu.VMEM((slots, ctx_len, kv), BF16),
        ),
        in_specs=[any_spec] * 8,
        out_specs=(vmem, vmem),
        scratch_shapes=[
            pltpu.VMEM((slots, HD), jnp.int32),
            pltpu.SMEM(lengths.shape, jnp.int32),
            pltpu.SMEM(moves.shape[::-1], jnp.int32),
            pltpu.VMEM((micros, H, T, R, S), BF16),
            pltpu.VMEM((slots, width), BF16),
            pltpu.VMEM((slots, W), BF16),
            pltpu.VMEM((slots, W), F32),
            pltpu.VMEM((slots, ctx_len, kv), BF16),
            pltpu.VMEM((1, width), F32),
            pltpu.VMEM((H, T * S, kv), BF16),
            pltpu.VMEM((H, W, T * S), BF16),
            pltpu.VMEM((heads, slots, HD), F32),
            pltpu.VMEM((heads, slots, HD), F32),
            pltpu.VMEM((heads, slots, HD), F32),
            pltpu.VMEM((slots, kv), F32),
            pltpu.VMEM((micros, H, R, S), F32),
            pltpu.VMEM((micros, H, R, S), BF16),
            pltpu.VMEM((slots, W), F32),
            pltpu.VMEM((micros, H, T - 1, R, S), BF16),
            pltpu.VMEM((micros, H, T - 1, R, S), BF16),
            pltpu.VMEM((movers, ctx_len, kv), BF16),
            pltpu.VMEM((movers, ctx_len, kv), BF16),
            pltpu.VMEM((G - 1, 16, 256), jnp.int32),
            pltpu.VMEM((G - 1, 16, 256), jnp.int32),
            pltpu.VMEM((1, 8, 256), jnp.int32),
            pltpu.SMEM((8, 256), jnp.int32),
            pltpu.SMEM((slots,), jnp.int32),
            pltpu.VMEM((slots, slots), BF16),
            pltpu.VMEM((slots, slots), BF16),
            pltpu.VMEM(((G - 1) * 32, pieces * R), BF16),
            pltpu.VMEM((pieces * slots, 256), BF16),
            pltpu.VMEM((pieces * slots, HD), F32),
            pltpu.VMEM((G - 1, 32, HD), BF16),
            pltpu.VMEM((G, 32, HD), BF16),
            dma((7,)), dma((H, T)),
            dma((micros, H, T - 1)), dma((micros, H)),
            dma((micros, H, T)), dma((micros, H)), dma((micros, H)), dma((micros, H, T - 1)),
            dma((G - 1,)), dma((G - 1,)), dma((G - 1,)), dma((G - 1,)), dma((G - 1,)), dma((G - 1,)),
            dma((1,)),
        ],
        compiler_params=pltpu.CompilerParams(
            collective_id=0, has_side_effects=True, vmem_limit_bytes=56 * 1024 * 1024),
        name="chain",
    )(lengths, moves.T, hidden_in, queries, cache, norm_gain, kv_weight, out_weight)
    chunks = 4
    return pl.pallas_call(
        functools.partial(finish, chunks),
        out_shape=(
            jax.ShapeDtypeStruct((1, slots, W), BF16),
            jax.ShapeDtypeStruct((1, slots, ctx_len, kv), BF16),
        ),
        in_specs=[vmem] * 2,
        out_specs=(any_spec, any_spec),
        scratch_shapes=[dma((chunks,)), dma((1,))],
        compiler_params=pltpu.CompilerParams(vmem_limit_bytes=16 * 1024 * 1024),
        name="finish",
    )(*(pltpu.with_memory_space_constraint(part, pltpu.VMEM) for part in (xout, base)))


def solution(mesh):
    G, L, T = mesh.shape["group"], mesh.shape["section"], mesh.shape["tensor"]

    def whole(hidden_in, queries, cache, lengths, moves, norm_gain, kv_weight, out_weight):
        slots = hidden_in.shape[0] // G
        sizes = (G, L, T, slots // ROWS, slots, hidden_in.shape[1], cache.shape[2])
        return jax.shard_map(
            functools.partial(per_device, sizes),
            mesh=mesh,
            in_specs=(
                P("group", None),
                P("section", "group", "tensor"),
                P("section", "group", None, "tensor"),
                P("group"),
                P("group", None),
                P("section", None),
                P("section", None, "tensor"),
                P("section", "tensor", None),
            ),
            out_specs=(P("section", "group", "tensor"), P("section", "group", None, "tensor")),
            check_vma=False,
        )(hidden_in, queries, cache, lengths, moves, norm_gain, kv_weight, out_weight)

    return whole
```

```python
import functools

import jax
import jax.numpy as jnp
from jax import lax
from jax.experimental import pallas as pl
from jax.experimental.pallas import tpu as pltpu
from jax.sharding import PartitionSpec as P

HD = 128
PAIR = 2
ROWS = 16
HALVES = 2
MESH = pl.DeviceIdType.MESH
F32 = jnp.float32
BF16 = jnp.bfloat16
NONE = 255
LOW = -1e30


def iota(shape, axis):
    return lax.broadcasted_iota(jnp.int32, shape, axis)


def kernel(
    sizes,
    lens_in, moves_in, hidden, query, cache, gain, kvw, outw,
    xout_ref, base_v,
    count_ref, lens_ref, moves_ref, xin, x0_v, q_v, qf_v, cache_v, gain_v, kvw_v, outw_v,
    mc_ref, sc_ref, ctx_ref, fresh_f, own_part, xnew, xnew_f, rs_send, rs_recv,
    pack, arr, info_pack, info_arr, place_v, place_s,
    perm_s, pick_ref, back_ref, sel_ref, sel2_ref, moved_ref, row_pack, row_arr,
    load_sem, outw_sem,
    rs_ss, rs_rs, ag_ss, ag_rs, hop_rs, fwd_ss, gc_ss, gc_rs, info_ss, info_rs, row_ss, row_rs,
    local_sem,
):
    G, L, T, micros, slots, width, ctx_len = sizes
    W = width // T
    H = HALVES
    S = W // H
    heads = W // HD
    pieces = heads + 2
    g = lax.axis_index("group")
    l = lax.axis_index("section")
    t = lax.axis_index("tensor")
    R = ROWS
    last = L - 1
    half = L // 2

    order = tuple(sorted(range(1, T), key=lambda d: -min(d, T - d)))

    def rs_copy(m, h, d):
        return pltpu.make_async_remote_copy(
            src_ref=rs_send.at[m, h, d - 1], dst_ref=rs_recv.at[m, h, d - 1],
            send_sem=rs_ss.at[m, h, d - 1], recv_sem=rs_rs.at[m, h],
            device_id={"tensor": lax.rem(t + d, T)}, device_id_type=MESH)

    def ag_copy(m, h, d):
        return pltpu.make_async_remote_copy(
            src_ref=xnew.at[m, h], dst_ref=xin.at[m, h, t],
            send_sem=ag_ss.at[m, h, d], recv_sem=ag_rs.at[m, h],
            device_id={"section": l + 1, "tensor": lax.rem(t + d, T)}, device_id_type=MESH)

    def hop_copy(m, h):
        return pltpu.make_async_remote_copy(
            src_ref=xnew.at[m, h], dst_ref=xin.at[m, h, t],
            send_sem=ag_ss.at[m, h, 0], recv_sem=hop_rs.at[m, h],
            device_id={"section": l + 1}, device_id_type=MESH)

    def fwd_copy(m, h, d):
        return pltpu.make_async_remote_copy(
            src_ref=xin.at[m, h, t], dst_ref=xin.at[m, h, t],
            send_sem=fwd_ss.at[m, h, d - 1], recv_sem=ag_rs.at[m, h],
            device_id={"tensor": lax.rem(t + d, T)}, device_id_type=MESH)

    def arrived(ref, sem):
        pltpu.make_async_copy(ref, ref, sem).wait()

    def to_group(src, dst, ss, rs, d):
        return pltpu.make_async_remote_copy(
            src_ref=src, dst_ref=dst, send_sem=ss.at[d - 1], recv_sem=rs.at[d - 1],
            device_id={"group": lax.rem(g + d, G)}, device_id_type=MESH)

    def gc_copy(d):
        e = PAIR * (d - 1)
        return to_group(pack.at[pl.ds(e, PAIR)], arr.at[pl.ds(e, PAIR)], gc_ss, gc_rs, d)

    def info_copy(d):
        return to_group(info_pack.at[d - 1], info_arr.at[d - 1], info_ss, info_rs, d)

    def row_copy(d):
        return to_group(row_pack.at[d - 1], row_arr.at[d - 1], row_ss, row_rs, d)

    def outw_load(h, d):
        start = pl.multiple_of(lax.rem(t + d, T) * W + h * S, S)
        place = order.index(d) if d else T - 1
        return pltpu.make_async_copy(
            outw.at[0, :, pl.ds(start, S)], outw_v.at[h, :, pl.ds(place * S, S)], outw_sem.at[h, d])

    query_load = pltpu.make_async_copy(query.at[0], q_v, load_sem.at[0])
    cache_load = pltpu.make_async_copy(cache.at[0], cache_v, load_sem.at[1])
    lens_load = pltpu.make_async_copy(lens_in, lens_ref, load_sem.at[5])
    moves_load = pltpu.make_async_copy(moves_in, moves_ref, load_sem.at[6])
    x_load = pltpu.make_async_copy(hidden, x0_v, load_sem.at[4])
    gain_load = pltpu.make_async_copy(gain, gain_v, load_sem.at[2])
    movers = moves_ref.shape[1]
    place_load = pltpu.make_async_copy(place_v.at[0], place_s, local_sem.at[0])

    lens_load.start(priority=1)
    moves_load.start(priority=1)
    query_load.start(priority=1)
    cache_load.start(priority=1)

    @pl.when(l == 0)
    def _():
        x_load.start(priority=1)

    gain_load.start(priority=1)
    for h in range(H):
        for q in range(T):
            pltpu.make_async_copy(
                kvw.at[0, pl.ds(q * W + h * S, S)], kvw_v.at[h, pl.ds(q * S, S)],
                load_sem.at[3]).start(priority=1)

    for h in range(H):
        for d in order:
            outw_load(h, d).start()

    barrier = pltpu.get_barrier_semaphore()
    for d in range(1, T):
        pl.semaphore_signal(barrier, inc=1, device_id={"tensor": lax.rem(t + d, T)}, device_id_type=MESH)
    for d in range(1, G):
        pl.semaphore_signal(barrier, inc=1, device_id={"group": lax.rem(g + d, G)}, device_id_type=MESH)

    @pl.when(l > 0)
    def _():
        for k in range(T):
            pl.semaphore_signal(
                barrier, inc=1, device_id={"section": l - 1, "tensor": k}, device_id_type=MESH)

    @pl.when((l > 0) & (l < last))
    def _():
        pl.semaphore_wait(barrier, T - 1 + G - 1 + T)

    @pl.when(l == last)
    def _():
        pl.semaphore_wait(barrier, T - 1 + G - 1)

    def arrange():
        leaving = [moves_ref[0, i] for i in range(movers)]
        ranked = list(leaving)
        for end in range(movers - 1, 0, -1):
            for i in range(end):
                low = jnp.minimum(ranked[i], ranked[i + 1])
                high = jnp.maximum(ranked[i], ranked[i + 1])
                ranked[i], ranked[i + 1] = low, high

        def staying(position):
            slot = position - movers
            for k in range(movers):
                slot = slot + (slot >= ranked[k]).astype(jnp.int32)
            return slot

        def slot_of(position):
            slot = staying(position)
            for i in range(movers):
                slot = jnp.where(position == i, leaving[i], slot)
            return slot

        def place(p, carry):
            perm_s[p] = staying(p)
            return carry

        for i in range(movers):
            perm_s[i] = leaving[i]
        lax.fori_loop(movers, slots, place, 0)
        square = (slots, slots)
        row, col = iota(square, 0), iota(square, 1)
        pick_ref[...] = jnp.where(slot_of(row) == col, 1.0, 0.0).astype(BF16)
        back_ref[...] = jnp.where((staying(col) == row) & (col >= movers), 1.0, 0.0).astype(BF16)

    block = 8
    blocks = slots // block

    def attend(first, end):
        span = block * ctx_len
        scale = HD ** -0.5

        def one(b, carry):
            rows = pl.ds(pl.multiple_of(b * block, block), block)
            lens = jnp.zeros((block, span), jnp.int32)
            row = iota((block, span), 0)
            slot = [perm_s[b * block + n] for n in range(block)]
            for n in range(block):
                lens = jnp.where(row == n, lens_ref[slot[n]], lens)
            tokens = jnp.concatenate([cache_v[slot[n]] for n in range(block)], axis=0)
            col = iota((block, span), 1)
            ok = (col // ctx_len == row) & (col % ctx_len < lens)
            bias = jnp.where(ok, 0.0, LOW).astype(F32)
            stacked = jnp.concatenate(
                [qf_v[rows, a * HD:(a + 1) * HD] for a in range(heads)], axis=0).astype(BF16)
            keys = tokens[:, 0:HD]
            values = tokens[:, HD:2 * HD]
            score = lax.dot_general(
                stacked, keys, (((1,), (1,)), ((), ())), preferred_element_type=F32)
            score = score.reshape(heads, block, span) * scale + bias[None]
            top = jnp.max(score, axis=-1, keepdims=True)
            weight = jnp.exp(score - top)
            total = jnp.sum(weight, axis=-1, keepdims=True)
            mixed = jnp.dot(
                weight.reshape(heads * block, span).astype(BF16), values,
                preferred_element_type=F32)
            ctx_ref[:, rows, :] = mixed.reshape(heads, block, HD)
            mc_ref[:, rows, :] = jnp.broadcast_to(top, (heads, block, HD))
            sc_ref[:, rows, :] = jnp.broadcast_to(total, (heads, block, HD))
            return carry

        lax.fori_loop(first, end, one, 0)

    def depart():
        lane = iota((8, 256), 1)
        sel_row = iota(sel_ref.shape, 0)
        slot_at = jnp.full(sel_ref.shape, NONE, jnp.int32)
        for d in range(1, G):
            e = d - 1
            dest = lax.rem(g + d, G)
            place_vec = jnp.zeros((8, 256), jnp.int32)
            len_vec = jnp.zeros((8, 256), jnp.int32)
            for i in range(PAIR):
                slot = jnp.int32(NONE)
                place = jnp.int32(NONE)
                from_slot = jnp.int32(0)
                for k in range(movers // PAIR):
                    hit = moves_ref[1, PAIR * k] == dest
                    slot = jnp.where(hit, PAIR * k + i, slot)
                    place = jnp.where(hit, moves_ref[2, PAIR * k + i], place)
                    from_slot = jnp.where(hit, moves_ref[0, PAIR * k + i], from_slot)
                here = lane // 16 == e * PAIR + i
                place_vec = jnp.where(here, place, place_vec)
                len_vec = jnp.where(here, lens_ref[from_slot], len_vec)
                slot_at = jnp.where(sel_row // 16 == e * PAIR + i, slot, slot_at)
                pack[PAIR * e + i] = cache_v[from_slot]
            info_pack[e, 0:8, :] = place_vec
            info_pack[e, 8:16, :] = len_vec
            info_copy(d).start()
            gc_copy(d).start()
        sel_col = iota(sel_ref.shape, 1)
        chosen = (sel_row % 16 == sel_col // R) & (slot_at == sel_col % R)
        sel_ref[...] = jnp.where(chosen, 1.0, 0.0).astype(BF16)

    def arrive():
        for d in range(1, G):
            info_copy(d).wait_recv()
        place = info_arr[0, 0:8, :]
        length = info_arr[0, 8:16, :]
        for e in range(1, G - 1):
            place = place + info_arr[e, 0:8, :]
            length = length + info_arr[e, 8:16, :]
        lane8 = iota((8, 256), 1)
        place = jnp.where(lane8 < (G - 1) * PAIR * 16, place, NONE)
        place_v[0] = place
        place_load.start()
        wide = (slots, 256)
        spot = jnp.broadcast_to(place[0:1, :], wide)
        long = jnp.broadcast_to(length[0:1, :], wide)
        lane = iota(wide, 1)
        row = iota(wide, 0)
        match = spot == row
        first = match & (lane % 16 == 0)
        has = jnp.max(jnp.where(first, 1.0, 0.0), axis=-1, keepdims=True)
        moved_len = jnp.max(jnp.where(first, long.astype(F32), 0.0), axis=-1, keepdims=True)
        own_len = jnp.zeros((slots, HD), F32)
        narrow = iota((slots, HD), 0)
        for n in range(slots):
            own_len = jnp.where(narrow == n, lens_ref[n].astype(F32), own_len)
        count_ref[...] = jnp.where(has > 0.5, moved_len, own_len).astype(jnp.int32)
        for c in range(pieces):
            sel2_ref[c * slots:(c + 1) * slots, :] = jnp.where(
                match & (lane % 16 == c), 1.0, 0.0).astype(BF16)
        for d in range(1, G):
            gc_copy(d).wait_recv()
        place_load.wait()

        def fill(j, carry):
            index = jnp.int32(-1)
            for e in range((G - 1) * PAIR):
                index = jnp.where(place_s[0, e * 16] == j, e, index)
            moved = arr[jnp.maximum(index, 0)]
            kept = cache_v[j]
            base_v[j] = lax.select_n(index >= 0, kept, moved)
            return carry

        lax.fori_loop(0, slots, fill, 0)

    def pass_on(m, h):
        arrived(xin.at[m, h, t], hop_rs.at[m, h])
        for d in order:
            fwd_copy(m, h, d).start()

    def forward(m):
        @pl.when(l == half)
        def _():
            pass_on(m, 0)

    def whole_fresh():
        acc = jnp.zeros((slots, 2 * HD), F32)
        square = jnp.zeros((slots, 1), F32)
        for h in range(H):
            scaled = []
            for q in range(T):
                cols = slice(q * W + h * S, q * W + (h + 1) * S)
                xq = x0_v[:, cols].astype(F32)
                square = square + jnp.sum(xq * xq, axis=-1, keepdims=True)
                scaled.append((xq * gain_v[:, cols]).astype(BF16))
            acc = acc + jnp.dot(
                jnp.concatenate(scaled, axis=1), kvw_v[h], preferred_element_type=F32)
        fresh = (acc * lax.rsqrt(square * (1.0 / width) + 1e-06)).astype(BF16)
        fresh_f[...] = jnp.dot(pick_ref[...], fresh, preferred_element_type=F32)
        mine = x0_v[:, pl.ds(pl.multiple_of(t * W, W), W)]
        ordered = jnp.dot(pick_ref[...], mine, preferred_element_type=F32).astype(BF16)
        for m in range(micros):
            for h in range(H):
                xin[m, h, t] = ordered[m * R:(m + 1) * R, h * S:(h + 1) * S]

    def fresh_part(m):
        rows = pl.ds(pl.multiple_of(m * R, R), R)
        acc = jnp.zeros((R, 2 * HD), F32)
        square = jnp.zeros((R, 1), F32)
        for h in range(H):

            if h:
                arrived(xin.at[m, h], ag_rs.at[m, h])
            else:

                @pl.when(l != half)
                def _():
                    arrived(xin.at[m, h], ag_rs.at[m, h])

                @pl.when(l == half)
                def _():
                    arrived(xin.at[m, h, pl.ds(0, T - 1)], ag_rs.at[m, h])

            scaled = []
            for q in range(T):
                cols = slice(q * W + h * S, q * W + (h + 1) * S)
                xq = xin[m, h, q].astype(F32)
                square = square + jnp.sum(xq * xq, axis=-1, keepdims=True)
                scaled.append((xq * gain_v[:, cols]).astype(BF16))
            acc = acc + jnp.dot(
                jnp.concatenate(scaled, axis=1), kvw_v[h], preferred_element_type=F32)
        fresh = (acc * lax.rsqrt(square * (1.0 / width) + 1e-06)).astype(BF16).astype(F32)
        fresh_f[rows, :] = fresh

    def front(m):
        rows = pl.ds(pl.multiple_of(m * R, R), R)

        @pl.when(l > 0)
        def _():
            fresh_part(m)

        fresh = fresh_f[rows, :]
        key = fresh[:, 0:HD]
        value = fresh[:, HD:2 * HD]
        parts = []
        for a in range(heads):
            qa = qf_v[rows, a * HD:(a + 1) * HD]
            own = jnp.sum(qa * key, axis=-1, keepdims=True) * (HD ** -0.5)
            old_top = mc_ref[a, rows, :]
            top = jnp.maximum(old_top, own)
            old_scale = jnp.exp(old_top - top)
            own_weight = jnp.exp(own - top)
            total = sc_ref[a, rows, :] * old_scale + own_weight
            mixed = (ctx_ref[a, rows, :] * old_scale + own_weight * value) / total
            parts.append(mixed.astype(BF16))
        return jnp.concatenate(parts, axis=1)

    def project(m, context, h):
        for i, d in enumerate(order):
            part = jnp.dot(
                context, outw_v[h, :, i * S:(i + 1) * S], preferred_element_type=F32)
            if i or h:
                rs_copy(m, h if i else h - 1, order[i - 1]).start()
            rs_send[m, h, d - 1] = part.astype(BF16)
        if h == H - 1:
            rs_copy(m, h, order[-1]).start()

    def project_own(m, context, h):
        own_part[m, h] = jnp.dot(
            context, outw_v[h, :, (T - 1) * S:T * S], preferred_element_type=F32)

    def reduce(m, h):
        total = own_part[m, h] + xin[m, h, t].astype(F32)
        arrived(rs_recv.at[m, h], rs_rs.at[m, h])
        for d in order:
            total = total + rs_recv[m, h, d - 1].astype(F32)
        rounded = total.astype(BF16)
        xnew[m, h] = rounded
        xnew_f[pl.ds(pl.multiple_of(m * R, R), R), h * S:(h + 1) * S] = rounded.astype(F32)

        @pl.when((l < last) if h else (l < last) & (l != half - 1))
        def _():
            for d in order + (0,):
                ag_copy(m, h, d).start()

        if h == 0:

            @pl.when(l == half - 1)
            def _():
                hop_copy(m, h).start()

    def exchange():
        stacked = jnp.concatenate(
            [xnew_f[0:R, c * HD:(c + 1) * HD] for c in range(heads)]
            + [fresh_f[0:R, c * HD:(c + 1) * HD] for c in range(2)], axis=0).astype(BF16)
        leaving = jnp.dot(sel_ref[...], stacked, preferred_element_type=F32).astype(BF16)
        for d in range(1, G):
            row_pack[d - 1] = leaving[(d - 1) * 32:d * 32]
            row_copy(d).start()

    def collect():
        row_arr[G - 1] = jnp.zeros((32, HD), BF16)
        for d in range(1, G):
            row_copy(d).wait_recv()
        moved_ref[...] = jnp.dot(
            sel2_ref[...], row_arr[...].reshape(G * 32, HD), preferred_element_type=F32)

    def settle():
        kept = jnp.dot(back_ref[...], fresh_f[...].astype(BF16), preferred_element_type=F32)
        token = iota((ctx_len, HD), 0)
        for k in range(2):
            cols = slice(k * HD, (k + 1) * HD)
            c = heads + k
            fresh = kept[:, cols] + moved_ref[c * slots:(c + 1) * slots, :]
            for j in range(slots):
                here = token == count_ref[j:j + 1, :]
                base_v[j, :, cols] = jnp.where(
                    here, fresh[j:j + 1, :], base_v[j, :, cols].astype(F32)).astype(BF16)

    def emit(h):
        cols = slice(h * S, (h + 1) * S)
        kept = jnp.dot(
            back_ref[...], xnew_f[:, cols].astype(BF16), preferred_element_type=F32)
        for k in range(S // HD):
            c = h * (S // HD) + k
            xout_ref[:, c * HD:(c + 1) * HD] = (
                kept[:, k * HD:(k + 1) * HD] + moved_ref[c * slots:(c + 1) * slots, :]).astype(BF16)

    def rs_sent(m):
        for h in range(H):
            for d in order:
                rs_copy(m, h, d).wait_send()

    def sent():
        for m in range(micros - 1):
            rs_sent(m)
        for d in range(1, G):
            info_copy(d).wait_send()
            gc_copy(d).wait_send()
            row_copy(d).wait_send()

    lens_load.wait()
    moves_load.wait()
    arrange()
    query_load.wait()
    cache_load.wait()
    qf_v[...] = jnp.dot(pick_ref[...], q_v[...], preferred_element_type=F32)
    first = R // block
    attend(0, first)
    for h in range(H):
        outw_load(h, 0).start()

    @pl.when(l > 0)
    def _():
        attend(first, blocks)
        depart()

    @pl.when(l == 0)
    def _():
        x_load.wait()
        gain_load.wait()
        arrived(kvw_v, load_sem.at[3])
        whole_fresh()

    @pl.when(l >= 3)
    def _():
        arrive()

    @pl.when(l > 0)
    def _():
        gain_load.wait()
        arrived(kvw_v, load_sem.at[3])

    forward(0)

    def batch(m, carry):
        context = front(m)

        @pl.when((l == 0) & (m == 0))
        def _():
            pl.semaphore_wait(barrier, T - 1 + G - 1 + T)

        @pl.when(m == 0)
        def _():
            for h in range(H):
                for d in order + (0,):
                    outw_load(h, d).wait()

        for h in range(H):
            project(m, context, h)

        @pl.when(m + 1 < micros)
        def _():
            forward(m + 1)

        for h in range(H):
            project_own(m, context, h)

        @pl.when((l == 0) & (m == 0))
        def _():
            attend(first, blocks)

        @pl.when((l == last) & (m == micros - 1))
        def _():
            collect()
            settle()
            sent()

        for h in range(H):
            reduce(m, h)
            if h < H - 1:

                @pl.when((l == last) & (m == micros - 1))
                def _():
                    emit(h)

        @pl.when((l == last) & (m == 0))
        def _():
            exchange()

        return carry

    lax.fori_loop(0, micros, batch, 0)

    @pl.when(l == 0)
    def _():
        depart()

    @pl.when(l < 3)
    def _():
        arrive()

    @pl.when(l < last)
    def _():
        exchange()
        collect()
        settle()

    @pl.when(l < last)
    def _():
        for h in range(H - 1):
            emit(h)

    emit(H - 1)

    @pl.when(l < last)
    def _():
        sent()

    rs_sent(micros - 1)

    @pl.when((l < last) & (l != half - 1))
    def _():
        for m in range(micros):
            for d in range(T):
                ag_copy(m, 0, d).wait_send()

    @pl.when(l < last)
    def _():
        for m in range(micros):
            for h in range(1, H):
                for d in range(T):
                    ag_copy(m, h, d).wait_send()

    @pl.when(l == half - 1)
    def _():
        for m in range(micros):
            hop_copy(m, 0).wait_send()

    @pl.when(l == half)
    def _():
        for m in range(micros):
            for d in order:
                fwd_copy(m, 0, d).wait_send()


def finish(chunks, xout, base, layer_out, new_cache, out_sem, x_sem):
    part = base.shape[0] // chunks

    def store(c):
        rows = pl.ds(c * part, part)
        return pltpu.make_async_copy(base.at[rows], new_cache.at[0, rows], out_sem.at[c])

    rows_copy = pltpu.make_async_copy(xout, layer_out.at[0], x_sem.at[0])
    for c in range(chunks):
        store(c).start()
    rows_copy.start()
    for c in range(chunks):
        store(c).wait()
    rows_copy.wait()


def per_device(sizes, hidden_in, queries, cache, lengths, moves, norm_gain, kv_weight, out_weight):
    G, L, T, micros, slots, width, ctx_len = sizes
    W = width // T
    heads = W // HD
    pieces = heads + 2
    R = ROWS
    H = HALVES
    S = W // H
    kv = 2 * HD
    movers = (G - 1) * PAIR
    any_spec = pl.BlockSpec(memory_space=pl.ANY)
    vmem = pl.BlockSpec(memory_space=pltpu.VMEM)
    dma = pltpu.SemaphoreType.DMA
    xout, base = pl.pallas_call(
        functools.partial(kernel, sizes),
        out_shape=(
            pltpu.VMEM((slots, W), BF16),
            pltpu.VMEM((slots, ctx_len, kv), BF16),
        ),
        in_specs=[any_spec] * 8,
        out_specs=(vmem, vmem),
        scratch_shapes=[
            pltpu.VMEM((slots, HD), jnp.int32),
            pltpu.SMEM(lengths.shape, jnp.int32),
            pltpu.SMEM(moves.shape[::-1], jnp.int32),
            pltpu.VMEM((micros, H, T, R, S), BF16),
            pltpu.VMEM((slots, width), BF16),
            pltpu.VMEM((slots, W), BF16),
            pltpu.VMEM((slots, W), F32),
            pltpu.VMEM((slots, ctx_len, kv), BF16),
            pltpu.VMEM((1, width), F32),
            pltpu.VMEM((H, T * S, kv), BF16),
            pltpu.VMEM((H, W, T * S), BF16),
            pltpu.VMEM((heads, slots, HD), F32),
            pltpu.VMEM((heads, slots, HD), F32),
            pltpu.VMEM((heads, slots, HD), F32),
            pltpu.VMEM((slots, kv), F32),
            pltpu.VMEM((micros, H, R, S), F32),
            pltpu.VMEM((micros, H, R, S), BF16),
            pltpu.VMEM((slots, W), F32),
            pltpu.VMEM((micros, H, T - 1, R, S), BF16),
            pltpu.VMEM((micros, H, T - 1, R, S), BF16),
            pltpu.VMEM((movers, ctx_len, kv), BF16),
            pltpu.VMEM((movers, ctx_len, kv), BF16),
            pltpu.VMEM((G - 1, 16, 256), jnp.int32),
            pltpu.VMEM((G - 1, 16, 256), jnp.int32),
            pltpu.VMEM((1, 8, 256), jnp.int32),
            pltpu.SMEM((8, 256), jnp.int32),
            pltpu.SMEM((slots,), jnp.int32),
            pltpu.VMEM((slots, slots), BF16),
            pltpu.VMEM((slots, slots), BF16),
            pltpu.VMEM(((G - 1) * 32, pieces * R), BF16),
            pltpu.VMEM((pieces * slots, 256), BF16),
            pltpu.VMEM((pieces * slots, HD), F32),
            pltpu.VMEM((G - 1, 32, HD), BF16),
            pltpu.VMEM((G, 32, HD), BF16),
            dma((7,)), dma((H, T)),
            dma((micros, H, T - 1)), dma((micros, H)),
            dma((micros, H, T)), dma((micros, H)), dma((micros, H)), dma((micros, H, T - 1)),
            dma((G - 1,)), dma((G - 1,)), dma((G - 1,)), dma((G - 1,)), dma((G - 1,)), dma((G - 1,)),
            dma((1,)),
        ],
        compiler_params=pltpu.CompilerParams(
            collective_id=0, has_side_effects=True, vmem_limit_bytes=56 * 1024 * 1024),
        name="chain",
    )(lengths, moves.T, hidden_in, queries, cache, norm_gain, kv_weight, out_weight)
    chunks = 4
    return pl.pallas_call(
        functools.partial(finish, chunks),
        out_shape=(
            jax.ShapeDtypeStruct((1, slots, W), BF16),
            jax.ShapeDtypeStruct((1, slots, ctx_len, kv), BF16),
        ),
        in_specs=[vmem] * 2,
        out_specs=(any_spec, any_spec),
        scratch_shapes=[dma((chunks,)), dma((1,))],
        compiler_params=pltpu.CompilerParams(vmem_limit_bytes=16 * 1024 * 1024),
        name="finish",
    )(*(pltpu.with_memory_space_constraint(part, pltpu.VMEM) for part in (xout, base)))


def solution(mesh):
    G, L, T = mesh.shape["group"], mesh.shape["section"], mesh.shape["tensor"]

    def whole(hidden_in, queries, cache, lengths, moves, norm_gain, kv_weight, out_weight):
        slots = hidden_in.shape[0] // G
        sizes = (G, L, T, slots // ROWS, slots, hidden_in.shape[1], cache.shape[2])
        return jax.shard_map(
            functools.partial(per_device, sizes),
            mesh=mesh,
            in_specs=(
                P("group", None),
                P("section", "group", "tensor"),
                P("section", "group", None, "tensor"),
                P("group"),
                P("group", None),
                P("section", None),
                P("section", None, "tensor"),
                P("section", "tensor", None),
            ),
            out_specs=(P("section", "group", "tensor"), P("section", "group", None, "tensor")),
            check_vma=False,
        )(hidden_in, queries, cache, lengths, moves, norm_gain, kv_weight, out_weight)

    return whole
```

```python
import functools

import jax
import jax.numpy as jnp
from jax import lax
from jax.experimental import pallas as pl
from jax.experimental.pallas import tpu as pltpu
from jax.sharding import PartitionSpec as P

HD = 128
PAIR = 2
ROWS = 16
HALVES = 2
MESH = pl.DeviceIdType.MESH
F32 = jnp.float32
BF16 = jnp.bfloat16
NONE = 255
LOW = -1e30


def iota(shape, axis):
    return lax.broadcasted_iota(jnp.int32, shape, axis)


def kernel(
    sizes,
    lens_in, moves_in, hidden, query, cache, gain, kvw, outw,
    xout_ref, base_v,
    count_ref, lens_ref, moves_ref, xin, x0_v, q_v, qf_v, cache_v, gain_v, kvw_v, outw_v,
    mc_ref, sc_ref, ctx_ref, fresh_f, own_part, xnew, xnew_f, rs_send, rs_recv,
    pack, arr, info_pack, info_arr, place_v, place_s,
    perm_s, pick_ref, back_ref, sel_ref, sel2_ref, moved_ref, row_pack, row_arr,
    load_sem, outw_sem,
    rs_ss, rs_rs, ag_ss, ag_rs, hop_rs, fwd_ss, gc_ss, gc_rs, info_ss, info_rs, row_ss, row_rs,
    local_sem,
):
    G, L, T, micros, slots, width, ctx_len = sizes
    W = width // T
    H = HALVES
    S = W // H
    heads = W // HD
    pieces = heads + 2
    g = lax.axis_index("group")
    l = lax.axis_index("section")
    t = lax.axis_index("tensor")
    R = ROWS
    last = L - 1
    half = L // 2

    order = tuple(sorted(range(1, T), key=lambda d: -min(d, T - d)))

    def turned(d):
        return lax.rem(t + T + (1 - 2 * lax.rem(g, 2)) * d, T)

    def rs_copy(m, h, d):
        return pltpu.make_async_remote_copy(
            src_ref=rs_send.at[m, h, d - 1], dst_ref=rs_recv.at[m, h, d - 1],
            send_sem=rs_ss.at[m, h, d - 1], recv_sem=rs_rs.at[m, h],
            device_id={"tensor": turned(d)}, device_id_type=MESH)

    def ag_copy(m, h, d):
        return pltpu.make_async_remote_copy(
            src_ref=xnew.at[m, h], dst_ref=xin.at[m, h, t],
            send_sem=ag_ss.at[m, h, d], recv_sem=ag_rs.at[m, h],
            device_id={"section": l + 1, "tensor": turned(d)}, device_id_type=MESH)

    def hop_copy(m, h):
        return pltpu.make_async_remote_copy(
            src_ref=xnew.at[m, h], dst_ref=xin.at[m, h, t],
            send_sem=ag_ss.at[m, h, 0], recv_sem=hop_rs.at[m, h],
            device_id={"section": l + 1}, device_id_type=MESH)

    def fwd_copy(m, h, d):
        return pltpu.make_async_remote_copy(
            src_ref=xin.at[m, h, t], dst_ref=xin.at[m, h, t],
            send_sem=fwd_ss.at[m, h, d - 1], recv_sem=ag_rs.at[m, h],
            device_id={"tensor": turned(d)}, device_id_type=MESH)

    def arrived(ref, sem):
        pltpu.make_async_copy(ref, ref, sem).wait()

    def to_group(src, dst, ss, rs, d):
        return pltpu.make_async_remote_copy(
            src_ref=src, dst_ref=dst, send_sem=ss.at[d - 1], recv_sem=rs.at[d - 1],
            device_id={"group": lax.rem(g + d, G)}, device_id_type=MESH)

    def gc_copy(d):
        e = PAIR * (d - 1)
        return to_group(pack.at[pl.ds(e, PAIR)], arr.at[pl.ds(e, PAIR)], gc_ss, gc_rs, d)

    def info_copy(d):
        return to_group(info_pack.at[d - 1], info_arr.at[d - 1], info_ss, info_rs, d)

    def row_copy(d):
        return to_group(row_pack.at[d - 1], row_arr.at[d - 1], row_ss, row_rs, d)

    def outw_load(h, d):
        start = pl.multiple_of(turned(d) * W + h * S, S)
        place = order.index(d) if d else T - 1
        return pltpu.make_async_copy(
            outw.at[0, :, pl.ds(start, S)], outw_v.at[h, :, pl.ds(place * S, S)], outw_sem.at[h, d])

    query_load = pltpu.make_async_copy(query.at[0], q_v, load_sem.at[0])
    cache_load = pltpu.make_async_copy(cache.at[0], cache_v, load_sem.at[1])
    lens_load = pltpu.make_async_copy(lens_in, lens_ref, load_sem.at[5])
    moves_load = pltpu.make_async_copy(moves_in, moves_ref, load_sem.at[6])
    x_load = pltpu.make_async_copy(hidden, x0_v, load_sem.at[4])
    gain_load = pltpu.make_async_copy(gain, gain_v, load_sem.at[2])
    movers = moves_ref.shape[1]
    place_load = pltpu.make_async_copy(place_v.at[0], place_s, local_sem.at[0])

    lens_load.start(priority=1)
    moves_load.start(priority=1)
    query_load.start(priority=1)
    cache_load.start(priority=1)

    @pl.when(l == 0)
    def _():
        x_load.start(priority=1)

    gain_load.start(priority=1)
    for h in range(H):
        for q in range(T):
            pltpu.make_async_copy(
                kvw.at[0, pl.ds(q * W + h * S, S)], kvw_v.at[h, pl.ds(q * S, S)],
                load_sem.at[3]).start(priority=1)

    barrier = pltpu.get_barrier_semaphore()
    for d in range(1, T):
        pl.semaphore_signal(barrier, inc=1, device_id={"tensor": lax.rem(t + d, T)}, device_id_type=MESH)
    for d in range(1, G):
        pl.semaphore_signal(barrier, inc=1, device_id={"group": lax.rem(g + d, G)}, device_id_type=MESH)

    @pl.when(l > 0)
    def _():
        for k in range(T):
            pl.semaphore_signal(
                barrier, inc=1, device_id={"section": l - 1, "tensor": k}, device_id_type=MESH)

    @pl.when((l > 0) & (l < last))
    def _():
        pl.semaphore_wait(barrier, T - 1 + G - 1 + T)

    @pl.when(l == last)
    def _():
        pl.semaphore_wait(barrier, T - 1 + G - 1)

    def arrange():
        leaving = [moves_ref[0, i] for i in range(movers)]
        ranked = list(leaving)
        for end in range(movers - 1, 0, -1):
            for i in range(end):
                low = jnp.minimum(ranked[i], ranked[i + 1])
                high = jnp.maximum(ranked[i], ranked[i + 1])
                ranked[i], ranked[i + 1] = low, high

        def staying(position):
            slot = position - movers
            for k in range(movers):
                slot = slot + (slot >= ranked[k]).astype(jnp.int32)
            return slot

        def slot_of(position):
            slot = staying(position)
            for i in range(movers):
                slot = jnp.where(position == i, leaving[i], slot)
            return slot

        def place(p, carry):
            perm_s[p] = staying(p)
            return carry

        for i in range(movers):
            perm_s[i] = leaving[i]
        lax.fori_loop(movers, slots, place, 0)
        square = (slots, slots)
        row, col = iota(square, 0), iota(square, 1)
        pick_ref[...] = jnp.where(slot_of(row) == col, 1.0, 0.0).astype(BF16)
        back_ref[...] = jnp.where((staying(col) == row) & (col >= movers), 1.0, 0.0).astype(BF16)

    block = 8
    blocks = slots // block

    def attend(first, end):
        span = block * ctx_len
        scale = HD ** -0.5

        def one(b, carry):
            rows = pl.ds(pl.multiple_of(b * block, block), block)
            lens = jnp.zeros((block, span), jnp.int32)
            row = iota((block, span), 0)
            slot = [perm_s[b * block + n] for n in range(block)]
            for n in range(block):
                lens = jnp.where(row == n, lens_ref[slot[n]], lens)
            tokens = jnp.concatenate([cache_v[slot[n]] for n in range(block)], axis=0)
            col = iota((block, span), 1)
            ok = (col // ctx_len == row) & (col % ctx_len < lens)
            bias = jnp.where(ok, 0.0, LOW).astype(F32)
            stacked = jnp.concatenate(
                [qf_v[rows, a * HD:(a + 1) * HD] for a in range(heads)], axis=0).astype(BF16)
            keys = tokens[:, 0:HD]
            values = tokens[:, HD:2 * HD]
            score = lax.dot_general(
                stacked, keys, (((1,), (1,)), ((), ())), preferred_element_type=F32)
            score = score.reshape(heads, block, span) * scale + bias[None]
            top = jnp.max(score, axis=-1, keepdims=True)
            weight = jnp.exp(score - top)
            total = jnp.sum(weight, axis=-1, keepdims=True)
            mixed = jnp.dot(
                weight.reshape(heads * block, span).astype(BF16), values,
                preferred_element_type=F32)
            ctx_ref[:, rows, :] = mixed.reshape(heads, block, HD)
            mc_ref[:, rows, :] = jnp.broadcast_to(top, (heads, block, HD))
            sc_ref[:, rows, :] = jnp.broadcast_to(total, (heads, block, HD))
            return carry

        lax.fori_loop(first, end, one, 0)

    def depart():
        lane = iota((8, 256), 1)
        sel_row = iota(sel_ref.shape, 0)
        slot_at = jnp.full(sel_ref.shape, NONE, jnp.int32)
        for d in range(1, G):
            e = d - 1
            dest = lax.rem(g + d, G)
            place_vec = jnp.zeros((8, 256), jnp.int32)
            len_vec = jnp.zeros((8, 256), jnp.int32)
            for i in range(PAIR):
                slot = jnp.int32(NONE)
                place = jnp.int32(NONE)
                from_slot = jnp.int32(0)
                for k in range(movers // PAIR):
                    hit = moves_ref[1, PAIR * k] == dest
                    slot = jnp.where(hit, PAIR * k + i, slot)
                    place = jnp.where(hit, moves_ref[2, PAIR * k + i], place)
                    from_slot = jnp.where(hit, moves_ref[0, PAIR * k + i], from_slot)
                here = lane // 16 == e * PAIR + i
                place_vec = jnp.where(here, place, place_vec)
                len_vec = jnp.where(here, lens_ref[from_slot], len_vec)
                slot_at = jnp.where(sel_row // 16 == e * PAIR + i, slot, slot_at)
                pack[PAIR * e + i] = cache_v[from_slot]
            info_pack[e, 0:8, :] = place_vec
            info_pack[e, 8:16, :] = len_vec
            info_copy(d).start()
            gc_copy(d).start()
        sel_col = iota(sel_ref.shape, 1)
        chosen = (sel_row % 16 == sel_col // R) & (slot_at == sel_col % R)
        sel_ref[...] = jnp.where(chosen, 1.0, 0.0).astype(BF16)

    def arrive():
        for d in range(1, G):
            info_copy(d).wait_recv()
        place = info_arr[0, 0:8, :]
        length = info_arr[0, 8:16, :]
        for e in range(1, G - 1):
            place = place + info_arr[e, 0:8, :]
            length = length + info_arr[e, 8:16, :]
        lane8 = iota((8, 256), 1)
        place = jnp.where(lane8 < (G - 1) * PAIR * 16, place, NONE)
        place_v[0] = place
        place_load.start()
        wide = (slots, 256)
        spot = jnp.broadcast_to(place[0:1, :], wide)
        long = jnp.broadcast_to(length[0:1, :], wide)
        lane = iota(wide, 1)
        row = iota(wide, 0)
        match = spot == row
        first = match & (lane % 16 == 0)
        has = jnp.max(jnp.where(first, 1.0, 0.0), axis=-1, keepdims=True)
        moved_len = jnp.max(jnp.where(first, long.astype(F32), 0.0), axis=-1, keepdims=True)
        own_len = jnp.zeros((slots, HD), F32)
        narrow = iota((slots, HD), 0)
        for n in range(slots):
            own_len = jnp.where(narrow == n, lens_ref[n].astype(F32), own_len)
        count_ref[...] = jnp.where(has > 0.5, moved_len, own_len).astype(jnp.int32)
        for c in range(pieces):
            sel2_ref[c * slots:(c + 1) * slots, :] = jnp.where(
                match & (lane % 16 == c), 1.0, 0.0).astype(BF16)
        for d in range(1, G):
            gc_copy(d).wait_recv()
        place_load.wait()

        def fill(j, carry):
            index = jnp.int32(-1)
            for e in range((G - 1) * PAIR):
                index = jnp.where(place_s[0, e * 16] == j, e, index)
            moved = arr[jnp.maximum(index, 0)]
            kept = cache_v[j]
            base_v[j] = lax.select_n(index >= 0, kept, moved)
            return carry

        lax.fori_loop(0, slots, fill, 0)

    def pass_on(m, h):
        arrived(xin.at[m, h, t], hop_rs.at[m, h])
        for d in order:
            fwd_copy(m, h, d).start()

    def forward(m):
        @pl.when(l == half)
        def _():
            pass_on(m, 0)

    def whole_fresh():
        acc = jnp.zeros((slots, 2 * HD), F32)
        square = jnp.zeros((slots, 1), F32)
        for h in range(H):
            scaled = []
            for q in range(T):
                cols = slice(q * W + h * S, q * W + (h + 1) * S)
                xq = x0_v[:, cols].astype(F32)
                square = square + jnp.sum(xq * xq, axis=-1, keepdims=True)
                scaled.append((xq * gain_v[:, cols]).astype(BF16))
            acc = acc + jnp.dot(
                jnp.concatenate(scaled, axis=1), kvw_v[h], preferred_element_type=F32)
        fresh = (acc * lax.rsqrt(square * (1.0 / width) + 1e-06)).astype(BF16)
        fresh_f[...] = jnp.dot(pick_ref[...], fresh, preferred_element_type=F32)
        mine = x0_v[:, pl.ds(pl.multiple_of(t * W, W), W)]
        ordered = jnp.dot(pick_ref[...], mine, preferred_element_type=F32).astype(BF16)
        for m in range(micros):
            for h in range(H):
                xin[m, h, t] = ordered[m * R:(m + 1) * R, h * S:(h + 1) * S]

    def fresh_part(m):
        rows = pl.ds(pl.multiple_of(m * R, R), R)
        acc = jnp.zeros((R, 2 * HD), F32)
        square = jnp.zeros((R, 1), F32)
        for h in range(H):

            if h:
                arrived(xin.at[m, h], ag_rs.at[m, h])
            else:

                @pl.when(l != half)
                def _():
                    arrived(xin.at[m, h], ag_rs.at[m, h])

                @pl.when(l == half)
                def _():
                    arrived(xin.at[m, h, pl.ds(0, T - 1)], ag_rs.at[m, h])

            scaled = []
            for q in range(T):
                cols = slice(q * W + h * S, q * W + (h + 1) * S)
                xq = xin[m, h, q].astype(F32)
                square = square + jnp.sum(xq * xq, axis=-1, keepdims=True)
                scaled.append((xq * gain_v[:, cols]).astype(BF16))
            acc = acc + jnp.dot(
                jnp.concatenate(scaled, axis=1), kvw_v[h], preferred_element_type=F32)
        fresh = (acc * lax.rsqrt(square * (1.0 / width) + 1e-06)).astype(BF16).astype(F32)
        fresh_f[rows, :] = fresh

    def front(m):
        rows = pl.ds(pl.multiple_of(m * R, R), R)

        @pl.when(l > 0)
        def _():
            fresh_part(m)

        fresh = fresh_f[rows, :]
        key = fresh[:, 0:HD]
        value = fresh[:, HD:2 * HD]
        parts = []
        for a in range(heads):
            qa = qf_v[rows, a * HD:(a + 1) * HD]
            own = jnp.sum(qa * key, axis=-1, keepdims=True) * (HD ** -0.5)
            old_top = mc_ref[a, rows, :]
            top = jnp.maximum(old_top, own)
            old_scale = jnp.exp(old_top - top)
            own_weight = jnp.exp(own - top)
            total = sc_ref[a, rows, :] * old_scale + own_weight
            mixed = (ctx_ref[a, rows, :] * old_scale + own_weight * value) / total
            parts.append(mixed.astype(BF16))
        return jnp.concatenate(parts, axis=1)

    def project(m, context, h):
        for i, d in enumerate(order):
            part = jnp.dot(
                context, outw_v[h, :, i * S:(i + 1) * S], preferred_element_type=F32)
            if i or h:
                rs_copy(m, h if i else h - 1, order[i - 1]).start()
            rs_send[m, h, d - 1] = part.astype(BF16)
        if h == H - 1:
            rs_copy(m, h, order[-1]).start()

    def project_own(m, context, h):
        own_part[m, h] = jnp.dot(
            context, outw_v[h, :, (T - 1) * S:T * S], preferred_element_type=F32)

    def reduce(m, h):
        total = own_part[m, h] + xin[m, h, t].astype(F32)
        arrived(rs_recv.at[m, h], rs_rs.at[m, h])
        for d in order:
            total = total + rs_recv[m, h, d - 1].astype(F32)
        rounded = total.astype(BF16)
        xnew[m, h] = rounded
        xnew_f[pl.ds(pl.multiple_of(m * R, R), R), h * S:(h + 1) * S] = rounded.astype(F32)

        @pl.when((l < last) if h else (l < last) & (l != half - 1))
        def _():
            for d in order + (0,):
                ag_copy(m, h, d).start()

        if h == 0:

            @pl.when(l == half - 1)
            def _():
                hop_copy(m, h).start()

    def exchange():
        stacked = jnp.concatenate(
            [xnew_f[0:R, c * HD:(c + 1) * HD] for c in range(heads)]
            + [fresh_f[0:R, c * HD:(c + 1) * HD] for c in range(2)], axis=0).astype(BF16)
        leaving = jnp.dot(sel_ref[...], stacked, preferred_element_type=F32).astype(BF16)
        for d in range(1, G):
            row_pack[d - 1] = leaving[(d - 1) * 32:d * 32]
            row_copy(d).start()

    def collect():
        row_arr[G - 1] = jnp.zeros((32, HD), BF16)
        for d in range(1, G):
            row_copy(d).wait_recv()
        moved_ref[...] = jnp.dot(
            sel2_ref[...], row_arr[...].reshape(G * 32, HD), preferred_element_type=F32)

    def settle():
        kept = jnp.dot(back_ref[...], fresh_f[...].astype(BF16), preferred_element_type=F32)
        token = iota((ctx_len, HD), 0)
        for k in range(2):
            cols = slice(k * HD, (k + 1) * HD)
            c = heads + k
            fresh = kept[:, cols] + moved_ref[c * slots:(c + 1) * slots, :]
            for j in range(slots):
                here = token == count_ref[j:j + 1, :]
                base_v[j, :, cols] = jnp.where(
                    here, fresh[j:j + 1, :], base_v[j, :, cols].astype(F32)).astype(BF16)

    def emit(h):
        cols = slice(h * S, (h + 1) * S)
        kept = jnp.dot(
            back_ref[...], xnew_f[:, cols].astype(BF16), preferred_element_type=F32)
        for k in range(S // HD):
            c = h * (S // HD) + k
            xout_ref[:, c * HD:(c + 1) * HD] = (
                kept[:, k * HD:(k + 1) * HD] + moved_ref[c * slots:(c + 1) * slots, :]).astype(BF16)

    def rs_sent(m):
        for h in range(H):
            for d in order:
                rs_copy(m, h, d).wait_send()

    def sent():
        for m in range(micros - 1):
            rs_sent(m)
        for d in range(1, G):
            info_copy(d).wait_send()
            gc_copy(d).wait_send()
            row_copy(d).wait_send()

    lens_load.wait()
    moves_load.wait()
    arrange()
    for h in range(H):
        for d in order:
            outw_load(h, d).start()
    query_load.wait()
    cache_load.wait()
    qf_v[...] = jnp.dot(pick_ref[...], q_v[...], preferred_element_type=F32)
    first = R // block
    attend(0, first)
    for h in range(H):
        outw_load(h, 0).start()

    @pl.when(l > 0)
    def _():
        attend(first, blocks)
        depart()

    @pl.when(l == 0)
    def _():
        x_load.wait()
        gain_load.wait()
        arrived(kvw_v, load_sem.at[3])
        whole_fresh()

    @pl.when(l >= 3)
    def _():
        arrive()

    @pl.when(l > 0)
    def _():
        gain_load.wait()
        arrived(kvw_v, load_sem.at[3])

    forward(0)

    def batch(m, carry):
        context = front(m)

        @pl.when((l == 0) & (m == 0))
        def _():
            pl.semaphore_wait(barrier, T - 1 + G - 1 + T)

        @pl.when(m == 0)
        def _():
            for h in range(H):
                for d in order + (0,):
                    outw_load(h, d).wait()

        for h in range(H):
            project(m, context, h)

        @pl.when(m + 1 < micros)
        def _():
            forward(m + 1)

        for h in range(H):
            project_own(m, context, h)

        @pl.when((l == 0) & (m == 0))
        def _():
            attend(first, blocks)

        @pl.when((l == last) & (m == micros - 1))
        def _():
            collect()
            settle()
            sent()

        for h in range(H):
            reduce(m, h)
            if h < H - 1:

                @pl.when((l == last) & (m == micros - 1))
                def _():
                    emit(h)

        @pl.when((l == last) & (m == 0))
        def _():
            exchange()

        return carry

    lax.fori_loop(0, micros, batch, 0)

    @pl.when(l == 0)
    def _():
        depart()

    @pl.when(l < 3)
    def _():
        arrive()

    @pl.when(l < last)
    def _():
        exchange()
        collect()
        settle()

    @pl.when(l < last)
    def _():
        for h in range(H - 1):
            emit(h)

    emit(H - 1)

    @pl.when(l < last)
    def _():
        sent()

    rs_sent(micros - 1)

    @pl.when((l < last) & (l != half - 1))
    def _():
        for m in range(micros):
            for d in range(T):
                ag_copy(m, 0, d).wait_send()

    @pl.when(l < last)
    def _():
        for m in range(micros):
            for h in range(1, H):
                for d in range(T):
                    ag_copy(m, h, d).wait_send()

    @pl.when(l == half - 1)
    def _():
        for m in range(micros):
            hop_copy(m, 0).wait_send()

    @pl.when(l == half)
    def _():
        for m in range(micros):
            for d in order:
                fwd_copy(m, 0, d).wait_send()


def finish(chunks, xout, base, layer_out, new_cache, out_sem, x_sem):
    part = base.shape[0] // chunks

    def store(c):
        rows = pl.ds(c * part, part)
        return pltpu.make_async_copy(base.at[rows], new_cache.at[0, rows], out_sem.at[c])

    rows_copy = pltpu.make_async_copy(xout, layer_out.at[0], x_sem.at[0])
    for c in range(chunks):
        store(c).start()
    rows_copy.start()
    for c in range(chunks):
        store(c).wait()
    rows_copy.wait()


def per_device(sizes, hidden_in, queries, cache, lengths, moves, norm_gain, kv_weight, out_weight):
    G, L, T, micros, slots, width, ctx_len = sizes
    W = width // T
    heads = W // HD
    pieces = heads + 2
    R = ROWS
    H = HALVES
    S = W // H
    kv = 2 * HD
    movers = (G - 1) * PAIR
    any_spec = pl.BlockSpec(memory_space=pl.ANY)
    vmem = pl.BlockSpec(memory_space=pltpu.VMEM)
    dma = pltpu.SemaphoreType.DMA
    xout, base = pl.pallas_call(
        functools.partial(kernel, sizes),
        out_shape=(
            pltpu.VMEM((slots, W), BF16),
            pltpu.VMEM((slots, ctx_len, kv), BF16),
        ),
        in_specs=[any_spec] * 8,
        out_specs=(vmem, vmem),
        scratch_shapes=[
            pltpu.VMEM((slots, HD), jnp.int32),
            pltpu.SMEM(lengths.shape, jnp.int32),
            pltpu.SMEM(moves.shape[::-1], jnp.int32),
            pltpu.VMEM((micros, H, T, R, S), BF16),
            pltpu.VMEM((slots, width), BF16),
            pltpu.VMEM((slots, W), BF16),
            pltpu.VMEM((slots, W), F32),
            pltpu.VMEM((slots, ctx_len, kv), BF16),
            pltpu.VMEM((1, width), F32),
            pltpu.VMEM((H, T * S, kv), BF16),
            pltpu.VMEM((H, W, T * S), BF16),
            pltpu.VMEM((heads, slots, HD), F32),
            pltpu.VMEM((heads, slots, HD), F32),
            pltpu.VMEM((heads, slots, HD), F32),
            pltpu.VMEM((slots, kv), F32),
            pltpu.VMEM((micros, H, R, S), F32),
            pltpu.VMEM((micros, H, R, S), BF16),
            pltpu.VMEM((slots, W), F32),
            pltpu.VMEM((micros, H, T - 1, R, S), BF16),
            pltpu.VMEM((micros, H, T - 1, R, S), BF16),
            pltpu.VMEM((movers, ctx_len, kv), BF16),
            pltpu.VMEM((movers, ctx_len, kv), BF16),
            pltpu.VMEM((G - 1, 16, 256), jnp.int32),
            pltpu.VMEM((G - 1, 16, 256), jnp.int32),
            pltpu.VMEM((1, 8, 256), jnp.int32),
            pltpu.SMEM((8, 256), jnp.int32),
            pltpu.SMEM((slots,), jnp.int32),
            pltpu.VMEM((slots, slots), BF16),
            pltpu.VMEM((slots, slots), BF16),
            pltpu.VMEM(((G - 1) * 32, pieces * R), BF16),
            pltpu.VMEM((pieces * slots, 256), BF16),
            pltpu.VMEM((pieces * slots, HD), F32),
            pltpu.VMEM((G - 1, 32, HD), BF16),
            pltpu.VMEM((G, 32, HD), BF16),
            dma((7,)), dma((H, T)),
            dma((micros, H, T - 1)), dma((micros, H)),
            dma((micros, H, T)), dma((micros, H)), dma((micros, H)), dma((micros, H, T - 1)),
            dma((G - 1,)), dma((G - 1,)), dma((G - 1,)), dma((G - 1,)), dma((G - 1,)), dma((G - 1,)),
            dma((1,)),
        ],
        compiler_params=pltpu.CompilerParams(
            collective_id=0, has_side_effects=True, vmem_limit_bytes=56 * 1024 * 1024),
        name="chain",
    )(lengths, moves.T, hidden_in, queries, cache, norm_gain, kv_weight, out_weight)
    chunks = 4
    return pl.pallas_call(
        functools.partial(finish, chunks),
        out_shape=(
            jax.ShapeDtypeStruct((1, slots, W), BF16),
            jax.ShapeDtypeStruct((1, slots, ctx_len, kv), BF16),
        ),
        in_specs=[vmem] * 2,
        out_specs=(any_spec, any_spec),
        scratch_shapes=[dma((chunks,)), dma((1,))],
        compiler_params=pltpu.CompilerParams(vmem_limit_bytes=16 * 1024 * 1024),
        name="finish",
    )(*(pltpu.with_memory_space_constraint(part, pltpu.VMEM) for part in (xout, base)))


def solution(mesh):
    G, L, T = mesh.shape["group"], mesh.shape["section"], mesh.shape["tensor"]

    def whole(hidden_in, queries, cache, lengths, moves, norm_gain, kv_weight, out_weight):
        slots = hidden_in.shape[0] // G
        sizes = (G, L, T, slots // ROWS, slots, hidden_in.shape[1], cache.shape[2])
        return jax.shard_map(
            functools.partial(per_device, sizes),
            mesh=mesh,
            in_specs=(
                P("group", None),
                P("section", "group", "tensor"),
                P("section", "group", None, "tensor"),
                P("group"),
                P("group", None),
                P("section", None),
                P("section", None, "tensor"),
                P("section", "tensor", None),
            ),
            out_specs=(P("section", "group", "tensor"), P("section", "group", None, "tensor")),
            check_vma=False,
        )(hidden_in, queries, cache, lengths, moves, norm_gain, kv_weight, out_weight)

    return whole
```
